512 devices in a mesh: lon: 32 (over x, z_hi, core), lat: 16 (over y, z_lo).
Axes of the slice: x: 4, y: 8, z: 8 (z_hi: 4, z_lo: 2; z = z_hi * 2 + z_lo), core: 2. Of those that a mesh axis runs over, the one named last changes fastest.
Arguments:
- fields: bfloat16 [1, 64, 256, 4096], P(None, None, 'lat', 'lon'), may hold values from -6 to 6
- cotangent: bfloat16 [1, 64, 256, 4096], P(None, None, 'lat', 'lon'), may hold values from -6 to 6
- ocean_mask: int32 [256, 4096], P('lat', 'lon'), may hold values 0 or 1
- seam_partner: int32 [4096], replicated, may hold values from 0 to 4095, as said below
- depth_weight: bfloat16 [64, 7, 7], replicated, may hold values from -0.875 to 0.875
- norm_gain: bfloat16 [64], replicated, may hold values from 0.5 to 1.5
- layer_norm_bias: bfloat16 [64], replicated, may hold values from -3 to 3
- up_weight: bfloat16 [256, 64], replicated, may hold values from -0.75 to 0.75
- up_bias: bfloat16 [256], replicated, may hold values from -3 to 3
- down_weight: bfloat16 [64, 256], replicated, may hold values from -0.375 to 0.375
- layer_scale: bfloat16 [64], replicated, may hold values from 0.5 to 1.5
Outputs:
- output: bfloat16 [1, 64, 256, 4096], P(None, None, 'lat', 'lon')
- grad_fields: bfloat16 [1, 64, 256, 4096], P(None, None, 'lat', 'lon')
- grad_depth: float32 [64, 7, 7], replicated
- grad_gain: float32 [64], replicated
- grad_bias: float32 [64], replicated
- grad_up_weight: float32 [256, 64], replicated
- grad_up_bias: float32 [256], replicated
- grad_down_weight: float32 [64, 256], replicated
- grad_scale: float32 [64], replicated
The draws below stay inside these ranges and needn't reach their ends.
Inputs may be any that keep to these rules, and one draw needn't show every extreme that they name: seam_partner[i] = (s - i) mod 4096 for one whole number s, so it is its own inverse.
All inputs are finite; a program needn't handle non-finite values. No bound on the sum of `ocean_mask` on one device may be relied on, other than what follows from the above.
Results may differ from the reference program's by a relative error of at most 0.0068.
Values may be sent and summed in bfloat16 or wider, within the bound.
A program may use at most 64 MiB of HBM per device.

```python
import math
import jax
import jax.numpy as jnp
from jax import lax

CHANNELS = 64
HIDDEN_SIZE = 256
SAMPLES = 1
LAT_DEV = 16
NLAT = 256
NLON = 4096


def draw_seam_partner(key, part):
    offset = jax.random.randint(jax.random.fold_in(key, 17), (), 0, NLON)
    return ((offset - jnp.arange(NLON, dtype=jnp.int32)) % NLON).astype(jnp.int32)


def set_ends(drawn, stream_key, least, largest):
    dims = drawn.shape
    index_at = [jax.random.randint(jax.random.fold_in(stream_key, axis), (), 0, dims[axis]) for axis in range(len(dims))]
    drawn = drawn.at[tuple(index_at)].set(least)
    longest = dims.index(max(dims))
    index_at[longest] = (index_at[longest] + 1) % dims[longest]
    return drawn.at[tuple(index_at)].set(largest)


def shard_levels(rng, dims, pieces, low, top_value):
    def one(dim, shards_of):
        steps = jax.random.uniform(jax.random.fold_in(jax.random.fold_in(rng, 6), dim), (shards_of,), jnp.float32, low / len(pieces), top_value / len(pieces))
        return jnp.repeat(jnp.exp(steps), dims[dim] // shards_of).reshape((-1,) + (1,) * (len(dims) - dim - 1))

    gain = one(*pieces[0])
    for cut in pieces[1:]:
        gain = gain * one(*cut)
    return gain


def bell_draw(stream_key, extent, deviation, reach, pieces=(), kind=jnp.bfloat16):
    result = deviation * jax.random.normal(stream_key, extent, jnp.float32)
    if pieces:
        result = result * shard_levels(stream_key, extent, pieces, -0.22, 0.18)
    return jnp.clip(result, -reach, reach).astype(kind)


def setup_inputs(seed: int = 0) -> dict:
    arg_keys = jax.random.split(jax.random.key(seed), 12)
    fields = bell_draw(arg_keys[0], (SAMPLES, CHANNELS, NLAT, NLON), 1.0, 6.0, ((2, 16), (3, 32)))
    cotangent = bell_draw(arg_keys[1], (SAMPLES, CHANNELS, NLAT, NLON), 1.0, 6.0, ((2, 16), (3, 32)))
    ocean_mask = set_ends((jax.random.randint(arg_keys[2], (NLAT, NLON), 0, 4) < 3).astype(jnp.int32), jax.random.fold_in(arg_keys[2], 1), 0, 1)
    seam_partner = draw_seam_partner(jax.random.fold_in(arg_keys[11], 71), 0)
    depth_weight = bell_draw(arg_keys[4], (CHANNELS, 7, 7), 49 ** -0.5, 0.875)
    norm_gain = jnp.clip(1.0 + 0.1 * jax.random.normal(arg_keys[5], (CHANNELS,), jnp.float32), 0.5, 1.5).astype(jnp.bfloat16)
    layer_norm_bias = bell_draw(arg_keys[6], (CHANNELS,), 0.5, 3.0)
    up_weight = bell_draw(arg_keys[7], (HIDDEN_SIZE, CHANNELS), CHANNELS ** -0.5, 0.75)
    up_bias = bell_draw(arg_keys[8], (HIDDEN_SIZE,), 0.5, 3.0)
    down_weight = bell_draw(arg_keys[9], (CHANNELS, HIDDEN_SIZE), HIDDEN_SIZE ** -0.5, 0.375)
    layer_scale = jnp.clip(jax.random.uniform(arg_keys[10], (CHANNELS,), jnp.float32, 0.5, 1.5), 0.5, 1.5).astype(jnp.bfloat16)
    return {"fields": fields, "cotangent": cotangent, "ocean_mask": ocean_mask, "seam_partner": seam_partner, "depth_weight": depth_weight, "norm_gain": norm_gain, "layer_norm_bias": layer_norm_bias, "up_weight": up_weight, "up_bias": up_bias, "down_weight": down_weight, "layer_scale": layer_scale}


def extend_field(field, partner):
    rows = field.shape[1]
    upper = field[:, rows - 3:, :][:, ::-1, :]
    upper = jnp.take(upper, partner, axis=2)
    lower = jnp.zeros((field.shape[0], 3, field.shape[2]), field.dtype)
    tall = jnp.concatenate([lower, field, upper], axis=1)
    return jnp.concatenate([tall[:, :, -3:], tall, tall[:, :, :3]], axis=2)

def depth_conv(extended, weight, rows, cols):
    weight_f = weight.astype(jnp.float32)
    total = jnp.zeros((extended.shape[0], rows, cols), jnp.float32)
    for row_tap in range(7):
        for col_tap in range(7):
            total = total + weight_f[:, row_tap, col_tap][:, None, None] * extended[:, row_tap:row_tap + rows, col_tap:col_tap + cols].astype(jnp.float32)
    return total

def gelu_slope(pre):
    cdf = 0.5 * (1.0 + lax.erf(pre / math.sqrt(2.0)))
    return cdf + pre * jnp.exp(-0.5 * pre * pre) / math.sqrt(2.0 * math.pi)

def cell_terms(conv, field, cot, mask, norm_gain, layer_norm_bias, up_weight, up_bias, down_weight, layer_scale):
    mean_c = lax.optimization_barrier(jnp.mean(conv, axis=0, keepdims=True))
    centered_input = conv - mean_c
    var_c = lax.optimization_barrier(jnp.mean(centered_input * centered_input, axis=0, keepdims=True))
    reciprocal_deviation = lax.rsqrt(var_c + 1e-06)
    standardized_input = centered_input * reciprocal_deviation
    layer_norm_gain = norm_gain.astype(jnp.float32)[:, None]
    normalized_output = (standardized_input * layer_norm_gain + layer_norm_bias.astype(jnp.float32)[:, None]).astype(jnp.bfloat16)
    pre = jnp.dot(up_weight, normalized_output, preferred_element_type=jnp.float32) + up_bias.astype(jnp.float32)[:, None]
    hidden = jax.nn.gelu(pre, approximate=False).astype(jnp.bfloat16)
    branch = jnp.dot(down_weight, hidden, preferred_element_type=jnp.float32)
    scale = layer_scale.astype(jnp.float32)[:, None]
    out = (mask * (field.astype(jnp.float32) + scale * branch)).astype(jnp.bfloat16)
    grad_in = mask * cot.astype(jnp.float32)
    d_branch = (grad_in * scale).astype(jnp.bfloat16)
    g_scale = lax.optimization_barrier(jnp.sum(grad_in * branch, axis=1))
    contract_cells = (((1,), (1,)), ((), ()))
    contract_first = (((0,), (0,)), ((), ()))
    g_down = lax.dot_general(d_branch, hidden, contract_cells, preferred_element_type=jnp.float32)
    d_hidden = lax.dot_general(down_weight, d_branch, contract_first, preferred_element_type=jnp.float32)
    d_pre = (d_hidden * gelu_slope(pre)).astype(jnp.bfloat16)
    g_up_b = lax.optimization_barrier(jnp.sum(d_pre.astype(jnp.float32), axis=1))
    g_up_w = lax.dot_general(d_pre, normalized_output, contract_cells, preferred_element_type=jnp.float32)
    normalized_gradient = lax.dot_general(up_weight, d_pre, contract_first, preferred_element_type=jnp.float32)
    gain_gradient = lax.optimization_barrier(jnp.sum(normalized_gradient * standardized_input, axis=1))
    g_bias = lax.optimization_barrier(jnp.sum(normalized_gradient, axis=1))
    gradient_through_norm = normalized_gradient * layer_norm_gain
    convolution_gradient = reciprocal_deviation * (gradient_through_norm - lax.optimization_barrier(jnp.mean(gradient_through_norm, axis=0, keepdims=True)) - standardized_input * lax.optimization_barrier(jnp.mean(gradient_through_norm * standardized_input, axis=0, keepdims=True)))
    return (out, convolution_gradient.astype(jnp.bfloat16), (gain_gradient, g_bias, g_up_w, g_up_b, g_down, g_scale))

def reference(fields, cotangent, ocean_mask, seam_partner, depth_weight, norm_gain, layer_norm_bias, up_weight, up_bias, down_weight, layer_scale):
    samples, chans, rows, cols = fields.shape
    hidden_n = up_weight.shape[0]
    mask_f = ocean_mask.astype(jnp.float32)
    block = LAT_DEV
    count = rows // block

    def split(arr):
        return jnp.transpose(arr.reshape(arr.shape[0], count, block, cols), (1, 0, 2, 3)).reshape(count, arr.shape[0], block * cols)

    def unsplit(arr):
        return jnp.transpose(arr.reshape(count, arr.shape[1], block, cols), (1, 0, 2, 3)).reshape(arr.shape[1], rows, cols)
    totals = (jnp.zeros((chans,), jnp.float32), jnp.zeros((chans,), jnp.float32), jnp.zeros((hidden_n, chans), jnp.float32), jnp.zeros((hidden_n,), jnp.float32), jnp.zeros((chans, hidden_n), jnp.float32), jnp.zeros((chans,), jnp.float32))
    g_depth = jnp.zeros((chans, 7, 7), jnp.float32)
    outputs = []
    grads = []
    weight_f = depth_weight.astype(jnp.float32)
    for sample in range(samples):
        field = fields[sample]
        cot = cotangent[sample]
        extended = extend_field(field, seam_partner)
        conv = depth_conv(extended, depth_weight, rows, cols)

        def step(carry, inputs):
            conv_b, field_b, cot_b, mask_b = inputs
            out_b, dconv_b, parts = cell_terms(conv_b, field_b, cot_b, mask_b, norm_gain, layer_norm_bias, up_weight, up_bias, down_weight, layer_scale)
            return (jax.tree.map(lambda left, right: left + right, carry, parts), (out_b, dconv_b))
        mask_blocks = split(mask_f[None])
        totals, (out_blocks, dconv_blocks) = lax.scan(step, totals, (split(conv), split(field), split(cot), mask_blocks))
        outputs.append(unsplit(out_blocks))
        convolution_gradient = unsplit(dconv_blocks).astype(jnp.float32)
        taps = []
        for row_tap in range(7):
            line = []
            for col_tap in range(7):
                line.append(lax.optimization_barrier(jnp.sum(convolution_gradient * extended[:, row_tap:row_tap + rows, col_tap:col_tap + cols].astype(jnp.float32), axis=(1, 2))))
            taps.append(jnp.stack(line, axis=1))
        g_depth = g_depth + jnp.stack(taps, axis=1)
        padded = jnp.pad(convolution_gradient, ((0, 0), (6, 6), (6, 6)))
        d_ext = jnp.zeros((chans, rows + 6, cols + 6), jnp.float32)
        for row_tap in range(7):
            for col_tap in range(7):
                d_ext = d_ext + weight_f[:, row_tap, col_tap][:, None, None] * padded[:, 6 - row_tap:12 - row_tap + rows, 6 - col_tap:12 - col_tap + cols]
        grid = d_ext[:, 3:rows + 3, 3:cols + 3]
        grid = grid.at[:, :, :3].add(d_ext[:, 3:rows + 3, cols + 3:])
        grid = grid.at[:, :, cols - 3:].add(d_ext[:, 3:rows + 3, :3])
        margin = d_ext[:, rows + 3:, :]
        wrapped = margin[:, :, 3:cols + 3]
        wrapped = wrapped.at[:, :, :3].add(margin[:, :, cols + 3:])
        wrapped = wrapped.at[:, :, cols - 3:].add(margin[:, :, :3])
        folded = jnp.take(wrapped, seam_partner, axis=2)
        grid = grid.at[:, rows - 3:, :].add(folded[:, ::-1, :])
        grads.append((mask_f[None] * cot.astype(jnp.float32) + grid).astype(jnp.bfloat16))
    gain_gradient, g_bias, g_up_w, g_up_b, g_down, g_scale = totals
    return (jnp.stack(outputs), jnp.stack(grads), g_depth, gain_gradient, g_bias, g_up_w, g_up_b, g_down, g_scale)
```

```python
import functools
import math

import jax
import jax.numpy as jnp
from jax import lax
from jax.experimental import pallas as pl
from jax.experimental.pallas import tpu as pltpu
from jax.sharding import PartitionSpec as P

F32 = jnp.float32
BF16 = jnp.bfloat16
MESH = pl.DeviceIdType.MESH
C = 64
R = 16
L = 128
HID = 256
RE = R + 6
AR_ROWS = 384
AR_DOWN = 144
AR_DEPTH = 288
CORES = 2

ERF_P = 0.3275911 / math.sqrt(2.0)
ERF_C = (
    0.5 * 0.254829592,
    0.5 * -0.284496736,
    0.5 * 1.421413741,
    0.5 * -1.453152027,
    0.5 * 1.061405429,
)
PDF = 1.0 / math.sqrt(2.0 * math.pi)


def phi_and_density(v):
    d = 1.0 + ERF_P * jnp.abs(v)
    t = pl.reciprocal(d, approx=True)
    t = t * (2.0 - d * t)
    e = jnp.exp(-0.5 * (v * v))
    poly = ERF_C[4]
    for coef in ERF_C[3::-1]:
        poly = poly * t + coef
    tail = poly * t * e
    return jnp.where(v >= 0.0, 1.0 - tail, tail), e


def nt_dot(a, b):
    return lax.dot_general(a, b, (((1,), (1,)), ((), ())), preferred_element_type=F32)


def dot(a, b):
    return jnp.dot(a, b, preferred_element_type=F32)


def roll(x, amount):
    amount %= L
    return pltpu.roll(x, amount, x.ndim - 1) if amount else x


def kernel(
    dims,
    fields_ref,
    cot_ref,
    mask_ref,
    seam_ref,
    par_ref,
    upx_ref,
    up_ref,
    down_ref,
    out_ref,
    gf_ref,
    ar_ref,
    rows_f,
    gmask,
    outr,
    xm,
    dm,
    shifts,
    hal,
    fshift,
    wts,
    conv,
    pks,
    pkr,
    fx,
    fzs,
    fzr,
    onehot,
    upt,
    downt,
    parb,
    acc_s,
    acc_down,
    acc_up,
    ar_src,
    ar1,
    ar2,
    ar3,
    ag,
    halo_send,
    halo_recv,
    fx_send,
    fx_recv,
    fz_send,
    fz_recv,
    a1_send,
    a1_recv,
    a2_send,
    a2_recv,
    a3_send,
    a3_recv,
    ag_send,
    ag_recv,
):
    nlon, nlat, nx = dims
    nzc = nlon // nx
    nz = nzc // CORES
    ng = nx * CORES
    chunk = AR_ROWS // nlat
    early = AR_DEPTH // chunk
    lon = lax.axis_index("lon")
    lat = lax.axis_index("lat")
    mx, mzc = lon // nzc, lon % nzc
    mz, mc = mzc // CORES, mzc % CORES
    mg = mx * CORES + mc
    left, right = (lon + nlon - 1) % nlon, (lon + 1) % nlon
    down_lat, up_lat = (lat + nlat - 1) % nlat, (lat + 1) % nlat
    lats = (down_lat, lat, up_lat)
    is_top = lat == nlat - 1
    is_bottom = lat == 0

    def place(a, b):
        return {"lon": a, "lat": b}

    def lon_of_group(g):
        return (g // CORES) * nzc + mz * CORES + g % CORES

    barrier = pltpu.get_barrier_semaphore()

    def hail(a, b):
        pl.semaphore_signal(barrier, inc=1, device_id=place(a, b), device_id_type=MESH)

    for b in lats:
        hail(left, b)
        hail(right, b)
    hail(lon, down_lat)
    hail(lon, up_lat)

    @pl.loop(1, nlat)
    def _(j):
        hail(lon, (lat + j) % nlat)

    @pl.loop(1, ng)
    def _(j):
        hail(lon_of_group((mg + j) % ng), lat)

    @pl.loop(1, nzc)
    def _(j):
        hail(mx * nzc + (mzc + j) % nzc, lat)

    lane = lax.broadcasted_iota(jnp.int32, (C, L), 1)
    slot_of_lane = lane // 8
    low_half = lane < 64

    def remote(src, dst, send, recv, where):
        return pltpu.make_async_remote_copy(
            src_ref=src, dst_ref=dst, send_sem=send, recv_sem=recv,
            device_id=where, device_id_type=MESH,
        )

    def halo_copies(ph, rows):
        made = [
            remote(rows.at[pl.ds(3, 3)], rows.at[pl.ds(R + 3, 3)],
                   halo_send.at[ph, 0], halo_recv.at[ph, 0], place(lon, down_lat)),
            remote(rows.at[pl.ds(R, 3)], rows.at[pl.ds(0, 3)],
                   halo_send.at[ph, 1], halo_recv.at[ph, 1], place(lon, up_lat)),
        ]
        for side, to in ((0, left), (1, right)):
            for k in range(3):
                sem = 2 + 3 * side + k
                made.append(
                    remote(pks.at[ph, side], pkr.at[ph, side, k],
                           halo_send.at[ph, sem], halo_recv.at[ph, sem], place(to, lats[k]))
                )
        return made

    def pack(ph, row):
        low = jnp.zeros((C, L), F32)
        high = jnp.zeros((C, L), F32)
        for i in range(R):
            here = slot_of_lane == i
            low = jnp.where(here, roll(row(i), 8 * i), low)
            high = jnp.where(here, roll(row(i), 8 * i + 8), high)
        pks[ph, 0] = low.astype(BF16)
        pks[ph, 1] = high.astype(BF16)

    def unpack(ph):
        for k, ext_rows, first in ((2, range(0, 3), 13), (1, range(3, R + 3), -3), (0, range(R + 3, RE), -R - 3)):
            from_right = pkr[ph, 0, k].astype(F32)
            from_left = pkr[ph, 1, k].astype(F32)
            for u in ext_rows:
                i = u + first
                hal[u] = jnp.where(low_half, roll(from_right, -8 * i), roll(from_left, 120 - 8 * i))

    def shifted(q, main, halo, lanes):
        if q == 3:
            return main
        edge = lanes >= 125 + q if q < 3 else lanes < q - 3
        return roll(jnp.where(edge, halo, main), 3 - q)

    def build_shifts(rows):
        @pl.loop(0, C // 16)
        def _(s):
            cs = pl.ds(pl.multiple_of(s * 16, 16), 16)
            main = rows[:, cs, :].astype(F32)
            halo = hal[:, cs, :]
            lanes = lax.broadcasted_iota(jnp.int32, (RE, 16, L), 2)
            for q in range(7):
                shifts[q, :, cs, :] = shifted(q, main, halo, lanes)

    def fold_first(ph, rows):
        fx[ph, mx] = rows[R : R + 3]

        @pl.loop(1, nx)
        def _(j):
            to = (mx + j) % nx
            remote(rows.at[pl.ds(R, 3)], fx.at[ph, mx], fx_send.at[ph, to], fx_recv.at[ph, mx],
                   place(to * nzc + mzc, lat)).start()

    def fold_second(ph, rows):
        @pl.loop(1, nx)
        def _(j):
            to = (mx + j) % nx
            remote(rows.at[pl.ds(R, 3)], fx.at[ph, to], fx_send.at[ph, to], fx_recv.at[ph, to],
                   place(to * nzc + mzc, lat)).wait()

        held = jnp.concatenate([fx[ph, x].reshape(3 * C, L) for x in range(nx)], axis=1)

        @pl.loop(0, nzc)
        def _(t):
            got = dot(held, onehot[t])
            mirrored = [got[C * (2 - k) : C * (3 - k)] for k in range(3)]
            slot = slot_of_lane % 8
            edges = mirrored[2][:, L:]
            for k in (1, 0):
                edges = jnp.where(slot == k, mirrored[k][:, L:], edges)
            for k in range(3):
                fzs[ph, t, k] = mirrored[k][:, :L].astype(BF16)
            fzs[ph, t, 3] = edges.astype(BF16)

        fzr[ph, mzc] = fzs[ph, mzc]

        @pl.loop(1, nzc)
        def _(j):
            t = (mzc + j) % nzc
            remote(fzs.at[ph, t], fzr.at[ph, mzc], fz_send.at[ph, t], fz_recv.at[ph, mzc],
                   place(mx * nzc + t, lat)).start()

    def fold_last(ph):
        @pl.loop(1, nzc)
        def _(j):
            t = (mzc + j) % nzc
            remote(fzs.at[ph, t], fzr.at[ph, t], fz_send.at[ph, t], fz_recv.at[ph, t],
                   place(mx * nzc + t, lat)).wait()

        total = fzr[ph, 0].astype(F32)
        for t in range(1, nzc):
            total = total + fzr[ph, t].astype(F32)
        halos = [
            jnp.where(low_half, roll(total[3], -8 * k), roll(total[3], 56 - 8 * k))
            for k in range(3)
        ]
        return [total[k] for k in range(3)], halos

    rows_f[...] = fields_ref[...].astype(F32).reshape(C * R, L)
    for i in range(R):
        xm[3 + i] = rows_f[pl.ds(i, C, stride=R), :].astype(BF16)
    pack(0, lambda i: xm[3 + i].astype(F32))
    pl.semaphore_wait(barrier, 8 + (nlat - 1) + (ng - 1) + (nzc - 1))
    sent = halo_copies(0, xm)
    for copy in sent:
        copy.start()

    @pl.when(is_top)
    def _():
        fold_first(0, xm)
        partner = seam_ref[0:1, 0:1]
        rows_i = lax.broadcasted_iota(jnp.int32, (nx * L, 2 * L), 0)
        held_col = L * ((rows_i // L) * nzc + mzc) + rows_i % L
        col = lax.broadcasted_iota(jnp.int32, (1, 2 * L), 1)
        packed = col - L
        ahead = jnp.where(packed < 64, L + packed % 8, packed % 8 - 8)
        offset = jnp.where(col < L, col, ahead)

        @pl.loop(0, nzc)
        def _(t):
            wanted = (partner - L * (mx * nzc + t) - offset) & (nlon * L - 1)
            onehot[t] = jnp.where(held_col == wanted, 1.0, 0.0).astype(BF16)

    rows_f[...] = cot_ref[...].astype(F32).reshape(C * R, L)
    for i in range(R):
        gmask[i] = rows_f[pl.ds(i, C, stride=R), :] * mask_ref[i : i + 1, :].astype(F32)
    par = par_ref[...]
    for tap in range(49):
        wts[tap] = jnp.broadcast_to(par[:, tap : tap + 1], (C, L))
    for n in range(3):
        parb[n] = jnp.broadcast_to(par[:, 64 + n : 65 + n], (C, 2 * L))

    def eye(n):
        return jnp.where(
            lax.broadcasted_iota(jnp.int32, (n, n), 0) == lax.broadcasted_iota(jnp.int32, (n, n), 1), 1.0, 0.0
        ).astype(BF16)

    upt[...] = nt_dot(eye(C), up_ref[...]).astype(BF16)
    downt[...] = nt_dot(eye(HID), down_ref[...]).astype(BF16)
    acc_s[...] = jnp.zeros_like(acc_s)
    acc_down[...] = jnp.zeros_like(acc_down)
    acc_up[...] = jnp.zeros_like(acc_up)

    @pl.when(is_top)
    def _():
        fold_second(0, xm)

    for copy in sent:
        copy.wait()
    unpack(0)

    @pl.when(is_bottom)
    def _():
        for u in range(3):
            xm[u] = jnp.zeros((C, L), BF16)
            hal[u] = jnp.zeros((C, L), F32)

    @pl.when(is_top)
    def _():
        mains, halos = fold_last(0)
        for k in range(3):
            xm[R + 3 + k] = mains[k].astype(BF16)
            hal[R + 3 + k] = halos[k]

    build_shifts(xm)

    @pl.loop(0, C // 8)
    def _(s):
        cs = pl.ds(pl.multiple_of(s * 8, 8), 8)
        total = jnp.zeros((R, 8, L), F32)
        for q in range(7):
            for a in range(7):
                total = total + wts[a * 7 + q, cs, :][None] * shifts[q, a : a + R, cs, :]
        conv[:, cs, :] = total

    @pl.loop(0, R // 2)
    def _(r):
        two = pl.ds(2 * r, 2)

        def flat(x):
            return jnp.concatenate([x[0], x[1]], axis=1)

        gain, bias, scale = parb[0], parb[1], parb[2]
        x = flat(conv[two])
        mean = jnp.mean(x, axis=0, keepdims=True)
        x = x - mean
        rstd = lax.rsqrt(jnp.mean(x * x, axis=0, keepdims=True) + 1e-06)
        xhat = x * rstd
        normed = (xhat * gain + bias).astype(BF16)
        normed_one = jnp.concatenate([normed, jnp.ones((16, 2 * L), BF16)], axis=0)
        pre = dot(upx_ref[...], normed_one)
        phi, density = phi_and_density(pre)
        hidden = (pre * phi).astype(BF16)
        slope = phi + pre * density * PDF
        branch = dot(down_ref[...], hidden)
        mask = mask_ref[two, :].astype(F32)
        mask = jnp.concatenate([mask[0:1], mask[1:2]], axis=1)
        field = flat(xm[pl.ds(3 + 2 * r, 2)].astype(F32))
        out = mask * (field + scale * branch)
        outr[2 * r] = out[:, :L]
        outr[2 * r + 1] = out[:, L:]
        g = flat(gmask[two])
        d_branch = (g * scale).astype(BF16)
        acc_s[2] += g * branch
        acc_down[...] += nt_dot(d_branch, hidden)
        d_hidden = dot(downt[...], d_branch)
        d_pre = (d_hidden * slope).astype(BF16)
        acc_up[...] += nt_dot(normed_one, d_pre)
        d_normed = dot(upt[...], d_pre)
        acc_s[0] += d_normed * xhat
        acc_s[1] += d_normed
        gd = d_normed * gain
        d_conv = rstd * (
            gd
            - jnp.mean(gd, axis=0, keepdims=True)
            - xhat * jnp.mean(gd * xhat, axis=0, keepdims=True)
        )
        d_conv = d_conv.astype(BF16)
        dm[3 + 2 * r] = d_conv[:, :L]
        dm[4 + 2 * r] = d_conv[:, L:]
        d_conv = d_conv.astype(F32)
        conv[2 * r] = d_conv[:, :L]
        conv[2 * r + 1] = d_conv[:, L:]

    pack(1, lambda i: conv[i])
    sent = halo_copies(1, dm)
    for copy in sent:
        copy.start()

    @pl.when(is_top)
    def _():
        fold_first(1, dm)

    def chunk_copy(to, slot):
        return remote(
            ar_src.at[pl.ds(pl.multiple_of(to * chunk, 8), chunk)], ar1.at[slot],
            a1_send.at[to], a1_recv.at[slot], place(lon, to),
        )

    def send_chunks(first, last):
        @pl.loop(first, last)
        def _(p):
            @pl.when(p != lat)
            def _():
                chunk_copy(p, lat).start()

    up = acc_up[...]
    ar_src[0:72] = up[:72, :L]
    ar_src[72:144] = up[:72, L:]
    down = acc_down[...]
    ar_src[AR_DOWN : AR_DOWN + C] = down[:, :L]
    ar_src[AR_DOWN + C : AR_DOWN + 2 * C] = down[:, L:]
    ar_src[AR_DOWN + 2 * C : AR_DEPTH] = jnp.zeros((AR_DEPTH - AR_DOWN - 2 * C, L), F32)
    ar_src[AR_DEPTH + C :] = jnp.zeros((AR_ROWS - AR_DEPTH - C, L), F32)
    send_chunks(0, early)

    @pl.when(is_top)
    def _():
        fold_second(1, dm)

    @pl.loop(0, C // 8)
    def _(s):
        cs = pl.ds(pl.multiple_of(s * 8, 8), 8)
        d_conv = conv[:, cs, :]
        lanes = lax.broadcasted_iota(jnp.int32, (8, L), 1)
        got = jnp.zeros((8, L), F32)
        for q in range(7):
            for a in range(7):
                tap = jnp.sum(d_conv * shifts[q, a : a + R, cs, :], axis=0)
                got = jnp.where(lanes == a * 7 + q, jnp.sum(tap, axis=1, keepdims=True), got)
        for n in range(3):
            got = jnp.where(lanes == 64 + n, jnp.sum(acc_s[n, cs, :], axis=1, keepdims=True), got)
        ar_src[pl.ds(pl.multiple_of(AR_DEPTH + s * 8, 8), 8)] = got

    send_chunks(early, nlat)

    for copy in sent:
        copy.wait()
    unpack(1)

    @pl.when(is_bottom)
    def _():
        for u in range(3):
            dm[u] = jnp.zeros((C, L), BF16)
            hal[u] = jnp.zeros((C, L), F32)

    @pl.when(is_top)
    def _():
        for u in range(R + 3, RE):
            dm[u] = jnp.zeros((C, L), BF16)
            hal[u] = jnp.zeros((C, L), F32)

    build_shifts(dm)

    @pl.loop(0, nlat)
    def _(p):
        @pl.when(p != lat)
        def _():
            chunk_copy(p, p).wait()

    own = pl.ds(pl.multiple_of(lat * chunk, 8), chunk)
    ar1[lat] = ar_src[own]
    ar2[mg] = jnp.sum(ar1[...], axis=0)

    def group_copy(j, slot):
        to = (mg + j) % ng
        return remote(ar2.at[mg], ar2.at[slot(to)], a2_send.at[to], a2_recv.at[slot(to)],
                      place(lon_of_group(to), lat))

    @pl.loop(1, ng)
    def _(j):
        group_copy(j, lambda to: mg).start()

    def adjoint(first, last):
        @pl.loop(first, last)
        def _(s):
            cs = pl.ds(pl.multiple_of(s * 8, 8), 8)
            total = gmask[:, cs, :]
            for q in range(7):
                for a in range(7):
                    total = total + wts[a * 7 + q, cs, :][None] * shifts[6 - q, 6 - a : 6 - a + R, cs, :]
            gmask[:, cs, :] = total

    adjoint(0, C // 16)

    @pl.loop(1, ng)
    def _(j):
        group_copy(j, lambda to: to).wait()

    ar3[mz] = jnp.sum(ar2[...], axis=0)

    def depth_copy(j, slot):
        to = (mz + j) % nz
        return remote(ar3.at[mz], ar3.at[slot(to)], a3_send.at[to], a3_recv.at[slot(to)],
                      place(mx * nzc + to * CORES + mc, lat))

    if nz > 1:

        @pl.loop(1, nz)
        def _(j):
            depth_copy(j, lambda to: mz).start()

    adjoint(C // 16, C // 8)

    if nz > 1:

        @pl.loop(1, nz)
        def _(j):
            depth_copy(j, lambda to: to).wait()

    ag[lat] = jnp.sum(ar3[...], axis=0)

    def spread_copy(j, slot):
        to = (lat + j) % nlat
        return remote(ag.at[lat], ag.at[slot(to)], ag_send.at[to], ag_recv.at[slot(to)],
                      place(lon, to))

    @pl.loop(1, nlat)
    def _(j):
        spread_copy(j, lambda to: lat).start()

    for i in range(R):
        rows_f[pl.ds(i, C, stride=R), :] = outr[i]
    out_ref[...] = rows_f[...].reshape(C, R, L).astype(BF16)

    @pl.when(is_top)
    def _():
        mains, halos = fold_last(1)
        for k in range(3):
            for q in range(7):
                fshift[q, k] = shifted(q, mains[k], halos[k], lane)
        for k in range(3):
            total = gmask[R - 1 - k]
            for a in range(k + 4, 7):
                for q in range(7):
                    total = total + wts[a * 7 + q] * fshift[q, a - k - 4]
            gmask[R - 1 - k] = total

    for i in range(R):
        rows_f[pl.ds(i, C, stride=R), :] = gmask[i]
    gf_ref[...] = rows_f[...].reshape(C, R, L).astype(BF16)

    @pl.loop(1, nlat)
    def _(j):
        spread_copy(j, lambda to: to).wait()

    for p in range(nlat):
        ar_ref[p * chunk : (p + 1) * chunk] = ag[p]


def shards(
    dims,
    fields,
    cotangent,
    ocean_mask,
    seam_partner,
    depth_weight,
    norm_gain,
    layer_norm_bias,
    up_weight,
    up_bias,
    down_weight,
    layer_scale,
):
    nlon, nlat, nx = dims
    nzc = nlon // nx
    nz = nzc // CORES
    ng = nx * CORES
    chunk = AR_ROWS // nlat
    params = jnp.concatenate(
        [
            depth_weight.reshape(C, 49),
            jnp.zeros((C, 15), BF16),
            norm_gain[:, None],
            layer_norm_bias[:, None],
            layer_scale[:, None],
            jnp.zeros((C, 61), BF16),
        ],
        axis=1,
    ).astype(F32)
    up_ext = jnp.concatenate([up_weight, up_bias[:, None], jnp.zeros((HID, 15), BF16)], axis=1)
    vmem = pl.BlockSpec(memory_space=pltpu.VMEM)
    dma = pltpu.SemaphoreType.DMA
    out, grad_fields, sums = pl.pallas_call(
        functools.partial(kernel, dims),
        out_shape=(
            jax.ShapeDtypeStruct((C, R, L), BF16),
            jax.ShapeDtypeStruct((C, R, L), BF16),
            jax.ShapeDtypeStruct((AR_ROWS, L), F32),
        ),
        in_specs=[vmem] * 8,
        out_specs=(vmem,) * 3,
        scratch_shapes=[
            pltpu.VMEM((C * R, L), F32),
            pltpu.VMEM((R, C, L), F32),
            pltpu.VMEM((R, C, L), F32),
            pltpu.VMEM((RE, C, L), BF16),
            pltpu.VMEM((RE, C, L), BF16),
            pltpu.VMEM((7, RE, C, L), F32),
            pltpu.VMEM((RE, C, L), F32),
            pltpu.VMEM((7, 3, C, L), F32),
            pltpu.VMEM((49, C, L), F32),
            pltpu.VMEM((R, C, L), F32),
            pltpu.VMEM((2, 2, C, L), BF16),
            pltpu.VMEM((2, 2, 3, C, L), BF16),
            pltpu.VMEM((2, nx, 3, C, L), BF16),
            pltpu.VMEM((2, nzc, 4, C, L), BF16),
            pltpu.VMEM((2, nzc, 4, C, L), BF16),
            pltpu.VMEM((nzc, nx * L, 2 * L), BF16),
            pltpu.VMEM((C, HID), BF16),
            pltpu.VMEM((HID, C), BF16),
            pltpu.VMEM((3, C, 2 * L), F32),
            pltpu.VMEM((3, C, 2 * L), F32),
            pltpu.VMEM((C, HID), F32),
            pltpu.VMEM((80, HID), F32),
            pltpu.VMEM((AR_ROWS, L), F32),
            pltpu.VMEM((nlat, chunk, L), F32),
            pltpu.VMEM((ng, chunk, L), F32),
            pltpu.VMEM((nz, chunk, L), F32),
            pltpu.VMEM((nlat, chunk, L), F32),
            dma((2, 8)),
            dma((2, 8)),
            dma((2, nx)),
            dma((2, nx)),
            dma((2, nzc)),
            dma((2, nzc)),
            dma((nlat,)),
            dma((nlat,)),
            dma((ng,)),
            dma((ng,)),
            dma((nz,)),
            dma((nz,)),
            dma((nlat,)),
            dma((nlat,)),
        ],
        compiler_params=pltpu.CompilerParams(
            collective_id=0, has_side_effects=True, vmem_limit_bytes=48 * 2**20
        ),
        name="block",
    )(
        fields[0],
        cotangent[0],
        ocean_mask,
        seam_partner.reshape(nlon, L),
        params,
        up_ext,
        up_weight,
        down_weight,
    )
    up = jnp.concatenate([sums[:72], sums[72:AR_DOWN]], axis=1)
    down = jnp.concatenate([sums[AR_DOWN : AR_DOWN + C], sums[AR_DOWN + C : AR_DOWN + 2 * C]], axis=1)
    last = sums[AR_DEPTH : AR_DEPTH + C]
    return (
        out[None],
        grad_fields[None],
        last[:, :49].reshape(C, 7, 7),
        last[:, 64],
        last[:, 65],
        up[:C].T,
        up[C],
        down,
        last[:, 66],
    )


def solution(mesh):
    nlon, nlat = mesh.shape["lon"], mesh.shape["lat"]
    dims = (nlon, nlat, 4 if nlon % 16 == 0 else 2)
    cells = P(None, None, "lat", "lon")
    return jax.shard_map(
        functools.partial(shards, dims),
        mesh=mesh,
        in_specs=(cells, cells, P("lat", "lon")) + (P(),) * 8,
        out_specs=(cells, cells) + (P(),) * 7,
        check_vma=False,
    )
```

```python
import functools
import math

import jax
import jax.numpy as jnp
from jax import lax
from jax.experimental import pallas as pl
from jax.experimental.pallas import tpu as pltpu
from jax.sharding import PartitionSpec as P

F32 = jnp.float32
BF16 = jnp.bfloat16
MESH = pl.DeviceIdType.MESH
C = 64
R = 16
L = 128
HID = 256
RE = R + 6
BLOCK = 4
WIDE = BLOCK * L
MLP_ROWS = 256
REST_ROWS = 32
CORES = 2

ERF_P = 0.3275911 / math.sqrt(2.0)
ERF_C = (
    0.5 * 0.254829592,
    0.5 * -0.284496736,
    0.5 * 1.421413741,
    0.5 * -1.453152027,
    0.5 * 1.061405429,
)
PDF = 1.0 / math.sqrt(2.0 * math.pi)


def phi_and_density(v):
    d = 1.0 + ERF_P * jnp.abs(v)
    t = pl.reciprocal(d, approx=True)
    t = t * (2.0 - d * t)
    e = jnp.exp(-0.5 * (v * v))
    poly = ERF_C[4]
    for coef in ERF_C[3::-1]:
        poly = poly * t + coef
    tail = poly * t * e
    return jnp.where(v >= 0.0, 1.0 - tail, tail), e


def nt_dot(a, b):
    return lax.dot_general(a, b, (((1,), (1,)), ((), ())), preferred_element_type=F32)


def dot(a, b):
    return jnp.dot(a, b, preferred_element_type=F32)


def roll(x, amount):
    amount %= L
    return pltpu.roll(x, amount, x.ndim - 1) if amount else x


class PartSum:
    def __init__(self, at, src, bufs, sems, owners):
        self.at, self.src, self.owners = at, src, owners
        self.b1, self.b2, self.b3, self.out = bufs
        self.sems = sems
        self.chunk = self.b1.shape[1]

    def piece(self, p):
        return self.src.at[pl.ds(pl.multiple_of(p * self.chunk, 8), self.chunk)]

    def others(self, count, body):
        @pl.loop(0, count)
        def _(p):
            @pl.when(p != self.at.lat)
            def _():
                body(p)

    def owner(self, body):
        if self.owners == self.at.nlat:
            body()
        else:
            pl.when(self.at.lat < self.owners)(body)

    def first(self, to, slot):
        return remote(self.piece(to), self.b1.at[slot], self.sems[0].at[to], self.sems[1].at[slot],
                      self.at.place(self.at.lon, to))

    def second(self, j, mine):
        at = self.at
        to = (at.mg + j) % at.ng
        slot = at.mg if mine else to
        return remote(self.b2.at[at.mg], self.b2.at[slot], self.sems[2].at[to], self.sems[3].at[slot],
                      at.place(at.lon_of_group(to), at.lat))

    def third(self, j, mine):
        at = self.at
        to = (at.mz + j) % at.nz
        slot = at.mz if mine else to
        return remote(self.b3.at[at.mz], self.b3.at[slot], self.sems[4].at[to], self.sems[5].at[slot],
                      at.place(at.mx * at.nzc + to * CORES + at.mc, at.lat))

    def last(self, to, slot):
        return remote(self.out.at[self.at.lat % self.owners], self.out.at[slot], self.sems[6].at[to],
                      self.sems[7].at[slot], self.at.place(self.at.lon, to))

    def step1(self):
        self.others(self.owners, lambda p: self.first(p, self.at.lat).start())

    def step2(self):
        at = self.at

        def go():
            self.others(at.nlat, lambda p: self.first(0, p).wait_recv())
            self.b1[at.lat] = self.src[pl.ds(pl.multiple_of(at.lat * self.chunk, 8), self.chunk)]
            self.b2[at.mg] = jnp.sum(self.b1[...], axis=0)

            @pl.loop(1, at.ng)
            def _(j):
                self.second(j, True).start()

        self.owner(go)

    def step3(self):
        at = self.at

        def go():
            @pl.loop(1, at.ng)
            def _(j):
                self.second(j, False).wait()

            self.b3[at.mz] = jnp.sum(self.b2[...], axis=0)

            @pl.loop(1, at.nz)
            def _(j):
                self.third(j, True).start()

        self.owner(go)

    def step4(self):
        at = self.at

        def go():
            @pl.loop(1, at.nz)
            def _(j):
                self.third(j, False).wait()

            self.out[at.lat] = jnp.sum(self.b3[...], axis=0)
            self.others(at.nlat, lambda p: self.last(p, at.lat).start())

        self.owner(go)

    def finish(self):
        at = self.at
        self.others(self.owners, lambda p: self.last(p, p).wait_recv())
        self.owner(lambda: self.others(at.nlat, lambda p: self.last(p, at.lat).wait_send()))
        self.others(self.owners, lambda p: self.first(p, at.lat).wait_send())


def remote(src, dst, send, recv, where):
    return pltpu.make_async_remote_copy(
        src_ref=src, dst_ref=dst, send_sem=send, recv_sem=recv,
        device_id=where, device_id_type=MESH,
    )


class Place:
    def __init__(self, dims):
        nlon, nlat, nx = dims
        self.nlon, self.nlat, self.nx = dims
        self.nzc = nlon // nx
        self.nz = self.nzc // CORES
        self.ng = nx * CORES
        self.lon = lax.axis_index("lon")
        self.lat = lax.axis_index("lat")
        self.mx, self.mzc = self.lon // self.nzc, self.lon % self.nzc
        self.mz, self.mc = self.mzc // CORES, self.mzc % CORES
        self.mg = self.mx * CORES + self.mc

    def place(self, a, b):
        return {"lon": a, "lat": b}

    def lon_of_group(self, g):
        return (g // CORES) * self.nzc + self.mz * CORES + g % CORES


def kernel(
    dims,
    fields_hbm,
    cot_hbm,
    mask_hbm,
    seam_hbm,
    depth_hbm,
    gain_hbm,
    bias_hbm,
    scale_hbm,
    upt_hbm,
    upb_hbm,
    down_hbm,
    out_ref,
    gf_ref,
    mlp_ref,
    rest_ref,
    rows_f,
    gmask,
    outr,
    xf,
    df,
    shifts,
    hal,
    fshift,
    wts,
    conv,
    edges,
    edgesr,
    pks,
    pkr,
    fx,
    fzs,
    fzr,
    onehot,
    pmat,
    upx,
    downt,
    parb,
    acc_s,
    acc_down,
    acc_up,
    mlp_src,
    rest_src,
    mlp1,
    mlp2,
    mlp3,
    mlpg,
    rest1,
    rest2,
    rest3,
    restg,
    halo_send,
    halo_recv,
    fx_send,
    fx_recv,
    fz_send,
    fz_recv,
    in_sems,
    fields_ref,
    cot_ref,
    mask_ref,
    seam_ref,
    depth_ref,
    gain_ref,
    bias_ref,
    scale_ref,
    upt_ref,
    upb_ref,
    down_ref,
    *part_sems,
):
    at = Place(dims)
    nlon, nlat, nx, nzc, ng = at.nlon, at.nlat, at.nx, at.nzc, at.ng
    lon, lat, mx, mzc, mg = at.lon, at.lat, at.mx, at.mzc, at.mg
    place = at.place
    left, right = (lon + nlon - 1) % nlon, (lon + 1) % nlon
    down_lat, up_lat = (lat + nlat - 1) % nlat, (lat + 1) % nlat
    lats = (down_lat, lat, up_lat)
    is_top = lat == nlat - 1
    is_bottom = lat == 0
    mlp_sum = PartSum(at, mlp_src, (mlp1, mlp2, mlp3, mlpg), part_sems[:8], nlat)
    rest_sum = PartSum(at, rest_src, (rest1, rest2, rest3, restg), part_sems[8:], restg.shape[0])

    barrier = pltpu.get_barrier_semaphore()

    def hail(a, b):
        pl.semaphore_signal(barrier, inc=1, device_id=place(a, b), device_id_type=MESH)

    for b in lats:
        hail(left, b)
        hail(right, b)
    hail(lon, down_lat)
    hail(lon, up_lat)

    @pl.loop(1, nlat)
    def _(j):
        hail(lon, (lat + j) % nlat)

    @pl.loop(1, ng)
    def _(j):
        hail(at.lon_of_group((mg + j) % ng), lat)

    @pl.loop(1, nzc)
    def _(j):
        hail(mx * nzc + (mzc + j) % nzc, lat)

    loads = [
        pltpu.make_async_copy(src, dst, in_sems.at[n])
        for n, (src, dst) in enumerate(
            (
                (fields_hbm, fields_ref),
                (cot_hbm, cot_ref),
                (mask_hbm, mask_ref),
                (seam_hbm, seam_ref),
                (depth_hbm, depth_ref),
                (gain_hbm, gain_ref),
                (bias_hbm, bias_ref),
                (scale_hbm, scale_ref),
                (upt_hbm, upt_ref),
                (upb_hbm, upb_ref),
                (down_hbm, down_ref),
            )
        )
    ]
    for load in loads:
        load.start()

    lane = lax.broadcasted_iota(jnp.int32, (C, L), 1)
    slot_of_lane = lane // 8
    low_half = lane < 64

    def row_copies(ph):
        return [
            remote(edges.at[ph, 0], edgesr.at[ph, 1],
                   halo_send.at[ph, 0], halo_recv.at[ph, 0], place(lon, down_lat)),
            remote(edges.at[ph, 1], edgesr.at[ph, 0],
                   halo_send.at[ph, 1], halo_recv.at[ph, 1], place(lon, up_lat)),
        ]

    def pack_copies(ph, kinds, src):
        return [
            remote(pks.at[src, side], pkr.at[ph, side, k],
                   halo_send.at[ph, 2 + 3 * side + k], halo_recv.at[ph, 2 + 3 * side + k], place(to, lats[k]))
            for side, to in ((0, left), (1, right))
            for k in kinds
        ]

    def pack(src, row, which):
        low = jnp.zeros((C, L), F32)
        high = jnp.zeros((C, L), F32)
        for i in which:
            here = slot_of_lane == i
            low = jnp.where(here, roll(row(i), 8 * i), low)
            high = jnp.where(here, roll(row(i), 8 * i + 8), high)
        pks[src, 0] = low.astype(BF16)
        pks[src, 1] = high.astype(BF16)

    def unpack(ph, rows):
        for k, ext_rows, first in ((2, range(0, 3), 13), (1, range(3, R + 3), -3), (0, range(R + 3, RE), -R - 3)):
            from_right = pkr[ph, 0, k].astype(F32)
            from_left = pkr[ph, 1, k].astype(F32)
            for u in ext_rows:
                i = u + first
                hal[u] = jnp.where(low_half, roll(from_right, -8 * i), roll(from_left, 120 - 8 * i))
        rows[0:3] = edgesr[ph, 0].astype(F32)
        rows[R + 3 : RE] = edgesr[ph, 1].astype(F32)

    def shifted(q, main, halo, lanes):
        if q == 3:
            return main
        edge = lanes >= 125 + q if q < 3 else lanes < q - 3
        return roll(jnp.where(edge, halo, main), 3 - q)

    def part_of(s):
        return pl.ds(pl.multiple_of(s * 8, 8), 8)

    def fold_copy(ph, j, mine):
        to = (mx + j) % nx
        slot = mx if mine else to
        return remote(edges.at[ph, 1], fx.at[ph, slot], fx_send.at[ph, to], fx_recv.at[ph, slot],
                      place(to * nzc + mzc, lat))

    def fold_copy2(ph, j, mine):
        t = (mzc + j) % nzc
        slot = mzc if mine else t
        return remote(fzs.at[ph, t], fzr.at[ph, slot], fz_send.at[ph, t], fz_recv.at[ph, slot],
                      place(mx * nzc + t, lat))

    def fold_first(ph):
        fx[ph, mx] = edges[ph, 1]

        @pl.loop(1, nx)
        def _(j):
            fold_copy(ph, j, True).start()

    def fold_second(ph):
        @pl.loop(1, nx)
        def _(j):
            fold_copy(ph, j, False).wait()

        held = jnp.concatenate([fx[ph, x].reshape(3 * C, L) for x in range(nx)], axis=1)

        @pl.loop(0, nzc)
        def _(t):
            got = dot(held, onehot[t])
            mirrored = [got[C * (2 - k) : C * (3 - k)] for k in range(3)]
            slot = slot_of_lane % 8
            ends = mirrored[2][:, L:]
            for k in (1, 0):
                ends = jnp.where(slot == k, mirrored[k][:, L:], ends)
            for k in range(3):
                fzs[ph, t, k] = mirrored[k][:, :L].astype(BF16)
            fzs[ph, t, 3] = ends.astype(BF16)

        fzr[ph, mzc] = fzs[ph, mzc]

        @pl.loop(1, nzc)
        def _(j):
            fold_copy2(ph, j, True).start()

    def fold_last(ph):
        @pl.loop(1, nzc)
        def _(j):
            fold_copy2(ph, j, False).wait()

        total = fzr[ph, 0].astype(F32)
        for t in range(1, nzc):
            total = total + fzr[ph, t].astype(F32)
        halos = [
            jnp.where(low_half, roll(total[3], -8 * k), roll(total[3], 56 - 8 * k))
            for k in range(3)
        ]
        return [total[k] for k in range(3)], halos

    loads[0].wait()
    rows_f[...] = fields_ref[...].astype(F32).reshape(C * R, L)
    for i in range(R):
        xf[3 + i] = rows_f[pl.ds(i, C, stride=R), :]
    edges[0, 0] = xf[3:6].astype(BF16)
    edges[0, 1] = xf[R : R + 3].astype(BF16)
    pack(0, lambda i: xf[3 + i], range(R))
    pl.semaphore_wait(barrier, 8 + (nlat - 1) + (ng - 1) + (nzc - 1))
    sent = row_copies(0) + pack_copies(0, (0, 1, 2), 0)
    for copy in sent:
        copy.start()
    for load in loads[1:]:
        load.wait()

    @pl.when(is_top)
    def _():
        fold_first(0)
        partner = seam_ref[0:1, 0:1]
        rows_i = lax.broadcasted_iota(jnp.int32, (nx * L, 2 * L), 0)
        held_col = L * ((rows_i // L) * nzc + mzc) + rows_i % L
        col = lax.broadcasted_iota(jnp.int32, (1, 2 * L), 1)
        packed = col - L
        ahead = jnp.where(packed < 64, L + packed % 8, packed % 8 - 8)
        offset = jnp.where(col < L, col, ahead)

        @pl.loop(0, nzc)
        def _(t):
            wanted = (partner - L * (mx * nzc + t) - offset) & (nlon * L - 1)
            onehot[t] = jnp.where(held_col == wanted, 1.0, 0.0).astype(BF16)

    def eye(n):
        return jnp.where(
            lax.broadcasted_iota(jnp.int32, (n, n), 0) == lax.broadcasted_iota(jnp.int32, (n, n), 1), 1.0, 0.0
        ).astype(BF16)

    pmat[...] = jnp.zeros_like(pmat)
    for a in range(7):
        pmat[8 * a : 8 * a + 7] = depth_ref[a].astype(F32)
    for n, ref in enumerate((gain_ref, bias_ref, scale_ref)):
        pmat[56 + n : 57 + n] = ref[...].astype(F32)
    par = nt_dot(eye(C), pmat[...].astype(BF16))
    for a in range(7):
        for q in range(7):
            wts[a * 7 + q] = jnp.broadcast_to(par[:, 8 * a + q : 8 * a + q + 1], (C, L))
    for n in range(3):
        parb[n] = jnp.broadcast_to(par[:, 56 + n : 57 + n], (C, WIDE))
    first_row = lax.broadcasted_iota(jnp.int32, (16, HID), 0) == 0
    upb = upb_ref[...].astype(F32)
    upb = jnp.concatenate([upb[0:1], upb[1:2]], axis=1)
    bias_row = jnp.where(first_row, jnp.broadcast_to(upb, (16, HID)), 0.0)
    with_bias = jnp.concatenate([upt_ref[...], bias_row.astype(BF16)], axis=0)
    upx[...] = nt_dot(eye(HID), with_bias).astype(BF16)
    downt[...] = nt_dot(eye(HID), down_ref[...]).astype(BF16)
    acc_s[...] = jnp.zeros_like(acc_s)
    acc_down[...] = jnp.zeros_like(acc_down)
    acc_up[...] = jnp.zeros_like(acc_up)
    rows_f[...] = cot_ref[...].astype(F32).reshape(C * R, L)
    for i in range(R):
        gmask[i] = rows_f[pl.ds(i, C, stride=R), :] * mask_ref[i : i + 1, :].astype(F32)

    @pl.when(is_top)
    def _():
        fold_second(0)

    for copy in sent:
        copy.wait()
    unpack(0, xf)

    @pl.when(is_bottom)
    def _():
        for u in range(3):
            xf[u] = jnp.zeros((C, L), F32)
            hal[u] = jnp.zeros((C, L), F32)

    @pl.when(is_top)
    def _():
        mains, halos = fold_last(0)
        for k in range(3):
            xf[R + 3 + k] = mains[k]
            hal[R + 3 + k] = halos[k]

    @pl.loop(0, C // 8)
    def _(s):
        cs = part_of(s)
        lanes = lax.broadcasted_iota(jnp.int32, (RE, 8, L), 2)
        total = jnp.zeros((R, 8, L), F32)
        for q in range(7):
            ext = shifted(q, xf[:, cs, :], hal[:, cs, :], lanes)
            shifts[q, :, cs, :] = ext
            for a in range(7):
                total = total + wts[a * 7 + q, cs, :][None] * ext[a : a + R]
        conv[:, cs, :] = total

    def flat(x):
        return jnp.concatenate([x[i] for i in range(BLOCK)], axis=1)

    @pl.loop(0, R // BLOCK)
    def _(step):
        first = BLOCK * ((3 * step) % (R // BLOCK))
        rows = pl.ds(first, BLOCK)
        gain, bias, scale = parb[0], parb[1], parb[2]
        x = flat(conv[rows])
        mean = jnp.mean(x, axis=0, keepdims=True)
        x = x - mean
        rstd = lax.rsqrt(jnp.mean(x * x, axis=0, keepdims=True) + 1e-06)
        xhat = x * rstd
        normed = (xhat * gain + bias).astype(BF16)
        normed_one = jnp.concatenate([normed, jnp.ones((16, WIDE), BF16)], axis=0)
        pre = dot(upx[...], normed_one)
        phi, density = phi_and_density(pre)
        hidden = (pre * phi).astype(BF16)
        slope = phi + pre * density * PDF
        branch = dot(down_ref[...], hidden)
        mask = mask_ref[rows, :].astype(F32)
        mask = jnp.concatenate([mask[i : i + 1] for i in range(BLOCK)], axis=1)
        out = mask * (flat(xf[pl.ds(3 + first, BLOCK)]) + scale * branch)
        g = flat(gmask[rows])
        d_branch = (g * scale).astype(BF16)
        acc_s[2] += g * branch
        acc_down[...] += nt_dot(d_branch, hidden)
        d_hidden = dot(downt[...], d_branch)
        d_pre = (d_hidden * slope).astype(BF16)
        acc_up[...] += nt_dot(normed_one, d_pre)
        d_normed = dot(upt_ref[...], d_pre)
        acc_s[0] += d_normed * xhat
        acc_s[1] += d_normed
        gd = d_normed * gain
        d_conv = rstd * (
            gd
            - jnp.mean(gd, axis=0, keepdims=True)
            - xhat * jnp.mean(gd * xhat, axis=0, keepdims=True)
        )
        d_conv = d_conv.astype(BF16).astype(F32)
        for i in range(BLOCK):
            outr[first + i] = out[:, L * i : L * (i + 1)]
            df[3 + first + i] = d_conv[:, L * i : L * (i + 1)]

        @pl.when(step == 1)
        def _():
            edges[1, 0] = df[3:6].astype(BF16)
            edges[1, 1] = df[R : R + 3].astype(BF16)
            pack(1, lambda i: df[3 + i], (0, 1, 2, 13, 14, 15))
            for copy in row_copies(1) + pack_copies(1, (0, 2), 1):
                copy.start()

            @pl.when(is_top)
            def _():
                fold_first(1)

    pack(2, lambda i: df[3 + i], range(R))
    for copy in pack_copies(1, (1,), 2):
        copy.start()

    up = acc_up[...]
    mlp_src[0:64] = up[:64, :L]
    mlp_src[64:128] = up[:64, L:]
    down = acc_down[...]
    mlp_src[128:192] = down[:, :L]
    mlp_src[192:256] = down[:, L:]
    mlp_sum.step1()

    @pl.when(is_top)
    def _():
        fold_second(1)

    @pl.loop(0, C // 8)
    def _(s):
        cs = part_of(s)
        d_conv = df[3 : R + 3, cs, :]
        lanes = lax.broadcasted_iota(jnp.int32, (8, L), 1)
        got = jnp.zeros((8, L), F32)
        for q in range(7):
            ext = shifts[q, :, cs, :]
            for a in range(7):
                tap = jnp.sum(d_conv * ext[a : a + R], axis=0)
                got = jnp.where(lanes == a * 8 + q, jnp.sum(tap, axis=1, keepdims=True), got)
        for n in range(3):
            got = jnp.where(lanes == 56 + n, jnp.sum(acc_s[n, cs, :], axis=1, keepdims=True), got)
        rows_f[cs, :] = got

    rows_f[C : 2 * C] = jnp.zeros((C, L), F32)
    taps = jnp.transpose(rows_f[0:L, :])[:C]
    up_b = up[C : C + 1]
    row_of = lax.broadcasted_iota(jnp.int32, (C, L), 0)
    for k in range(4):
        piece = jnp.broadcast_to(up_b[:, L * (k // 2) : L * (k // 2) + L], (C, L))
        taps = jnp.where(row_of == 59 + k, roll(piece, 64 * (k % 2)), taps)
    rest_src[...] = jnp.where(low_half[:32], taps[:32], roll(taps[32:], 64))
    rest_sum.step1()
    mlp_sum.step2()

    for copy in row_copies(1) + pack_copies(1, (0, 2), 1) + pack_copies(1, (1,), 2):
        copy.wait()
    unpack(1, df)

    def clear(u):
        df[u] = jnp.zeros((C, L), F32)
        hal[u] = jnp.zeros((C, L), F32)

    @pl.when(is_bottom)
    def _():
        for u in range(3):
            clear(u)

    @pl.when(is_top)
    def _():
        for u in range(R + 3, RE):
            clear(u)

    def adjoint(first, last):
        @pl.loop(first, last)
        def _(s):
            cs = part_of(s)
            lanes = lax.broadcasted_iota(jnp.int32, (RE, 8, L), 2)
            total = gmask[:, cs, :]
            for q in range(7):
                ext = shifted(6 - q, df[:, cs, :], hal[:, cs, :], lanes)
                for a in range(7):
                    total = total + wts[a * 7 + q, cs, :][None] * ext[6 - a : 6 - a + R]
            gmask[:, cs, :] = total

    adjoint(0, C // 16)
    rest_sum.step2()
    mlp_sum.step3()
    adjoint(C // 16, C // 8)
    rest_sum.step3()
    mlp_sum.step4()

    @pl.when(is_top)
    def _():
        mains, halos = fold_last(1)
        for k in range(3):
            for q in range(7):
                fshift[q, k] = shifted(q, mains[k], halos[k], lane)
        for k in range(3):
            total = gmask[R - 1 - k]
            for a in range(k + 4, 7):
                for q in range(7):
                    total = total + wts[a * 7 + q] * fshift[q, a - k - 4]
            gmask[R - 1 - k] = total

    for i in range(R):
        rows_f[pl.ds(i, C, stride=R), :] = gmask[i]
    gf_ref[...] = rows_f[...].reshape(C, R, L).astype(BF16)
    rest_sum.step4()
    for i in range(R):
        rows_f[pl.ds(i, C, stride=R), :] = outr[i]
    out_ref[...] = rows_f[...].reshape(C, R, L).astype(BF16)
    mlp_sum.finish()
    for p in range(nlat):
        mlp_ref[p * mlp_sum.chunk : (p + 1) * mlp_sum.chunk] = mlpg[p]
    rest_sum.finish()
    for p in range(restg.shape[0]):
        rest_ref[p * rest_sum.chunk : (p + 1) * rest_sum.chunk] = restg[p]


def unpack_sums(out_ref, gf_ref, mlp_ref, rest_ref, o_out, o_gf, o_depth, o_gain, o_bias, o_up, o_upb, o_down, o_scale, sems):
    stores = [pltpu.make_async_copy(out_ref, o_out, sems.at[0]), pltpu.make_async_copy(gf_ref, o_gf, sems.at[1])]
    for store in stores:
        store.start()
    o_up[:, :L] = mlp_ref[0:64]
    o_up[:, L:] = mlp_ref[64:128]
    o_down[:, :L] = mlp_ref[128:192]
    o_down[:, L:] = mlp_ref[192:256]
    low = rest_ref[...]
    high = pltpu.roll(low, 64, 1)
    for a in range(7):
        part = low[8 * a : 8 * a + 7] if a < 4 else high[8 * a - 32 : 8 * a - 25]
        o_depth[a] = part[:, :C]
    o_gain[...] = high[24:25, :C]
    o_bias[...] = high[25:26, :C]
    o_scale[...] = high[26:27, :C]
    lane = lax.broadcasted_iota(jnp.int32, (1, L), 1)
    for k in range(2):
        o_upb[:, L * k : L * (k + 1)] = jnp.where(lane < 64, high[27 + 2 * k : 28 + 2 * k], low[28 + 2 * k : 29 + 2 * k])
    for store in stores:
        store.wait()


def shards(
    dims,
    fields,
    cotangent,
    ocean_mask,
    seam_partner,
    depth_weight,
    norm_gain,
    layer_norm_bias,
    up_weight,
    up_bias,
    down_weight,
    layer_scale,
):
    nlon, nlat, nx = dims
    nzc = nlon // nx
    nz = nzc // CORES
    ng = nx * CORES
    owners = min(4, nlat)
    vmem = pl.BlockSpec(memory_space=pltpu.VMEM)
    hbm = pl.BlockSpec(memory_space=pltpu.HBM)
    dma = pltpu.SemaphoreType.DMA

    def part_bufs(rows, n):
        chunk = rows // n
        return [pltpu.VMEM((count, chunk, L), F32) for count in (nlat, ng, nz, n)]

    def part_sems(n):
        return [dma((count,)) for count in (n, nlat, ng, ng, nz, nz, nlat, n)]

    cells = jax.ShapeDtypeStruct((C, R, L), BF16)
    out, grad_fields, mlp, rest = pl.pallas_call(
        functools.partial(kernel, dims),
        out_shape=(
            pltpu.VMEM((C, R, L), BF16),
            pltpu.VMEM((C, R, L), BF16),
            pltpu.VMEM((MLP_ROWS, L), F32),
            pltpu.VMEM((REST_ROWS, L), F32),
        ),
        in_specs=[hbm] * 11,
        out_specs=(vmem,) * 4,
        scratch_shapes=[
            pltpu.VMEM((C * R, L), F32),
            pltpu.VMEM((R, C, L), F32),
            pltpu.VMEM((R, C, L), F32),
            pltpu.VMEM((RE, C, L), F32),
            pltpu.VMEM((RE, C, L), F32),
            pltpu.VMEM((7, RE, C, L), F32),
            pltpu.VMEM((RE, C, L), F32),
            pltpu.VMEM((7, 3, C, L), F32),
            pltpu.VMEM((49, C, L), F32),
            pltpu.VMEM((R, C, L), F32),
            pltpu.VMEM((2, 2, 3, C, L), BF16),
            pltpu.VMEM((2, 2, 3, C, L), BF16),
            pltpu.VMEM((3, 2, C, L), BF16),
            pltpu.VMEM((2, 2, 3, C, L), BF16),
            pltpu.VMEM((2, nx, 3, C, L), BF16),
            pltpu.VMEM((2, nzc, 4, C, L), BF16),
            pltpu.VMEM((2, nzc, 4, C, L), BF16),
            pltpu.VMEM((nzc, nx * L, 2 * L), BF16),
            pltpu.VMEM((C, C), F32),
            pltpu.VMEM((HID, 80), BF16),
            pltpu.VMEM((HID, C), BF16),
            pltpu.VMEM((3, C, WIDE), F32),
            pltpu.VMEM((3, C, WIDE), F32),
            pltpu.VMEM((C, HID), F32),
            pltpu.VMEM((80, HID), F32),
            pltpu.VMEM((MLP_ROWS, L), F32),
            pltpu.VMEM((REST_ROWS, L), F32),
            *part_bufs(MLP_ROWS, nlat),
            *part_bufs(REST_ROWS, owners),
            dma((2, 8)),
            dma((2, 8)),
            dma((2, nx)),
            dma((2, nx)),
            dma((2, nzc)),
            dma((2, nzc)),
            dma((11,)),
            pltpu.VMEM((C, R, L), BF16),
            pltpu.VMEM((C, R, L), BF16),
            pltpu.VMEM((R, L), jnp.int32),
            pltpu.VMEM((nlon, L), jnp.int32),
            pltpu.VMEM((7, 7, C), BF16),
            pltpu.VMEM((1, C), BF16),
            pltpu.VMEM((1, C), BF16),
            pltpu.VMEM((1, C), BF16),
            pltpu.VMEM((C, HID), BF16),
            pltpu.VMEM((2, L), BF16),
            pltpu.VMEM((C, HID), BF16),
            *part_sems(nlat),
            *part_sems(owners),
        ],
        compiler_params=pltpu.CompilerParams(
            collective_id=0, has_side_effects=True, vmem_limit_bytes=60 * 2**20
        ),
        name="block",
    )(
        fields[0],
        cotangent[0],
        ocean_mask,
        seam_partner.reshape(nlon, L),
        jnp.transpose(depth_weight, (1, 2, 0)),
        norm_gain[None],
        layer_norm_bias[None],
        layer_scale[None],
        up_weight.T,
        up_bias.reshape(2, L),
        down_weight,
    )
    vector = jax.ShapeDtypeStruct((1, C), F32)
    wide = jax.ShapeDtypeStruct((C, HID), F32)
    out, grad_fields, depth, gain, bias, up, up_b, down, scale = pl.pallas_call(
        unpack_sums,
        out_shape=(
            cells,
            cells,
            jax.ShapeDtypeStruct((7, 7, C), F32),
            vector,
            vector,
            wide,
            jax.ShapeDtypeStruct((1, HID), F32),
            wide,
            vector,
        ),
        in_specs=[vmem] * 4,
        out_specs=(hbm,) * 2 + (vmem,) * 7,
        name="unpack_sums",
        scratch_shapes=[dma((2,))],
    )(*(pltpu.with_memory_space_constraint(x, pltpu.VMEM) for x in (out, grad_fields, mlp, rest)))
    return (
        out[None],
        grad_fields[None],
        jnp.transpose(depth, (2, 0, 1)),
        gain[0],
        bias[0],
        up.T,
        up_b[0],
        down,
        scale[0],
    )


def solution(mesh):
    nlon, nlat = mesh.shape["lon"], mesh.shape["lat"]
    dims = (nlon, nlat, 4 if nlon % 16 == 0 else 2)
    cells = P(None, None, "lat", "lon")
    return jax.shard_map(
        functools.partial(shards, dims),
        mesh=mesh,
        in_specs=(cells, cells, P("lat", "lon")) + (P(),) * 8,
        out_specs=(cells, cells) + (P(),) * 7,
        check_vma=False,
    )
```

```python
import functools
import math

import jax
import jax.numpy as jnp
from jax import lax
from jax.experimental import pallas as pl
from jax.experimental.pallas import tpu as pltpu
from jax.sharding import PartitionSpec as P

F32 = jnp.float32
BF16 = jnp.bfloat16
MESH = pl.DeviceIdType.MESH
C = 64
R = 16
L = 128
HID = 256
RE = R + 6
BLOCK = 4
WIDE = BLOCK * L
MLP_ROWS = 256
REST_ROWS = 32
CORES = 2

ERF_P = 0.3275911 / math.sqrt(2.0)
ERF_C = (
    0.5 * 0.254829592,
    0.5 * -0.284496736,
    0.5 * 1.421413741,
    0.5 * -1.453152027,
    0.5 * 1.061405429,
)
PDF = 1.0 / math.sqrt(2.0 * math.pi)


def phi_and_density(v):
    d = 1.0 + ERF_P * jnp.abs(v)
    t = pl.reciprocal(d, approx=True)
    t = t * (2.0 - d * t)
    e = jnp.exp(-0.5 * (v * v))
    poly = ERF_C[4]
    for coef in ERF_C[3::-1]:
        poly = poly * t + coef
    tail = poly * t * e
    return jnp.where(v >= 0.0, 1.0 - tail, tail), e


def nt_dot(a, b):
    return lax.dot_general(a, b, (((1,), (1,)), ((), ())), preferred_element_type=F32)


def dot(a, b):
    return jnp.dot(a, b, preferred_element_type=F32)


def roll(x, amount):
    amount %= L
    return pltpu.roll(x, amount, x.ndim - 1) if amount else x


class PartSum:
    def __init__(self, at, src, bufs, sems, owners):
        self.at, self.src, self.owners = at, src, owners
        self.b1, self.b2, self.b3, self.out = bufs
        self.sems = sems
        self.chunk = self.b1.shape[1]

    def piece(self, p):
        return self.src.at[pl.ds(pl.multiple_of(p * self.chunk, 8), self.chunk)]

    def others(self, count, body):
        @pl.loop(0, count)
        def _(p):
            @pl.when(p != self.at.lat)
            def _():
                body(p)

    def owner(self, body):
        if self.owners == self.at.nlat:
            body()
        else:
            pl.when(self.at.lat < self.owners)(body)

    def first(self, to, slot):
        return remote(self.piece(to), self.b1.at[slot], self.sems[0].at[to], self.sems[1].at[slot],
                      self.at.place(self.at.lon, to))

    def second(self, j, mine):
        at = self.at
        to = (at.mg + j) % at.ng
        slot = at.mg if mine else to
        return remote(self.b2.at[at.mg], self.b2.at[slot], self.sems[2].at[to], self.sems[3].at[slot],
                      at.place(at.lon_of_group(to), at.lat))

    def third(self, j, mine):
        at = self.at
        to = (at.mz + j) % at.nz
        slot = at.mz if mine else to
        return remote(self.b3.at[at.mz], self.b3.at[slot], self.sems[4].at[to], self.sems[5].at[slot],
                      at.place(at.mx * at.nzc + to * CORES + at.mc, at.lat))

    def last(self, to, slot):
        return remote(self.out.at[self.at.lat % self.owners], self.out.at[slot], self.sems[6].at[to],
                      self.sems[7].at[slot], self.at.place(self.at.lon, to))

    def step1(self):
        self.others(self.owners, lambda p: self.first(p, self.at.lat).start())

    def step2(self):
        at = self.at

        def go():
            self.others(at.nlat, lambda p: self.first(0, p).wait_recv())
            self.b1[at.lat] = self.src[pl.ds(pl.multiple_of(at.lat * self.chunk, 8), self.chunk)]
            self.b2[at.mg] = jnp.sum(self.b1[...], axis=0)

            @pl.loop(1, at.ng)
            def _(j):
                self.second(j, True).start()

        self.owner(go)

    def step3(self):
        at = self.at

        def go():
            @pl.loop(1, at.ng)
            def _(j):
                self.second(j, False).wait()

            self.b3[at.mz] = jnp.sum(self.b2[...], axis=0)

            @pl.loop(1, at.nz)
            def _(j):
                self.third(j, True).start()

        self.owner(go)

    def step4(self):
        at = self.at

        def go():
            @pl.loop(1, at.nz)
            def _(j):
                self.third(j, False).wait()

            self.out[at.lat] = jnp.sum(self.b3[...], axis=0)
            self.others(at.nlat, lambda p: self.last(p, at.lat).start())

        self.owner(go)

    def finish(self):
        at = self.at
        self.others(self.owners, lambda p: self.last(p, p).wait_recv())
        self.owner(lambda: self.others(at.nlat, lambda p: self.last(p, at.lat).wait_send()))
        self.others(self.owners, lambda p: self.first(p, at.lat).wait_send())


def remote(src, dst, send, recv, where):
    return pltpu.make_async_remote_copy(
        src_ref=src, dst_ref=dst, send_sem=send, recv_sem=recv,
        device_id=where, device_id_type=MESH,
    )


class Place:
    def __init__(self, dims):
        nlon, nlat, nx = dims
        self.nlon, self.nlat, self.nx = dims
        self.nzc = nlon // nx
        self.nz = self.nzc // CORES
        self.ng = nx * CORES
        self.lon = lax.axis_index("lon")
        self.lat = lax.axis_index("lat")
        self.mx, self.mzc = self.lon // self.nzc, self.lon % self.nzc
        self.mz, self.mc = self.mzc // CORES, self.mzc % CORES
        self.mg = self.mx * CORES + self.mc

    def place(self, a, b):
        return {"lon": a, "lat": b}

    def lon_of_group(self, g):
        return (g // CORES) * self.nzc + self.mz * CORES + g % CORES


def kernel(
    dims,
    fields_hbm,
    cot_hbm,
    mask_hbm,
    seam_hbm,
    depth_hbm,
    gain_hbm,
    bias_hbm,
    scale_hbm,
    upt_hbm,
    upb_hbm,
    down_hbm,
    out_ref,
    gf_ref,
    mlp_ref,
    rest_ref,
    rows_f,
    gmask,
    outr,
    xf,
    df,
    shifts,
    hal,
    fshift,
    wts,
    conv,
    edges,
    edgesr,
    pks,
    pkr,
    fx,
    fzs,
    fzr,
    onehot,
    pmat,
    upx,
    downt,
    parb,
    acc_s,
    acc_down,
    acc_up,
    mlp_src,
    rest_src,
    mlp1,
    mlp2,
    mlp3,
    mlpg,
    rest1,
    rest2,
    rest3,
    restg,
    halo_send,
    halo_recv,
    fx_send,
    fx_recv,
    fz_send,
    fz_recv,
    in_sems,
    fields_ref,
    cot_ref,
    mask_ref,
    seam_ref,
    depth_ref,
    gain_ref,
    bias_ref,
    scale_ref,
    upt_ref,
    upb_ref,
    down_ref,
    *part_sems,
):
    at = Place(dims)
    nlon, nlat, nx, nzc, ng = at.nlon, at.nlat, at.nx, at.nzc, at.ng
    lon, lat, mx, mzc, mg = at.lon, at.lat, at.mx, at.mzc, at.mg
    place = at.place
    left, right = (lon + nlon - 1) % nlon, (lon + 1) % nlon
    down_lat, up_lat = (lat + nlat - 1) % nlat, (lat + 1) % nlat
    lats = (down_lat, lat, up_lat)
    is_top = lat == nlat - 1
    is_bottom = lat == 0
    mlp_sum = PartSum(at, mlp_src, (mlp1, mlp2, mlp3, mlpg), part_sems[:8], nlat)
    rest_sum = PartSum(at, rest_src, (rest1, rest2, rest3, restg), part_sems[8:], restg.shape[0])

    barrier = pltpu.get_barrier_semaphore()

    def hail(a, b):
        pl.semaphore_signal(barrier, inc=1, device_id=place(a, b), device_id_type=MESH)

    for b in lats:
        hail(left, b)
        hail(right, b)
    hail(lon, down_lat)
    hail(lon, up_lat)

    @pl.loop(1, nlat)
    def _(j):
        hail(lon, (lat + j) % nlat)

    @pl.loop(1, ng)
    def _(j):
        hail(at.lon_of_group((mg + j) % ng), lat)

    @pl.loop(1, nzc)
    def _(j):
        hail(mx * nzc + (mzc + j) % nzc, lat)

    loads = [
        pltpu.make_async_copy(src, dst, in_sems.at[n])
        for n, (src, dst) in enumerate(
            (
                (fields_hbm, fields_ref),
                (cot_hbm, cot_ref),
                (mask_hbm, mask_ref),
                (seam_hbm, seam_ref),
                (depth_hbm, depth_ref),
                (gain_hbm, gain_ref),
                (bias_hbm, bias_ref),
                (scale_hbm, scale_ref),
                (upt_hbm, upt_ref),
                (upb_hbm, upb_ref),
                (down_hbm, down_ref),
            )
        )
    ]
    for load in loads:
        load.start()

    lane = lax.broadcasted_iota(jnp.int32, (C, L), 1)
    slot_of_lane = lane // 8
    low_half = lane < 64

    def row_copies(ph):
        return [
            remote(edges.at[ph, 0], edgesr.at[ph, 1],
                   halo_send.at[ph, 0], halo_recv.at[ph, 0], place(lon, down_lat)),
            remote(edges.at[ph, 1], edgesr.at[ph, 0],
                   halo_send.at[ph, 1], halo_recv.at[ph, 1], place(lon, up_lat)),
        ]

    def pack_copies(ph, kinds, src):
        return [
            remote(pks.at[src, side], pkr.at[ph, side, k],
                   halo_send.at[ph, 2 + 3 * side + k], halo_recv.at[ph, 2 + 3 * side + k], place(to, lats[k]))
            for side, to in ((0, left), (1, right))
            for k in kinds
        ]

    def pack(src, row, which):
        low = jnp.zeros((C, L), F32)
        high = jnp.zeros((C, L), F32)
        for i in which:
            here = slot_of_lane == i
            low = jnp.where(here, roll(row(i), 8 * i), low)
            high = jnp.where(here, roll(row(i), 8 * i + 8), high)
        pks[src, 0] = low.astype(BF16)
        pks[src, 1] = high.astype(BF16)

    def unpack(ph, rows):
        for k, ext_rows, first in ((2, range(0, 3), 13), (1, range(3, R + 3), -3), (0, range(R + 3, RE), -R - 3)):
            from_right = pkr[ph, 0, k].astype(F32)
            from_left = pkr[ph, 1, k].astype(F32)
            for u in ext_rows:
                i = u + first
                hal[u] = jnp.where(low_half, roll(from_right, -8 * i), roll(from_left, 120 - 8 * i))
        rows[0:3] = edgesr[ph, 0].astype(F32)
        rows[R + 3 : RE] = edgesr[ph, 1].astype(F32)

    def shifted(q, main, halo, lanes):
        if q == 3:
            return main
        edge = lanes >= 125 + q if q < 3 else lanes < q - 3
        return roll(jnp.where(edge, halo, main), 3 - q)

    def part_of(s):
        return pl.ds(pl.multiple_of(s * 8, 8), 8)

    def fold_copy(ph, j, mine):
        to = (mx + j) % nx
        slot = mx if mine else to
        return remote(fx.at[ph, mx], fx.at[ph, slot], fx_send.at[ph, to], fx_recv.at[ph, slot],
                      place(to * nzc + mzc, lat))

    def fold_copy2(ph, j, mine):
        t = (mzc + j) % nzc
        slot = mzc if mine else t
        return remote(fzs.at[ph, t], fzr.at[ph, slot], fz_send.at[ph, t], fz_recv.at[ph, slot],
                      place(mx * nzc + t, lat))

    def fold_first(ph, rows):
        fx[ph, mx] = rows[R : R + 3].astype(BF16)

        @pl.loop(1, nx)
        def _(j):
            fold_copy(ph, j, True).start()

    def fold_second(ph):
        @pl.loop(1, nx)
        def _(j):
            fold_copy(ph, j, False).wait()

        held = jnp.concatenate([fx[ph, x].reshape(3 * C, L) for x in range(nx)], axis=1)

        @pl.loop(0, nzc)
        def _(t):
            got = dot(held, onehot[t])
            mirrored = [got[C * (2 - k) : C * (3 - k)] for k in range(3)]
            slot = slot_of_lane % 8
            ends = mirrored[2][:, L:]
            for k in (1, 0):
                ends = jnp.where(slot == k, mirrored[k][:, L:], ends)
            for k in range(3):
                fzs[ph, t, k] = mirrored[k][:, :L].astype(BF16)
            fzs[ph, t, 3] = ends.astype(BF16)

        fzr[ph, mzc] = fzs[ph, mzc]

        @pl.loop(1, nzc)
        def _(j):
            fold_copy2(ph, j, True).start()

    def fold_last(ph):
        @pl.loop(1, nzc)
        def _(j):
            fold_copy2(ph, j, False).wait()

        total = fzr[ph, 0].astype(F32)
        for t in range(1, nzc):
            total = total + fzr[ph, t].astype(F32)
        halos = [
            jnp.where(low_half, roll(total[3], -8 * k), roll(total[3], 56 - 8 * k))
            for k in range(3)
        ]
        return [total[k] for k in range(3)], halos

    loads[0].wait()
    rows_f[...] = fields_ref[...].astype(F32).reshape(C * R, L)
    for i in range(R):
        xf[3 + i] = rows_f[pl.ds(i, C, stride=R), :]
    edges[0, 0] = xf[3:6].astype(BF16)
    edges[0, 1] = xf[R : R + 3].astype(BF16)
    pack(0, lambda i: xf[3 + i], range(R))
    pl.semaphore_wait(barrier, 8 + (nlat - 1) + (ng - 1) + (nzc - 1))
    sent = row_copies(0) + pack_copies(0, (0, 1, 2), 0)
    for copy in sent:
        copy.start()
    for load in loads[1:]:
        load.wait()

    @pl.when(is_top)
    def _():
        fold_first(0, xf)
        partner = seam_ref[0:1, 0:1]
        rows_i = lax.broadcasted_iota(jnp.int32, (nx * L, 2 * L), 0)
        held_col = L * ((rows_i // L) * nzc + mzc) + rows_i % L
        col = lax.broadcasted_iota(jnp.int32, (1, 2 * L), 1)
        packed = col - L
        ahead = jnp.where(packed < 64, L + packed % 8, packed % 8 - 8)
        offset = jnp.where(col < L, col, ahead)

        @pl.loop(0, nzc)
        def _(t):
            wanted = (partner - L * (mx * nzc + t) - offset) & (nlon * L - 1)
            onehot[t] = jnp.where(held_col == wanted, 1.0, 0.0).astype(BF16)

    def eye(n):
        return jnp.where(
            lax.broadcasted_iota(jnp.int32, (n, n), 0) == lax.broadcasted_iota(jnp.int32, (n, n), 1), 1.0, 0.0
        ).astype(BF16)

    pmat[...] = jnp.zeros_like(pmat)
    for a in range(7):
        pmat[8 * a : 8 * a + 7] = depth_ref[a].astype(F32)
    for n, ref in enumerate((gain_ref, bias_ref, scale_ref)):
        pmat[56 + n : 57 + n] = ref[...].astype(F32)
    par = nt_dot(eye(C), pmat[...].astype(BF16))
    for a in range(7):
        for q in range(7):
            wts[a * 7 + q] = jnp.broadcast_to(par[:, 8 * a + q : 8 * a + q + 1], (C, L))
    for n in range(3):
        parb[n] = jnp.broadcast_to(par[:, 56 + n : 57 + n], (C, WIDE))
    first_row = lax.broadcasted_iota(jnp.int32, (16, HID), 0) == 0
    upb = upb_ref[...].astype(F32)
    upb = jnp.concatenate([upb[0:1], upb[1:2]], axis=1)
    bias_row = jnp.where(first_row, jnp.broadcast_to(upb, (16, HID)), 0.0)
    with_bias = jnp.concatenate([upt_ref[...], bias_row.astype(BF16)], axis=0)
    upx[...] = nt_dot(eye(HID), with_bias).astype(BF16)
    downt[...] = nt_dot(eye(HID), down_ref[...]).astype(BF16)
    acc_s[...] = jnp.zeros_like(acc_s)
    acc_down[...] = jnp.zeros_like(acc_down)
    acc_up[...] = jnp.zeros_like(acc_up)
    rows_f[...] = cot_ref[...].astype(F32).reshape(C * R, L)
    for i in range(R):
        gmask[i] = rows_f[pl.ds(i, C, stride=R), :] * mask_ref[i : i + 1, :].astype(F32)

    @pl.when(is_top)
    def _():
        fold_second(0)

    for copy in sent:
        copy.wait()
    unpack(0, xf)

    @pl.when(is_bottom)
    def _():
        for u in range(3):
            xf[u] = jnp.zeros((C, L), F32)
            hal[u] = jnp.zeros((C, L), F32)

    def conv_rows(first, count):
        ext_rows = pl.ds(first, count + 6)

        @pl.loop(0, C // 8)
        def _(s):
            cs = part_of(s)
            lanes = lax.broadcasted_iota(jnp.int32, (count + 6, 8, L), 2)
            total = jnp.zeros((count, 8, L), F32)
            for q in range(7):
                ext = shifted(q, xf[ext_rows, cs, :], hal[ext_rows, cs, :], lanes)
                shifts[q, ext_rows, cs, :] = ext
                for a in range(7):
                    total = total + wts[a * 7 + q, cs, :][None] * ext[a : a + count]
            conv[pl.ds(first, count), cs, :] = total

    conv_rows(0, R - BLOCK)
    top_flag = (lat + 1) // nlat

    def flat(x):
        return jnp.concatenate([x[i] for i in range(BLOCK)], axis=1)

    @pl.loop(0, R // BLOCK)
    def _(step):
        first = BLOCK * (((3 - 2 * top_flag) * step) % (R // BLOCK))

        @pl.when(step == 3 * top_flag)
        def _():
            @pl.when(is_top)
            def _():
                mains, halos = fold_last(0)
                for k in range(3):
                    xf[R + 3 + k] = mains[k]
                    hal[R + 3 + k] = halos[k]

            conv_rows(R - BLOCK, BLOCK)

        rows = pl.ds(first, BLOCK)
        gain, bias, scale = parb[0], parb[1], parb[2]
        x = flat(conv[rows])
        mean = jnp.mean(x, axis=0, keepdims=True)
        x = x - mean
        rstd = lax.rsqrt(jnp.mean(x * x, axis=0, keepdims=True) + 1e-06)
        xhat = x * rstd
        normed = (xhat * gain + bias).astype(BF16)
        normed_one = jnp.concatenate([normed, jnp.ones((16, WIDE), BF16)], axis=0)
        pre = dot(upx[...], normed_one)
        phi, density = phi_and_density(pre)
        hidden = (pre * phi).astype(BF16)
        slope = phi + pre * density * PDF
        branch = dot(down_ref[...], hidden)
        mask = mask_ref[rows, :].astype(F32)
        mask = jnp.concatenate([mask[i : i + 1] for i in range(BLOCK)], axis=1)
        out = mask * (flat(xf[pl.ds(3 + first, BLOCK)]) + scale * branch)
        g = flat(gmask[rows])
        d_branch = (g * scale).astype(BF16)
        acc_s[2] += g * branch
        acc_down[...] += nt_dot(d_branch, hidden)
        d_hidden = dot(downt[...], d_branch)
        d_pre = (d_hidden * slope).astype(BF16)
        acc_up[...] += nt_dot(normed_one, d_pre)
        d_normed = dot(upt_ref[...], d_pre)
        acc_s[0] += d_normed * xhat
        acc_s[1] += d_normed
        gd = d_normed * gain
        d_conv = rstd * (
            gd
            - jnp.mean(gd, axis=0, keepdims=True)
            - xhat * jnp.mean(gd * xhat, axis=0, keepdims=True)
        )
        d_conv = d_conv.astype(BF16).astype(F32)
        for i in range(BLOCK):
            outr[first + i] = out[:, L * i : L * (i + 1)]
            df[3 + first + i] = d_conv[:, L * i : L * (i + 1)]

        @pl.when(step == 1)
        def _():
            edges[1, 0] = df[3:6].astype(BF16)
            edges[1, 1] = df[R : R + 3].astype(BF16)
            pack(1, lambda i: df[3 + i], (0, 1, 2, 13, 14, 15))
            for copy in row_copies(1) + pack_copies(1, (0, 2), 1):
                copy.start()

    @pl.when(is_top)
    def _():
        fold_first(1, df)

    pack(2, lambda i: df[3 + i], range(R))
    for copy in pack_copies(1, (1,), 2):
        copy.start()

    up = acc_up[...]
    mlp_src[0:64] = up[:64, :L]
    mlp_src[64:128] = up[:64, L:]
    down = acc_down[...]
    mlp_src[128:192] = down[:, :L]
    mlp_src[192:256] = down[:, L:]
    mlp_sum.step1()

    @pl.loop(0, C // 8)
    def _(s):
        cs = part_of(s)
        d_conv = df[3 : R + 3, cs, :]
        lanes = lax.broadcasted_iota(jnp.int32, (8, L), 1)
        got = jnp.zeros((8, L), F32)
        for q in range(7):
            ext = shifts[q, :, cs, :]
            for a in range(7):
                tap = jnp.sum(d_conv * ext[a : a + R], axis=0)
                got = jnp.where(lanes == a * 8 + q, jnp.sum(tap, axis=1, keepdims=True), got)
        for n in range(3):
            got = jnp.where(lanes == 56 + n, jnp.sum(acc_s[n, cs, :], axis=1, keepdims=True), got)
        rows_f[cs, :] = got

    rows_f[C : 2 * C] = jnp.zeros((C, L), F32)
    taps = jnp.transpose(rows_f[0:L, :])[:C]
    up_b = up[C : C + 1]
    row_of = lax.broadcasted_iota(jnp.int32, (C, L), 0)
    for k in range(4):
        piece = jnp.broadcast_to(up_b[:, L * (k // 2) : L * (k // 2) + L], (C, L))
        taps = jnp.where(row_of == 59 + k, roll(piece, 64 * (k % 2)), taps)
    rest_src[...] = jnp.where(low_half[:32], taps[:32], roll(taps[32:], 64))
    rest_sum.step1()

    @pl.when(is_top)
    def _():
        fold_second(1)

    mlp_sum.step2()

    for copy in row_copies(1) + pack_copies(1, (0, 2), 1) + pack_copies(1, (1,), 2):
        copy.wait()
    unpack(1, df)

    def clear(u):
        df[u] = jnp.zeros((C, L), F32)
        hal[u] = jnp.zeros((C, L), F32)

    @pl.when(is_bottom)
    def _():
        for u in range(3):
            clear(u)

    @pl.when(is_top)
    def _():
        for u in range(R + 3, RE):
            clear(u)

    def adjoint(first, last):
        @pl.loop(first, last)
        def _(s):
            cs = part_of(s)
            lanes = lax.broadcasted_iota(jnp.int32, (RE, 8, L), 2)
            total = gmask[:, cs, :]
            for q in range(7):
                ext = shifted(6 - q, df[:, cs, :], hal[:, cs, :], lanes)
                for a in range(7):
                    total = total + wts[a * 7 + q, cs, :][None] * ext[6 - a : 6 - a + R]
            gmask[:, cs, :] = total

    adjoint(0, C // 16)
    rest_sum.step2()
    mlp_sum.step3()
    adjoint(C // 16, C // 8)
    rest_sum.step3()
    mlp_sum.step4()

    @pl.when(is_top)
    def _():
        mains, halos = fold_last(1)
        for k in range(3):
            for q in range(7):
                fshift[q, k] = shifted(q, mains[k], halos[k], lane)
        for k in range(3):
            total = gmask[R - 1 - k]
            for a in range(k + 4, 7):
                for q in range(7):
                    total = total + wts[a * 7 + q] * fshift[q, a - k - 4]
            gmask[R - 1 - k] = total

    for i in range(R):
        rows_f[pl.ds(i, C, stride=R), :] = gmask[i]
    gf_ref[...] = rows_f[...].reshape(C, R, L).astype(BF16)
    rest_sum.step4()
    for i in range(R):
        rows_f[pl.ds(i, C, stride=R), :] = outr[i]
    out_ref[...] = rows_f[...].reshape(C, R, L).astype(BF16)
    mlp_sum.finish()
    for p in range(nlat):
        mlp_ref[p * mlp_sum.chunk : (p + 1) * mlp_sum.chunk] = mlpg[p]
    rest_sum.finish()
    for p in range(restg.shape[0]):
        rest_ref[p * rest_sum.chunk : (p + 1) * rest_sum.chunk] = restg[p]


def unpack_sums(out_ref, gf_ref, mlp_ref, rest_ref, o_out, o_gf, o_depth, o_gain, o_bias, o_up, o_upb, o_down, o_scale, sems):
    stores = [pltpu.make_async_copy(out_ref, o_out, sems.at[0]), pltpu.make_async_copy(gf_ref, o_gf, sems.at[1])]
    for store in stores:
        store.start()
    o_up[:, :L] = mlp_ref[0:64]
    o_up[:, L:] = mlp_ref[64:128]
    o_down[:, :L] = mlp_ref[128:192]
    o_down[:, L:] = mlp_ref[192:256]
    low = rest_ref[...]
    high = pltpu.roll(low, 64, 1)
    for a in range(7):
        part = low[8 * a : 8 * a + 7] if a < 4 else high[8 * a - 32 : 8 * a - 25]
        o_depth[a] = part[:, :C]
    o_gain[...] = high[24:25, :C]
    o_bias[...] = high[25:26, :C]
    o_scale[...] = high[26:27, :C]
    lane = lax.broadcasted_iota(jnp.int32, (1, L), 1)
    for k in range(2):
        o_upb[:, L * k : L * (k + 1)] = jnp.where(lane < 64, high[27 + 2 * k : 28 + 2 * k], low[28 + 2 * k : 29 + 2 * k])
    for store in stores:
        store.wait()


def shards(
    dims,
    fields,
    cotangent,
    ocean_mask,
    seam_partner,
    depth_weight,
    norm_gain,
    layer_norm_bias,
    up_weight,
    up_bias,
    down_weight,
    layer_scale,
):
    nlon, nlat, nx = dims
    nzc = nlon // nx
    nz = nzc // CORES
    ng = nx * CORES
    owners = min(4, nlat)
    vmem = pl.BlockSpec(memory_space=pltpu.VMEM)
    hbm = pl.BlockSpec(memory_space=pltpu.HBM)
    dma = pltpu.SemaphoreType.DMA

    def part_bufs(rows, n):
        chunk = rows // n
        return [pltpu.VMEM((count, chunk, L), F32) for count in (nlat, ng, nz, n)]

    def part_sems(n):
        return [dma((count,)) for count in (n, nlat, ng, ng, nz, nz, nlat, n)]

    cells = jax.ShapeDtypeStruct((C, R, L), BF16)
    out, grad_fields, mlp, rest = pl.pallas_call(
        functools.partial(kernel, dims),
        out_shape=(
            pltpu.VMEM((C, R, L), BF16),
            pltpu.VMEM((C, R, L), BF16),
            pltpu.VMEM((MLP_ROWS, L), F32),
            pltpu.VMEM((REST_ROWS, L), F32),
        ),
        in_specs=[hbm] * 11,
        out_specs=(vmem,) * 4,
        scratch_shapes=[
            pltpu.VMEM((C * R, L), F32),
            pltpu.VMEM((R, C, L), F32),
            pltpu.VMEM((R, C, L), F32),
            pltpu.VMEM((RE, C, L), F32),
            pltpu.VMEM((RE, C, L), F32),
            pltpu.VMEM((7, RE, C, L), F32),
            pltpu.VMEM((RE, C, L), F32),
            pltpu.VMEM((7, 3, C, L), F32),
            pltpu.VMEM((49, C, L), F32),
            pltpu.VMEM((R, C, L), F32),
            pltpu.VMEM((2, 2, 3, C, L), BF16),
            pltpu.VMEM((2, 2, 3, C, L), BF16),
            pltpu.VMEM((3, 2, C, L), BF16),
            pltpu.VMEM((2, 2, 3, C, L), BF16),
            pltpu.VMEM((2, nx, 3, C, L), BF16),
            pltpu.VMEM((2, nzc, 4, C, L), BF16),
            pltpu.VMEM((2, nzc, 4, C, L), BF16),
            pltpu.VMEM((nzc, nx * L, 2 * L), BF16),
            pltpu.VMEM((C, C), F32),
            pltpu.VMEM((HID, 80), BF16),
            pltpu.VMEM((HID, C), BF16),
            pltpu.VMEM((3, C, WIDE), F32),
            pltpu.VMEM((3, C, WIDE), F32),
            pltpu.VMEM((C, HID), F32),
            pltpu.VMEM((80, HID), F32),
            pltpu.VMEM((MLP_ROWS, L), F32),
            pltpu.VMEM((REST_ROWS, L), F32),
            *part_bufs(MLP_ROWS, nlat),
            *part_bufs(REST_ROWS, owners),
            dma((2, 8)),
            dma((2, 8)),
            dma((2, nx)),
            dma((2, nx)),
            dma((2, nzc)),
            dma((2, nzc)),
            dma((11,)),
            pltpu.VMEM((C, R, L), BF16),
            pltpu.VMEM((C, R, L), BF16),
            pltpu.VMEM((R, L), jnp.int32),
            pltpu.VMEM((nlon, L), jnp.int32),
            pltpu.VMEM((7, 7, C), BF16),
            pltpu.VMEM((1, C), BF16),
            pltpu.VMEM((1, C), BF16),
            pltpu.VMEM((1, C), BF16),
            pltpu.VMEM((C, HID), BF16),
            pltpu.VMEM((2, L), BF16),
            pltpu.VMEM((C, HID), BF16),
            *part_sems(nlat),
            *part_sems(owners),
        ],
        compiler_params=pltpu.CompilerParams(
            collective_id=0, has_side_effects=True, vmem_limit_bytes=60 * 2**20
        ),
        name="block",
    )(
        fields[0],
        cotangent[0],
        ocean_mask,
        seam_partner.reshape(nlon, L),
        jnp.transpose(depth_weight, (1, 2, 0)),
        norm_gain[None],
        layer_norm_bias[None],
        layer_scale[None],
        up_weight.T,
        up_bias.reshape(2, L),
        down_weight,
    )
    vector = jax.ShapeDtypeStruct((1, C), F32)
    wide = jax.ShapeDtypeStruct((C, HID), F32)
    out, grad_fields, depth, gain, bias, up, up_b, down, scale = pl.pallas_call(
        unpack_sums,
        out_shape=(
            cells,
            cells,
            jax.ShapeDtypeStruct((7, 7, C), F32),
            vector,
            vector,
            wide,
            jax.ShapeDtypeStruct((1, HID), F32),
            wide,
            vector,
        ),
        in_specs=[vmem] * 4,
        out_specs=(hbm,) * 2 + (vmem,) * 7,
        name="unpack_sums",
        scratch_shapes=[dma((2,))],
    )(*(pltpu.with_memory_space_constraint(x, pltpu.VMEM) for x in (out, grad_fields, mlp, rest)))
    return (
        out[None],
        grad_fields[None],
        jnp.transpose(depth, (2, 0, 1)),
        gain[0],
        bias[0],
        up.T,
        up_b[0],
        down,
        scale[0],
    )


def solution(mesh):
    nlon, nlat = mesh.shape["lon"], mesh.shape["lat"]
    dims = (nlon, nlat, 4 if nlon % 16 == 0 else 2)
    cells = P(None, None, "lat", "lon")
    return jax.shard_map(
        functools.partial(shards, dims),
        mesh=mesh,
        in_specs=(cells, cells, P("lat", "lon")) + (P(),) * 8,
        out_specs=(cells, cells) + (P(),) * 7,
        check_vma=False,
    )
```

```python
import functools
import math

import jax
import jax.numpy as jnp
from jax import lax
from jax.experimental import pallas as pl
from jax.experimental.pallas import tpu as pltpu
from jax.sharding import PartitionSpec as P

F32 = jnp.float32
BF16 = jnp.bfloat16
MESH = pl.DeviceIdType.MESH
C = 64
R = 16
L = 128
HID = 256
RE = R + 6
BLOCK = 4
WIDE = BLOCK * L
MLP_ROWS = 256
REST_ROWS = 32
CORES = 2

ERF_P = 0.3275911 / math.sqrt(2.0)
ERF_C = (
    0.5 * 0.254829592,
    0.5 * -0.284496736,
    0.5 * 1.421413741,
    0.5 * -1.453152027,
    0.5 * 1.061405429,
)
PDF = 1.0 / math.sqrt(2.0 * math.pi)


def phi_and_density(v):
    d = 1.0 + ERF_P * jnp.abs(v)
    t = pl.reciprocal(d, approx=True)
    t = t * (2.0 - d * t)
    e = jnp.exp(-0.5 * (v * v))
    poly = ERF_C[4]
    for coef in ERF_C[3::-1]:
        poly = poly * t + coef
    tail = poly * t * e
    return jnp.where(v >= 0.0, 1.0 - tail, tail), e


def nt_dot(a, b):
    return lax.dot_general(a, b, (((1,), (1,)), ((), ())), preferred_element_type=F32)


def dot(a, b):
    return jnp.dot(a, b, preferred_element_type=F32)


def roll(x, amount):
    amount %= L
    return pltpu.roll(x, amount, x.ndim - 1) if amount else x


class PartSum:
    def __init__(self, at, src, bufs, sems, owners):
        self.at, self.src, self.owners = at, src, owners
        self.b1, self.b2, self.b3, self.out = bufs
        self.sems = sems
        self.chunk = self.b1.shape[1]

    def piece(self, p):
        return self.src.at[pl.ds(pl.multiple_of(p * self.chunk, 8), self.chunk)]

    def others(self, count, body):
        @pl.loop(0, count)
        def _(p):
            @pl.when(p != self.at.lat)
            def _():
                body(p)

    def owner(self, body):
        if self.owners == self.at.nlat:
            body()
        else:
            pl.when(self.at.lat < self.owners)(body)

    def first(self, to, slot):
        return remote(self.piece(to), self.b1.at[slot], self.sems[0].at[to], self.sems[1].at[slot],
                      self.at.place(self.at.lon, to))

    def second(self, j, mine):
        at = self.at
        to = (at.mg + j) % at.ng
        slot = at.mg if mine else to
        return remote(self.b2.at[at.mg], self.b2.at[slot], self.sems[2].at[to], self.sems[3].at[slot],
                      at.place(at.lon_of_group(to), at.lat))

    def third(self, j, mine):
        at = self.at
        to = (at.mz + j) % at.nz
        slot = at.mz if mine else to
        return remote(self.b3.at[at.mz], self.b3.at[slot], self.sems[4].at[to], self.sems[5].at[slot],
                      at.place(at.mx * at.nzc + to * CORES + at.mc, at.lat))

    def last(self, to, slot):
        return remote(self.out.at[self.at.lat % self.owners], self.out.at[slot], self.sems[6].at[to],
                      self.sems[7].at[slot], self.at.place(self.at.lon, to))

    def step1(self):
        self.others(self.owners, lambda p: self.first(p, self.at.lat).start())

    def step2(self):
        at = self.at

        def go():
            self.others(at.nlat, lambda p: self.first(0, p).wait_recv())
            self.b1[at.lat] = self.src[pl.ds(pl.multiple_of(at.lat * self.chunk, 8), self.chunk)]
            self.b2[at.mg] = jnp.sum(self.b1[...], axis=0)

            @pl.loop(1, at.ng)
            def _(j):
                self.second(j, True).start()

        self.owner(go)

    def step3(self):
        at = self.at

        def go():
            @pl.loop(1, at.ng)
            def _(j):
                self.second(j, False).wait()

            self.b3[at.mz] = jnp.sum(self.b2[...], axis=0)

            @pl.loop(1, at.nz)
            def _(j):
                self.third(j, True).start()

        self.owner(go)

    def step4(self):
        at = self.at

        def go():
            @pl.loop(1, at.nz)
            def _(j):
                self.third(j, False).wait()

            self.out[at.lat] = jnp.sum(self.b3[...], axis=0)
            self.others(at.nlat, lambda p: self.last(p, at.lat).start())

        self.owner(go)

    def finish(self):
        at = self.at
        self.others(self.owners, lambda p: self.last(p, p).wait_recv())
        self.owner(lambda: self.others(at.nlat, lambda p: self.last(p, at.lat).wait_send()))
        self.others(self.owners, lambda p: self.first(p, at.lat).wait_send())


def remote(src, dst, send, recv, where):
    return pltpu.make_async_remote_copy(
        src_ref=src, dst_ref=dst, send_sem=send, recv_sem=recv,
        device_id=where, device_id_type=MESH,
    )


class Place:
    def __init__(self, dims):
        nlon, nlat, nx = dims
        self.nlon, self.nlat, self.nx = dims
        self.nzc = nlon // nx
        self.nz = self.nzc // CORES
        self.ng = nx * CORES
        self.lon = lax.axis_index("lon")
        self.lat = lax.axis_index("lat")
        self.mx, self.mzc = self.lon // self.nzc, self.lon % self.nzc
        self.mz, self.mc = self.mzc // CORES, self.mzc % CORES
        self.mg = self.mx * CORES + self.mc

    def place(self, a, b):
        return {"lon": a, "lat": b}

    def lon_of_group(self, g):
        return (g // CORES) * self.nzc + self.mz * CORES + g % CORES


def kernel(
    dims,
    fields_hbm,
    cot_hbm,
    mask_hbm,
    seam_hbm,
    depth_hbm,
    gain_hbm,
    bias_hbm,
    scale_hbm,
    upt_hbm,
    upb_hbm,
    down_hbm,
    out_ref,
    gf_ref,
    mlp_ref,
    rest_ref,
    rows_f,
    gmask,
    outr,
    xf,
    df,
    shifts,
    hal,
    fshift,
    wts,
    conv,
    edges,
    edgesr,
    pks,
    pkr,
    fx,
    fsel,
    fz,
    fout,
    fin,
    onehot,
    pmat,
    upx,
    downt,
    parb,
    acc_s,
    acc_down,
    acc_up,
    mlp_src,
    rest_src,
    mlp1,
    mlp2,
    mlp3,
    mlpg,
    rest1,
    rest2,
    rest3,
    restg,
    halo_send,
    halo_recv,
    fx_send,
    fx_recv,
    fz_send,
    fz_recv,
    fc_send,
    fc_recv,
    in_sems,
    fields_ref,
    cot_ref,
    mask_ref,
    seam_ref,
    depth_ref,
    gain_ref,
    bias_ref,
    scale_ref,
    upt_ref,
    upb_ref,
    down_ref,
    *part_sems,
):
    at = Place(dims)
    nlon, nlat, nx, nzc, ng = at.nlon, at.nlat, at.nx, at.nzc, at.ng
    lon, lat, mx, mzc, mg = at.lon, at.lat, at.mx, at.mzc, at.mg
    nz, mz, mc = at.nz, at.mz, at.mc
    place = at.place
    left, right = (lon + nlon - 1) % nlon, (lon + 1) % nlon
    down_lat, up_lat = (lat + nlat - 1) % nlat, (lat + 1) % nlat
    lats = (down_lat, lat, up_lat)
    is_top = lat == nlat - 1
    is_bottom = lat == 0
    mlp_sum = PartSum(at, mlp_src, (mlp1, mlp2, mlp3, mlpg), part_sems[:8], nlat)
    rest_sum = PartSum(at, rest_src, (rest1, rest2, rest3, restg), part_sems[8:], restg.shape[0])

    barrier = pltpu.get_barrier_semaphore()

    def hail(a, b):
        pl.semaphore_signal(barrier, inc=1, device_id=place(a, b), device_id_type=MESH)

    for b in lats:
        hail(left, b)
        hail(right, b)
    hail(lon, down_lat)
    hail(lon, up_lat)

    @pl.loop(1, nlat)
    def _(j):
        hail(lon, (lat + j) % nlat)

    @pl.loop(1, ng)
    def _(j):
        hail(at.lon_of_group((mg + j) % ng), lat)

    @pl.loop(1, nz)
    def _(j):
        hail(mx * nzc + (mz + j) % nz * CORES + mc, lat)

    loads = [
        pltpu.make_async_copy(src, dst, in_sems.at[n])
        for n, (src, dst) in enumerate(
            (
                (fields_hbm, fields_ref),
                (cot_hbm, cot_ref),
                (mask_hbm, mask_ref),
                (seam_hbm, seam_ref),
                (depth_hbm, depth_ref),
                (gain_hbm, gain_ref),
                (bias_hbm, bias_ref),
                (scale_hbm, scale_ref),
                (upt_hbm, upt_ref),
                (upb_hbm, upb_ref),
                (down_hbm, down_ref),
            )
        )
    ]
    for load in loads:
        load.start()

    lane = lax.broadcasted_iota(jnp.int32, (C, L), 1)
    slot_of_lane = lane // 8
    low_half = lane < 64

    def row_copies(ph):
        return [
            remote(edges.at[ph, 0], edgesr.at[ph, 1],
                   halo_send.at[ph, 0], halo_recv.at[ph, 0], place(lon, down_lat)),
            remote(edges.at[ph, 1], edgesr.at[ph, 0],
                   halo_send.at[ph, 1], halo_recv.at[ph, 1], place(lon, up_lat)),
        ]

    def pack_copies(ph, kinds, src):
        return [
            remote(pks.at[src, side], pkr.at[ph, side, k],
                   halo_send.at[ph, 2 + 3 * side + k], halo_recv.at[ph, 2 + 3 * side + k], place(to, lats[k]))
            for side, to in ((0, left), (1, right))
            for k in kinds
        ]

    def pack(src, row, which):
        low = jnp.zeros((C, L), F32)
        high = jnp.zeros((C, L), F32)
        for i in which:
            here = slot_of_lane == i
            low = jnp.where(here, roll(row(i), 8 * i), low)
            high = jnp.where(here, roll(row(i), 8 * i + 8), high)
        pks[src, 0] = low.astype(BF16)
        pks[src, 1] = high.astype(BF16)

    def unpack(ph, rows):
        for k, ext_rows, first in ((2, range(0, 3), 13), (1, range(3, R + 3), -3), (0, range(R + 3, RE), -R - 3)):
            from_right = pkr[ph, 0, k].astype(F32)
            from_left = pkr[ph, 1, k].astype(F32)
            for u in ext_rows:
                i = u + first
                hal[u] = jnp.where(low_half, roll(from_right, -8 * i), roll(from_left, 120 - 8 * i))
        rows[0:3] = edgesr[ph, 0].astype(F32)
        rows[R + 3 : RE] = edgesr[ph, 1].astype(F32)

    def shifted(q, main, halo, lanes):
        if q == 3:
            return main
        edge = lanes >= 125 + q if q < 3 else lanes < q - 3
        return roll(jnp.where(edge, halo, main), 3 - q)

    def part_of(s):
        return pl.ds(pl.multiple_of(s * 8, 8), 8)

    def fold_copy(ph, j, mine):
        to = (mx + j) % nx
        slot = mx if mine else to
        return remote(fx.at[ph, mx], fx.at[ph, slot], fx_send.at[ph, to], fx_recv.at[ph, slot],
                      place(to * nzc + mzc, lat))

    def fold_copy2(ph, j, mine):
        to = (mz + j) % nz
        slot = mz if mine else to
        return remote(fsel.at[ph, to], fz.at[ph, slot], fz_send.at[ph, to], fz_recv.at[ph, slot],
                      place(mx * nzc + to * CORES + mc, lat))

    def fold_copy3(ph):
        return remote(fout.at[ph, 1], fin.at[ph], fc_send.at[ph], fc_recv.at[ph],
                      place(mx * nzc + mz * CORES + 1 - mc, lat))

    def needed(x, m, z):
        start = L * (x * nzc + m)
        least = seam_ref[0:1, 0:1] - L * (mx * nzc + z * CORES) - (CORES * L + 2)
        last = nlon * L - 1
        return (((start - least) & last) < CORES * L + 6) | (((least - start) & last) < L)

    def fold_first(ph, rows):
        fx[ph, mx] = rows[R : R + 3].astype(BF16)

        @pl.loop(1, nx)
        def _(j):
            fold_copy(ph, j, True).start()

    def fold_second(ph):
        @pl.loop(1, nx)
        def _(j):
            fold_copy(ph, j, False).wait()

        @pl.loop(0, nz)
        def _(z):
            picked = jnp.zeros((3, C, L), F32)
            for x in range(nx):
                use = jnp.where(needed(x, mzc, z), 1.0, 0.0)
                picked = jnp.where(jnp.broadcast_to(use, (C, L))[None] > 0.5, fx[ph, x].astype(F32), picked)
            fsel[ph, z] = picked.astype(BF16)

        fz[ph, mz] = fsel[ph, mz]

        @pl.loop(1, nz)
        def _(j):
            fold_copy2(ph, j, True).start()

    def fold_third(ph):
        @pl.loop(1, nz)
        def _(j):
            fold_copy2(ph, j, False).wait()

        held = jnp.concatenate([fz[ph, z].reshape(3 * C, L) for z in range(nz)], axis=1)
        for other in range(CORES):
            got = dot(held, onehot[other])
            mirrored = [got[C * (2 - k) : C * (3 - k)] for k in range(3)]
            slot = slot_of_lane % 8
            ends = mirrored[2][:, L:]
            for k in (1, 0):
                ends = jnp.where(slot == k, mirrored[k][:, L:], ends)
            for k in range(3):
                fout[ph, other, k] = mirrored[k][:, :L].astype(BF16)
            fout[ph, other, 3] = ends.astype(BF16)
        fold_copy3(ph).start()

    def fold_last(ph):
        fold_copy3(ph).wait()
        total = fout[ph, 0].astype(F32) + fin[ph].astype(F32)
        halos = [
            jnp.where(low_half, roll(total[3], -8 * k), roll(total[3], 56 - 8 * k))
            for k in range(3)
        ]
        return [total[k] for k in range(3)], halos

    loads[0].wait()
    rows_f[...] = fields_ref[...].astype(F32).reshape(C * R, L)
    for i in range(R):
        xf[3 + i] = rows_f[pl.ds(i, C, stride=R), :]
    edges[0, 0] = xf[3:6].astype(BF16)
    edges[0, 1] = xf[R : R + 3].astype(BF16)
    pack(0, lambda i: xf[3 + i], range(R))
    pl.semaphore_wait(barrier, 8 + (nlat - 1) + (ng - 1) + (nz - 1))
    sent = row_copies(0) + pack_copies(0, (0, 1, 2), 0)
    for copy in sent:
        copy.start()
    loads[3].wait()

    @pl.when(is_top)
    def _():
        fold_first(0, xf)
        rows_i = lax.broadcasted_iota(jnp.int32, (nz * L, L), 0)
        block = jnp.full((nz * L, L), -(2**20), jnp.int32)
        for z in range(nz):
            for x in range(nx):
                here = jnp.where(needed(x, z * CORES + mc, mz), 1, 0)
                here = (jnp.broadcast_to(here, (nz * L, L)) > 0) & (rows_i // L == z)
                block = jnp.where(here, L * (x * nzc + z * CORES + mc), block)
        held_col = block + rows_i % L
        col = lax.broadcasted_iota(jnp.int32, (1, L), 1)
        ahead = jnp.where(col < 64, L + col % 8, col % 8 - 8)
        for other in range(CORES):
            core = mc + other * (1 - 2 * mc)
            origin = seam_ref[0:1, 0:1] - L * (mx * nzc + mz * CORES + core)
            for half, offset in enumerate((col, ahead)):
                wanted = (origin - offset) & (nlon * L - 1)
                onehot[other, :, L * half : L * (half + 1)] = jnp.where(held_col == wanted, 1.0, 0.0).astype(BF16)

    for load in loads[1:3] + loads[4:]:
        load.wait()

    def eye(n):
        return jnp.where(
            lax.broadcasted_iota(jnp.int32, (n, n), 0) == lax.broadcasted_iota(jnp.int32, (n, n), 1), 1.0, 0.0
        ).astype(BF16)

    pmat[...] = jnp.zeros_like(pmat)
    for a in range(7):
        pmat[8 * a : 8 * a + 7] = depth_ref[a].astype(F32)
    for n, ref in enumerate((gain_ref, bias_ref, scale_ref)):
        pmat[56 + n : 57 + n] = ref[...].astype(F32)
    par = nt_dot(eye(C), pmat[...].astype(BF16))
    for a in range(7):
        for q in range(7):
            wts[a * 7 + q] = jnp.broadcast_to(par[:, 8 * a + q : 8 * a + q + 1], (C, L))
    for n in range(3):
        parb[n] = jnp.broadcast_to(par[:, 56 + n : 57 + n], (C, WIDE))
    first_row = lax.broadcasted_iota(jnp.int32, (16, HID), 0) == 0
    upb = upb_ref[...].astype(F32)
    upb = jnp.concatenate([upb[0:1], upb[1:2]], axis=1)
    bias_row = jnp.where(first_row, jnp.broadcast_to(upb, (16, HID)), 0.0)
    with_bias = jnp.concatenate([upt_ref[...], bias_row.astype(BF16)], axis=0)
    upx[...] = nt_dot(eye(HID), with_bias).astype(BF16)
    downt[...] = nt_dot(eye(HID), down_ref[...]).astype(BF16)
    acc_s[...] = jnp.zeros_like(acc_s)
    acc_down[...] = jnp.zeros_like(acc_down)
    acc_up[...] = jnp.zeros_like(acc_up)
    rows_f[...] = cot_ref[...].astype(F32).reshape(C * R, L)
    for i in range(R):
        gmask[i] = rows_f[pl.ds(i, C, stride=R), :] * mask_ref[i : i + 1, :].astype(F32)

    @pl.when(is_top)
    def _():
        fold_second(0)

    for copy in sent:
        copy.wait()
    unpack(0, xf)

    @pl.when(is_bottom)
    def _():
        for u in range(3):
            xf[u] = jnp.zeros((C, L), F32)
            hal[u] = jnp.zeros((C, L), F32)

    def conv_rows(first, count):
        ext_rows = pl.ds(first, count + 6)

        @pl.loop(0, C // 8)
        def _(s):
            cs = part_of(s)
            lanes = lax.broadcasted_iota(jnp.int32, (count + 6, 8, L), 2)
            total = jnp.zeros((count, 8, L), F32)
            for q in range(7):
                ext = shifted(q, xf[ext_rows, cs, :], hal[ext_rows, cs, :], lanes)
                shifts[q, ext_rows, cs, :] = ext
                for a in range(7):
                    total = total + wts[a * 7 + q, cs, :][None] * ext[a : a + count]
            conv[pl.ds(first, count), cs, :] = total

    conv_rows(0, R - BLOCK)

    @pl.when(is_top)
    def _():
        fold_third(0)

    top_flag = (lat + 1) // nlat

    def flat(x):
        return jnp.concatenate([x[i] for i in range(BLOCK)], axis=1)

    @pl.loop(0, R // BLOCK)
    def _(step):
        first = BLOCK * (((3 - 2 * top_flag) * step) % (R // BLOCK))

        @pl.when(step == 3 * top_flag)
        def _():
            @pl.when(is_top)
            def _():
                mains, halos = fold_last(0)
                for k in range(3):
                    xf[R + 3 + k] = mains[k]
                    hal[R + 3 + k] = halos[k]

            conv_rows(R - BLOCK, BLOCK)

        rows = pl.ds(first, BLOCK)
        gain, bias, scale = parb[0], parb[1], parb[2]
        x = flat(conv[rows])
        mean = jnp.mean(x, axis=0, keepdims=True)
        x = x - mean
        rstd = lax.rsqrt(jnp.mean(x * x, axis=0, keepdims=True) + 1e-06)
        xhat = x * rstd
        normed = (xhat * gain + bias).astype(BF16)
        normed_one = jnp.concatenate([normed, jnp.ones((16, WIDE), BF16)], axis=0)
        pre = dot(upx[...], normed_one)
        phi, density = phi_and_density(pre)
        hidden = (pre * phi).astype(BF16)
        slope = phi + pre * density * PDF
        branch = dot(down_ref[...], hidden)
        mask = mask_ref[rows, :].astype(F32)
        mask = jnp.concatenate([mask[i : i + 1] for i in range(BLOCK)], axis=1)
        out = mask * (flat(xf[pl.ds(3 + first, BLOCK)]) + scale * branch)
        g = flat(gmask[rows])
        d_branch = (g * scale).astype(BF16)
        acc_s[2] += g * branch
        acc_down[...] += nt_dot(d_branch, hidden)
        d_hidden = dot(downt[...], d_branch)
        d_pre = (d_hidden * slope).astype(BF16)
        acc_up[...] += nt_dot(normed_one, d_pre)
        d_normed = dot(upt_ref[...], d_pre)
        acc_s[0] += d_normed * xhat
        acc_s[1] += d_normed
        gd = d_normed * gain
        d_conv = rstd * (
            gd
            - jnp.mean(gd, axis=0, keepdims=True)
            - xhat * jnp.mean(gd * xhat, axis=0, keepdims=True)
        )
        d_conv = d_conv.astype(BF16).astype(F32)
        for i in range(BLOCK):
            outr[first + i] = out[:, L * i : L * (i + 1)]
            df[3 + first + i] = d_conv[:, L * i : L * (i + 1)]

        @pl.when(step == 1)
        def _():
            edges[1, 0] = df[3:6].astype(BF16)
            edges[1, 1] = df[R : R + 3].astype(BF16)
            pack(1, lambda i: df[3 + i], (0, 1, 2, 13, 14, 15))
            for copy in row_copies(1) + pack_copies(1, (0, 2), 1):
                copy.start()

    @pl.when(is_top)
    def _():
        fold_first(1, df)

    pack(2, lambda i: df[3 + i], range(R))
    for copy in pack_copies(1, (1,), 2):
        copy.start()

    up = acc_up[...]
    mlp_src[0:64] = up[:64, :L]
    mlp_src[64:128] = up[:64, L:]
    down = acc_down[...]
    mlp_src[128:192] = down[:, :L]
    mlp_src[192:256] = down[:, L:]
    mlp_sum.step1()

    @pl.loop(0, C // 8)
    def _(s):
        cs = part_of(s)
        d_conv = df[3 : R + 3, cs, :]
        lanes = lax.broadcasted_iota(jnp.int32, (8, L), 1)
        got = jnp.zeros((8, L), F32)
        for q in range(7):
            ext = shifts[q, :, cs, :]
            for a in range(7):
                tap = jnp.sum(d_conv * ext[a : a + R], axis=0)
                got = jnp.where(lanes == a * 8 + q, jnp.sum(tap, axis=1, keepdims=True), got)
        for n in range(3):
            got = jnp.where(lanes == 56 + n, jnp.sum(acc_s[n, cs, :], axis=1, keepdims=True), got)
        rows_f[cs, :] = got

    rows_f[C : 2 * C] = jnp.zeros((C, L), F32)
    taps = jnp.transpose(rows_f[0:L, :])[:C]
    up_b = up[C : C + 1]
    row_of = lax.broadcasted_iota(jnp.int32, (C, L), 0)
    for k in range(4):
        piece = jnp.broadcast_to(up_b[:, L * (k // 2) : L * (k // 2) + L], (C, L))
        taps = jnp.where(row_of == 59 + k, roll(piece, 64 * (k % 2)), taps)
    rest_src[...] = jnp.where(low_half[:32], taps[:32], roll(taps[32:], 64))
    rest_sum.step1()

    @pl.when(is_top)
    def _():
        fold_second(1)

    mlp_sum.step2()

    for copy in row_copies(1) + pack_copies(1, (0, 2), 1) + pack_copies(1, (1,), 2):
        copy.wait()
    unpack(1, df)

    def clear(u):
        df[u] = jnp.zeros((C, L), F32)
        hal[u] = jnp.zeros((C, L), F32)

    @pl.when(is_bottom)
    def _():
        for u in range(3):
            clear(u)

    @pl.when(is_top)
    def _():
        for u in range(R + 3, RE):
            clear(u)

    def adjoint(first, last):
        @pl.loop(first, last)
        def _(s):
            cs = part_of(s)
            lanes = lax.broadcasted_iota(jnp.int32, (RE, 8, L), 2)
            total = gmask[:, cs, :]
            for q in range(7):
                ext = shifted(6 - q, df[:, cs, :], hal[:, cs, :], lanes)
                for a in range(7):
                    total = total + wts[a * 7 + q, cs, :][None] * ext[6 - a : 6 - a + R]
            gmask[:, cs, :] = total

    adjoint(0, C // 16)

    @pl.when(is_top)
    def _():
        fold_third(1)

    rest_sum.step2()
    mlp_sum.step3()
    adjoint(C // 16, C // 8)
    rest_sum.step3()
    mlp_sum.step4()

    @pl.when(is_top)
    def _():
        mains, halos = fold_last(1)
        for k in range(3):
            for q in range(7):
                fshift[q, k] = shifted(q, mains[k], halos[k], lane)
        for k in range(3):
            total = gmask[R - 1 - k]
            for a in range(k + 4, 7):
                for q in range(7):
                    total = total + wts[a * 7 + q] * fshift[q, a - k - 4]
            gmask[R - 1 - k] = total

    for i in range(R):
        rows_f[pl.ds(i, C, stride=R), :] = gmask[i]
    gf_ref[...] = rows_f[...].reshape(C, R, L).astype(BF16)
    rest_sum.step4()
    for i in range(R):
        rows_f[pl.ds(i, C, stride=R), :] = outr[i]
    out_ref[...] = rows_f[...].reshape(C, R, L).astype(BF16)
    mlp_sum.finish()
    for p in range(nlat):
        mlp_ref[p * mlp_sum.chunk : (p + 1) * mlp_sum.chunk] = mlpg[p]
    rest_sum.finish()
    for p in range(restg.shape[0]):
        rest_ref[p * rest_sum.chunk : (p + 1) * rest_sum.chunk] = restg[p]


def unpack_sums(out_ref, gf_ref, mlp_ref, rest_ref, o_out, o_gf, o_depth, o_gain, o_bias, o_up, o_upb, o_down, o_scale, sems):
    stores = [pltpu.make_async_copy(out_ref, o_out, sems.at[0]), pltpu.make_async_copy(gf_ref, o_gf, sems.at[1])]
    for store in stores:
        store.start()
    o_up[:, :L] = mlp_ref[0:64]
    o_up[:, L:] = mlp_ref[64:128]
    o_down[:, :L] = mlp_ref[128:192]
    o_down[:, L:] = mlp_ref[192:256]
    low = rest_ref[...]
    high = pltpu.roll(low, 64, 1)
    for a in range(7):
        part = low[8 * a : 8 * a + 7] if a < 4 else high[8 * a - 32 : 8 * a - 25]
        o_depth[a] = part[:, :C]
    o_gain[...] = high[24:25, :C]
    o_bias[...] = high[25:26, :C]
    o_scale[...] = high[26:27, :C]
    lane = lax.broadcasted_iota(jnp.int32, (1, L), 1)
    for k in range(2):
        o_upb[:, L * k : L * (k + 1)] = jnp.where(lane < 64, high[27 + 2 * k : 28 + 2 * k], low[28 + 2 * k : 29 + 2 * k])
    for store in stores:
        store.wait()


def shards(
    dims,
    fields,
    cotangent,
    ocean_mask,
    seam_partner,
    depth_weight,
    norm_gain,
    layer_norm_bias,
    up_weight,
    up_bias,
    down_weight,
    layer_scale,
):
    nlon, nlat, nx = dims
    nzc = nlon // nx
    nz = nzc // CORES
    ng = nx * CORES
    owners = min(4, nlat)
    vmem = pl.BlockSpec(memory_space=pltpu.VMEM)
    hbm = pl.BlockSpec(memory_space=pltpu.HBM)
    dma = pltpu.SemaphoreType.DMA

    def part_bufs(rows, n):
        chunk = rows // n
        return [pltpu.VMEM((count, chunk, L), F32) for count in (nlat, ng, nz, n)]

    def part_sems(n):
        return [dma((count,)) for count in (n, nlat, ng, ng, nz, nz, nlat, n)]

    cells = jax.ShapeDtypeStruct((C, R, L), BF16)
    out, grad_fields, mlp, rest = pl.pallas_call(
        functools.partial(kernel, dims),
        out_shape=(
            pltpu.VMEM((C, R, L), BF16),
            pltpu.VMEM((C, R, L), BF16),
            pltpu.VMEM((MLP_ROWS, L), F32),
            pltpu.VMEM((REST_ROWS, L), F32),
        ),
        in_specs=[hbm] * 11,
        out_specs=(vmem,) * 4,
        scratch_shapes=[
            pltpu.VMEM((C * R, L), F32),
            pltpu.VMEM((R, C, L), F32),
            pltpu.VMEM((R, C, L), F32),
            pltpu.VMEM((RE, C, L), F32),
            pltpu.VMEM((RE, C, L), F32),
            pltpu.VMEM((7, RE, C, L), F32),
            pltpu.VMEM((RE, C, L), F32),
            pltpu.VMEM((7, 3, C, L), F32),
            pltpu.VMEM((49, C, L), F32),
            pltpu.VMEM((R, C, L), F32),
            pltpu.VMEM((2, 2, 3, C, L), BF16),
            pltpu.VMEM((2, 2, 3, C, L), BF16),
            pltpu.VMEM((3, 2, C, L), BF16),
            pltpu.VMEM((2, 2, 3, C, L), BF16),
            pltpu.VMEM((2, nx, 3, C, L), BF16),
            pltpu.VMEM((2, nz, 3, C, L), BF16),
            pltpu.VMEM((2, nz, 3, C, L), BF16),
            pltpu.VMEM((2, CORES, 4, C, L), BF16),
            pltpu.VMEM((2, 4, C, L), BF16),
            pltpu.VMEM((CORES, nz * L, 2 * L), BF16),
            pltpu.VMEM((C, C), F32),
            pltpu.VMEM((HID, 80), BF16),
            pltpu.VMEM((HID, C), BF16),
            pltpu.VMEM((3, C, WIDE), F32),
            pltpu.VMEM((3, C, WIDE), F32),
            pltpu.VMEM((C, HID), F32),
            pltpu.VMEM((80, HID), F32),
            pltpu.VMEM((MLP_ROWS, L), F32),
            pltpu.VMEM((REST_ROWS, L), F32),
            *part_bufs(MLP_ROWS, nlat),
            *part_bufs(REST_ROWS, owners),
            dma((2, 8)),
            dma((2, 8)),
            dma((2, nx)),
            dma((2, nx)),
            dma((2, nz)),
            dma((2, nz)),
            dma((2,)),
            dma((2,)),
            dma((11,)),
            pltpu.VMEM((C, R, L), BF16),
            pltpu.VMEM((C, R, L), BF16),
            pltpu.VMEM((R, L), jnp.int32),
            pltpu.VMEM((nlon, L), jnp.int32),
            pltpu.VMEM((7, 7, C), BF16),
            pltpu.VMEM((1, C), BF16),
            pltpu.VMEM((1, C), BF16),
            pltpu.VMEM((1, C), BF16),
            pltpu.VMEM((C, HID), BF16),
            pltpu.VMEM((2, L), BF16),
            pltpu.VMEM((C, HID), BF16),
            *part_sems(nlat),
            *part_sems(owners),
        ],
        compiler_params=pltpu.CompilerParams(
            collective_id=0, has_side_effects=True, vmem_limit_bytes=60 * 2**20
        ),
        name="block",
    )(
        fields[0],
        cotangent[0],
        ocean_mask,
        seam_partner.reshape(nlon, L),
        jnp.transpose(depth_weight, (1, 2, 0)),
        norm_gain[None],
        layer_norm_bias[None],
        layer_scale[None],
        up_weight.T,
        up_bias.reshape(2, L),
        down_weight,
    )
    vector = jax.ShapeDtypeStruct((1, C), F32)
    wide = jax.ShapeDtypeStruct((C, HID), F32)
    out, grad_fields, depth, gain, bias, up, up_b, down, scale = pl.pallas_call(
        unpack_sums,
        out_shape=(
            cells,
            cells,
            jax.ShapeDtypeStruct((7, 7, C), F32),
            vector,
            vector,
            wide,
            jax.ShapeDtypeStruct((1, HID), F32),
            wide,
            vector,
        ),
        in_specs=[vmem] * 4,
        out_specs=(hbm,) * 2 + (vmem,) * 7,
        name="unpack_sums",
        scratch_shapes=[dma((2,))],
    )(*(pltpu.with_memory_space_constraint(x, pltpu.VMEM) for x in (out, grad_fields, mlp, rest)))
    return (
        out[None],
        grad_fields[None],
        jnp.transpose(depth, (2, 0, 1)),
        gain[0],
        bias[0],
        up.T,
        up_b[0],
        down,
        scale[0],
    )


def solution(mesh):
    nlon, nlat = mesh.shape["lon"], mesh.shape["lat"]
    dims = (nlon, nlat, 4 if nlon % 16 == 0 else 2)
    cells = P(None, None, "lat", "lon")
    return jax.shard_map(
        functools.partial(shards, dims),
        mesh=mesh,
        in_specs=(cells, cells, P("lat", "lon")) + (P(),) * 8,
        out_specs=(cells, cells) + (P(),) * 7,
        check_vma=False,
    )
```

```python
import functools
import math

import jax
import jax.numpy as jnp
from jax import lax
from jax.experimental import pallas as pl
from jax.experimental.pallas import tpu as pltpu
from jax.sharding import PartitionSpec as P

F32 = jnp.float32
BF16 = jnp.bfloat16
MESH = pl.DeviceIdType.MESH
C = 64
R = 16
L = 128
HID = 256
RE = R + 6
BLOCK = 4
WIDE = BLOCK * L
MLP_ROWS = 256
REST_ROWS = 32
CORES = 2

ERF_P = 0.3275911 / math.sqrt(2.0)
ERF_C = (
    0.5 * 0.254829592,
    0.5 * -0.284496736,
    0.5 * 1.421413741,
    0.5 * -1.453152027,
    0.5 * 1.061405429,
)
PDF = 1.0 / math.sqrt(2.0 * math.pi)


def phi_and_density(v):
    d = 1.0 + ERF_P * jnp.abs(v)
    t = pl.reciprocal(d, approx=True)
    t = t * (2.0 - d * t)
    e = jnp.exp(-0.5 * (v * v))
    poly = ERF_C[4]
    for coef in ERF_C[3::-1]:
        poly = poly * t + coef
    tail = poly * t * e
    return jnp.where(v >= 0.0, 1.0 - tail, tail), e


def nt_dot(a, b):
    return lax.dot_general(a, b, (((1,), (1,)), ((), ())), preferred_element_type=F32)


def dot(a, b):
    return jnp.dot(a, b, preferred_element_type=F32)


def roll(x, amount):
    amount %= L
    return pltpu.roll(x, amount, x.ndim - 1) if amount else x


class PartSum:
    def __init__(self, at, src, bufs, sems, owners):
        self.at, self.src, self.owners = at, src, owners
        self.b1, self.b2, self.b3, self.out = bufs
        self.sems = sems
        self.chunk = self.b1.shape[1]

    def piece(self, p):
        return self.src.at[pl.ds(pl.multiple_of(p * self.chunk, 8), self.chunk)]

    def others(self, count, body):
        @pl.loop(0, count)
        def _(p):
            @pl.when(p != self.at.lat)
            def _():
                body(p)

    def owner(self, body):
        if self.owners == self.at.nlat:
            body()
        else:
            pl.when(self.at.lat < self.owners)(body)

    def first(self, to, slot):
        return remote(self.piece(to), self.b1.at[slot], self.sems[0].at[to], self.sems[1].at[slot],
                      self.at.place(self.at.lon, to))

    def second(self, j, mine):
        at = self.at
        to = (at.mg + j) % at.ng
        slot = at.mg if mine else to
        return remote(self.b2.at[at.mg], self.b2.at[slot], self.sems[2].at[to], self.sems[3].at[slot],
                      at.place(at.lon_of_group(to), at.lat))

    def third(self, j, mine):
        at = self.at
        to = (at.mz + j) % at.nz
        slot = at.mz if mine else to
        return remote(self.b3.at[at.mz], self.b3.at[slot], self.sems[4].at[to], self.sems[5].at[slot],
                      at.place(at.mx * at.nzc + to * CORES + at.mc, at.lat))

    def last(self, to, slot):
        return remote(self.out.at[self.at.lat % self.owners], self.out.at[slot], self.sems[6].at[to],
                      self.sems[7].at[slot], self.at.place(self.at.lon, to))

    def step1(self):
        self.others(self.owners, lambda p: self.first(p, self.at.lat).start())

    def step2(self):
        at = self.at

        def go():
            self.others(at.nlat, lambda p: self.first(0, p).wait_recv())
            self.b1[at.lat] = self.src[pl.ds(pl.multiple_of(at.lat * self.chunk, 8), self.chunk)]
            self.b2[at.mg] = jnp.sum(self.b1[...], axis=0)

            @pl.loop(1, at.ng)
            def _(j):
                self.second(j, True).start()

        self.owner(go)

    def step3(self):
        at = self.at

        def go():
            @pl.loop(1, at.ng)
            def _(j):
                self.second(j, False).wait()

            self.b3[at.mz] = jnp.sum(self.b2[...], axis=0)

            @pl.loop(1, at.nz)
            def _(j):
                self.third(j, True).start()

        self.owner(go)

    def step4(self):
        at = self.at

        def go():
            @pl.loop(1, at.nz)
            def _(j):
                self.third(j, False).wait()

            self.out[at.lat] = jnp.sum(self.b3[...], axis=0)
            self.others(at.nlat, lambda p: self.last(p, at.lat).start())

        self.owner(go)

    def finish(self):
        at = self.at
        self.others(self.owners, lambda p: self.last(p, p).wait_recv())
        self.owner(lambda: self.others(at.nlat, lambda p: self.last(p, at.lat).wait_send()))
        self.others(self.owners, lambda p: self.first(p, at.lat).wait_send())


def remote(src, dst, send, recv, where):
    return pltpu.make_async_remote_copy(
        src_ref=src, dst_ref=dst, send_sem=send, recv_sem=recv,
        device_id=where, device_id_type=MESH,
    )


class Place:
    def __init__(self, dims):
        nlon, nlat, nx = dims
        self.nlon, self.nlat, self.nx = dims
        self.nzc = nlon // nx
        self.nz = self.nzc // CORES
        self.ng = nx * CORES
        self.lon = lax.axis_index("lon")
        self.lat = lax.axis_index("lat")
        self.mx, self.mzc = self.lon // self.nzc, self.lon % self.nzc
        self.mz, self.mc = self.mzc // CORES, self.mzc % CORES
        self.mg = self.mx * CORES + self.mc

    def place(self, a, b):
        return {"lon": a, "lat": b}

    def lon_of_group(self, g):
        return (g // CORES) * self.nzc + self.mz * CORES + g % CORES


def kernel(
    dims,
    fields_hbm,
    cot_hbm,
    mask_hbm,
    seam_hbm,
    depth_hbm,
    gain_hbm,
    bias_hbm,
    scale_hbm,
    upt_hbm,
    upb_hbm,
    down_hbm,
    out_ref,
    gf_ref,
    mlp_ref,
    rest_ref,
    rows_f,
    gmask,
    outr,
    xf,
    df,
    shifts,
    hal,
    fshift,
    wts,
    conv,
    edges,
    edgesr,
    pks,
    pkr,
    fx,
    fsel,
    fz,
    fout,
    fin,
    onehot,
    pmat,
    upx,
    downt,
    parb,
    acc_s,
    acc_down,
    acc_up,
    mlp_src,
    rest_src,
    mlp1,
    mlp2,
    mlp3,
    mlpg,
    rest1,
    rest2,
    rest3,
    restg,
    halo_send,
    halo_recv,
    fx_send,
    fx_recv,
    fz_send,
    fz_recv,
    fc_send,
    fc_recv,
    in_sems,
    fields_ref,
    cot_ref,
    mask_ref,
    seam_ref,
    depth_ref,
    gain_ref,
    bias_ref,
    scale_ref,
    upt_ref,
    upb_ref,
    down_ref,
    *part_sems,
):
    at = Place(dims)
    nlon, nlat, nx, nzc, ng = at.nlon, at.nlat, at.nx, at.nzc, at.ng
    lon, lat, mx, mzc, mg = at.lon, at.lat, at.mx, at.mzc, at.mg
    nz, mz, mc = at.nz, at.mz, at.mc
    place = at.place
    left, right = (lon + nlon - 1) % nlon, (lon + 1) % nlon
    down_lat, up_lat = (lat + nlat - 1) % nlat, (lat + 1) % nlat
    lats = (down_lat, lat, up_lat)
    is_top = lat == nlat - 1
    is_bottom = lat == 0
    mlp_sum = PartSum(at, mlp_src, (mlp1, mlp2, mlp3, mlpg), part_sems[:8], nlat)
    rest_sum = PartSum(at, rest_src, (rest1, rest2, rest3, restg), part_sems[8:], restg.shape[0])

    barrier = pltpu.get_barrier_semaphore()

    def hail(a, b):
        pl.semaphore_signal(barrier, inc=1, device_id=place(a, b), device_id_type=MESH)

    for b in lats:
        hail(left, b)
        hail(right, b)
    hail(lon, down_lat)
    hail(lon, up_lat)

    @pl.loop(1, nlat)
    def _(j):
        hail(lon, (lat + j) % nlat)

    @pl.loop(1, ng)
    def _(j):
        hail(at.lon_of_group((mg + j) % ng), lat)

    @pl.loop(1, nz)
    def _(j):
        hail(mx * nzc + (mz + j) % nz * CORES + mc, lat)

    loads = [
        pltpu.make_async_copy(src, dst, in_sems.at[n])
        for n, (src, dst) in enumerate(
            (
                (fields_hbm, fields_ref),
                (cot_hbm, cot_ref),
                (mask_hbm, mask_ref),
                (seam_hbm, seam_ref),
                (depth_hbm, depth_ref),
                (gain_hbm, gain_ref),
                (bias_hbm, bias_ref),
                (scale_hbm, scale_ref),
                (upt_hbm, upt_ref),
                (upb_hbm, upb_ref),
                (down_hbm, down_ref),
            )
        )
    ]
    for load in loads:
        load.start()

    lane = lax.broadcasted_iota(jnp.int32, (C, L), 1)
    slot_of_lane = lane // 8
    low_half = lane < 64

    def row_copies(ph):
        return [
            remote(edges.at[ph, 0], edgesr.at[ph, 1],
                   halo_send.at[ph, 0], halo_recv.at[ph, 0], place(lon, down_lat)),
            remote(edges.at[ph, 1], edgesr.at[ph, 0],
                   halo_send.at[ph, 1], halo_recv.at[ph, 1], place(lon, up_lat)),
        ]

    def pack_copies(ph, kinds, src):
        return [
            remote(pks.at[src, side], pkr.at[ph, side, k],
                   halo_send.at[ph, 2 + 3 * side + k], halo_recv.at[ph, 2 + 3 * side + k], place(to, lats[k]))
            for side, to in ((0, left), (1, right))
            for k in kinds
        ]

    def pack(src, row, which):
        low = jnp.zeros((C, L), F32)
        high = jnp.zeros((C, L), F32)
        for i in which:
            here = slot_of_lane == i
            low = jnp.where(here, roll(row(i), 8 * i), low)
            high = jnp.where(here, roll(row(i), 8 * i + 8), high)
        pks[src, 0] = low.astype(BF16)
        pks[src, 1] = high.astype(BF16)

    def unpack(ph, k, ext_rows):
        from_right = pkr[ph, 0, k].astype(F32)
        from_left = pkr[ph, 1, k].astype(F32)
        for u in ext_rows:
            i = (u - 3) % R
            hal[u] = jnp.where(low_half, roll(from_right, -8 * i), roll(from_left, 120 - 8 * i))

    def unpack_beside(ph):
        unpack(ph, 1, range(3, R + 3))

    def unpack_rows(ph, rows):
        unpack(ph, 2, range(0, 3))
        unpack(ph, 0, range(R + 3, RE))
        rows[0:3] = edgesr[ph, 0].astype(F32)
        rows[R + 3 : RE] = edgesr[ph, 1].astype(F32)

    def shifted(q, main, halo, lanes):
        if q == 3:
            return main
        edge = lanes >= 125 + q if q < 3 else lanes < q - 3
        return roll(jnp.where(edge, halo, main), 3 - q)

    def part_of(s):
        return pl.ds(pl.multiple_of(s * 8, 8), 8)

    def fold_copy(ph, j, mine):
        to = (mx + j) % nx
        slot = mx if mine else to
        return remote(fx.at[ph, mx], fx.at[ph, slot], fx_send.at[ph, to], fx_recv.at[ph, slot],
                      place(to * nzc + mzc, lat))

    def fold_copy2(ph, j, mine):
        to = (mz + j) % nz
        slot = mz if mine else to
        return remote(fsel.at[ph, to], fz.at[ph, slot], fz_send.at[ph, to], fz_recv.at[ph, slot],
                      place(mx * nzc + to * CORES + mc, lat))

    def fold_copy3(ph):
        return remote(fout.at[ph, 1], fin.at[ph], fc_send.at[ph], fc_recv.at[ph],
                      place(mx * nzc + mz * CORES + 1 - mc, lat))

    def needed(x, m, z):
        start = L * (x * nzc + m)
        least = seam_ref[0:1, 0:1] - L * (mx * nzc + z * CORES) - (CORES * L + 2)
        last = nlon * L - 1
        return (((start - least) & last) < CORES * L + 6) | (((least - start) & last) < L)

    def fold_first(ph, rows):
        fx[ph, mx] = rows[R : R + 3].astype(BF16)

        @pl.loop(1, nx)
        def _(j):
            fold_copy(ph, j, True).start()

    def fold_second(ph):
        @pl.loop(1, nx)
        def _(j):
            fold_copy(ph, j, False).wait()

        @pl.loop(0, nz)
        def _(z):
            picked = jnp.zeros((3, C, L), F32)
            for x in range(nx):
                use = jnp.where(needed(x, mzc, z), 1.0, 0.0)
                picked = jnp.where(jnp.broadcast_to(use, (C, L))[None] > 0.5, fx[ph, x].astype(F32), picked)
            fsel[ph, z] = picked.astype(BF16)

        fz[ph, mz] = fsel[ph, mz]

        @pl.loop(1, nz)
        def _(j):
            fold_copy2(ph, j, True).start()

    def fold_third(ph):
        @pl.loop(1, nz)
        def _(j):
            fold_copy2(ph, j, False).wait()

        held = jnp.concatenate([fz[ph, z].reshape(3 * C, L) for z in range(nz)], axis=1)
        for other in range(CORES):
            got = dot(held, onehot[other])
            mirrored = [got[C * (2 - k) : C * (3 - k)] for k in range(3)]
            slot = slot_of_lane % 8
            ends = mirrored[2][:, L:]
            for k in (1, 0):
                ends = jnp.where(slot == k, mirrored[k][:, L:], ends)
            for k in range(3):
                fout[ph, other, k] = mirrored[k][:, :L].astype(BF16)
            fout[ph, other, 3] = ends.astype(BF16)
        fold_copy3(ph).start()

    def fold_last(ph):
        fold_copy3(ph).wait()
        total = fout[ph, 0].astype(F32) + fin[ph].astype(F32)
        halos = [
            jnp.where(low_half, roll(total[3], -8 * k), roll(total[3], 56 - 8 * k))
            for k in range(3)
        ]
        return [total[k] for k in range(3)], halos

    loads[0].wait()
    rows_f[...] = fields_ref[...].astype(F32).reshape(C * R, L)
    for i in range(R):
        xf[3 + i] = rows_f[pl.ds(i, C, stride=R), :]
    edges[0, 0] = xf[3:6].astype(BF16)
    edges[0, 1] = xf[R : R + 3].astype(BF16)
    pack(0, lambda i: xf[3 + i], range(R))
    pl.semaphore_wait(barrier, 8 + (nlat - 1) + (ng - 1) + (nz - 1))
    beside = pack_copies(0, (1,), 0)
    sent = row_copies(0) + pack_copies(0, (0, 2), 0)
    for copy in beside + sent:
        copy.start()
    loads[3].wait()

    @pl.when(is_top)
    def _():
        fold_first(0, xf)
        rows_i = lax.broadcasted_iota(jnp.int32, (nz * L, L), 0)
        block = jnp.full((nz * L, L), -(2**20), jnp.int32)
        for z in range(nz):
            for x in range(nx):
                here = jnp.where(needed(x, z * CORES + mc, mz), 1, 0)
                here = (jnp.broadcast_to(here, (nz * L, L)) > 0) & (rows_i // L == z)
                block = jnp.where(here, L * (x * nzc + z * CORES + mc), block)
        held_col = block + rows_i % L
        col = lax.broadcasted_iota(jnp.int32, (1, L), 1)
        ahead = jnp.where(col < 64, L + col % 8, col % 8 - 8)
        for other in range(CORES):
            core = mc + other * (1 - 2 * mc)
            origin = seam_ref[0:1, 0:1] - L * (mx * nzc + mz * CORES + core)
            for half, offset in enumerate((col, ahead)):
                wanted = (origin - offset) & (nlon * L - 1)
                onehot[other, :, L * half : L * (half + 1)] = jnp.where(held_col == wanted, 1.0, 0.0).astype(BF16)

    for load in loads[1:3] + loads[4:]:
        load.wait()

    def eye(n):
        return jnp.where(
            lax.broadcasted_iota(jnp.int32, (n, n), 0) == lax.broadcasted_iota(jnp.int32, (n, n), 1), 1.0, 0.0
        ).astype(BF16)

    pmat[...] = jnp.zeros_like(pmat)
    for a in range(7):
        pmat[8 * a : 8 * a + 7] = depth_ref[a].astype(F32)
    for n, ref in enumerate((gain_ref, bias_ref, scale_ref)):
        pmat[56 + n : 57 + n] = ref[...].astype(F32)
    par = nt_dot(eye(C), pmat[...].astype(BF16))
    for a in range(7):
        for q in range(7):
            wts[a * 7 + q] = jnp.broadcast_to(par[:, 8 * a + q : 8 * a + q + 1], (C, L))
    for n in range(3):
        parb[n] = jnp.broadcast_to(par[:, 56 + n : 57 + n], (C, WIDE))
    first_row = lax.broadcasted_iota(jnp.int32, (16, HID), 0) == 0
    upb = upb_ref[...].astype(F32)
    upb = jnp.concatenate([upb[0:1], upb[1:2]], axis=1)
    bias_row = jnp.where(first_row, jnp.broadcast_to(upb, (16, HID)), 0.0)
    with_bias = jnp.concatenate([upt_ref[...], bias_row.astype(BF16)], axis=0)
    upx[...] = nt_dot(eye(HID), with_bias).astype(BF16)
    downt[...] = nt_dot(eye(HID), down_ref[...]).astype(BF16)
    acc_s[...] = jnp.zeros_like(acc_s)
    acc_down[...] = jnp.zeros_like(acc_down)
    acc_up[...] = jnp.zeros_like(acc_up)
    rows_f[...] = cot_ref[...].astype(F32).reshape(C * R, L)
    for i in range(R):
        gmask[i] = rows_f[pl.ds(i, C, stride=R), :] * mask_ref[i : i + 1, :].astype(F32)

    def conv_rows(first, count):
        ext_rows = pl.ds(first, count + 6)

        @pl.loop(0, C // 8)
        def _(s):
            cs = part_of(s)
            lanes = lax.broadcasted_iota(jnp.int32, (count + 6, 8, L), 2)
            total = jnp.zeros((count, 8, L), F32)
            for q in range(7):
                ext = shifted(q, xf[ext_rows, cs, :], hal[ext_rows, cs, :], lanes)
                shifts[q, ext_rows, cs, :] = ext
                for a in range(7):
                    total = total + wts[a * 7 + q, cs, :][None] * ext[a : a + count]
            conv[pl.ds(first, count), cs, :] = total

    for copy in beside:
        copy.wait()
    unpack_beside(0)
    conv_rows(3, R - 6)

    @pl.when(is_top)
    def _():
        fold_second(0)

    for copy in sent:
        copy.wait()
    unpack_rows(0, xf)

    @pl.when(is_bottom)
    def _():
        for u in range(3):
            xf[u] = jnp.zeros((C, L), F32)
            hal[u] = jnp.zeros((C, L), F32)

    conv_rows(0, 3)

    top_flag = (lat + 1) // nlat

    def flat(x):
        return jnp.concatenate([x[i] for i in range(BLOCK)], axis=1)

    @pl.loop(0, R // BLOCK)
    def _(step):
        first = BLOCK * (((3 - 2 * top_flag) * step) % (R // BLOCK))

        @pl.when(step == 3 * top_flag)
        def _():
            @pl.when(is_top)
            def _():
                mains, halos = fold_last(0)
                for k in range(3):
                    xf[R + 3 + k] = mains[k]
                    hal[R + 3 + k] = halos[k]

            conv_rows(R - 3, 3)

        rows = pl.ds(first, BLOCK)
        gain, bias, scale = parb[0], parb[1], parb[2]
        x = flat(conv[rows])
        mean = jnp.mean(x, axis=0, keepdims=True)
        x = x - mean
        rstd = lax.rsqrt(jnp.mean(x * x, axis=0, keepdims=True) + 1e-06)
        xhat = x * rstd
        normed = (xhat * gain + bias).astype(BF16)
        normed_one = jnp.concatenate([normed, jnp.ones((16, WIDE), BF16)], axis=0)
        pre = dot(upx[...], normed_one)
        phi, density = phi_and_density(pre)
        hidden = (pre * phi).astype(BF16)
        slope = phi + pre * density * PDF
        branch = dot(down_ref[...], hidden)
        mask = mask_ref[rows, :].astype(F32)
        mask = jnp.concatenate([mask[i : i + 1] for i in range(BLOCK)], axis=1)
        out = mask * (flat(xf[pl.ds(3 + first, BLOCK)]) + scale * branch)
        g = flat(gmask[rows])
        d_branch = (g * scale).astype(BF16)
        acc_s[2] += g * branch
        acc_down[...] += nt_dot(d_branch, hidden)
        d_hidden = dot(downt[...], d_branch)
        d_pre = (d_hidden * slope).astype(BF16)
        acc_up[...] += nt_dot(normed_one, d_pre)
        d_normed = dot(upt_ref[...], d_pre)
        acc_s[0] += d_normed * xhat
        acc_s[1] += d_normed
        gd = d_normed * gain
        d_conv = rstd * (
            gd
            - jnp.mean(gd, axis=0, keepdims=True)
            - xhat * jnp.mean(gd * xhat, axis=0, keepdims=True)
        )
        d_conv = d_conv.astype(BF16).astype(F32)
        for i in range(BLOCK):
            outr[first + i] = out[:, L * i : L * (i + 1)]
            df[3 + first + i] = d_conv[:, L * i : L * (i + 1)]

        @pl.when(step == 1)
        def _():
            edges[1, 0] = df[3:6].astype(BF16)
            edges[1, 1] = df[R : R + 3].astype(BF16)
            pack(1, lambda i: df[3 + i], (0, 1, 2, 13, 14, 15))
            for copy in row_copies(1) + pack_copies(1, (0, 2), 1):
                copy.start()

            @pl.when(is_top)
            def _():
                fold_third(0)

    @pl.when(is_top)
    def _():
        fold_first(1, df)

    pack(2, lambda i: df[3 + i], range(R))
    for copy in pack_copies(1, (1,), 2):
        copy.start()

    up = acc_up[...]
    mlp_src[0:64] = up[:64, :L]
    mlp_src[64:128] = up[:64, L:]
    down = acc_down[...]
    mlp_src[128:192] = down[:, :L]
    mlp_src[192:256] = down[:, L:]
    mlp_sum.step1()

    @pl.loop(0, C // 8)
    def _(s):
        cs = part_of(s)
        d_conv = df[3 : R + 3, cs, :]
        lanes = lax.broadcasted_iota(jnp.int32, (8, L), 1)
        got = jnp.zeros((8, L), F32)
        for q in range(7):
            ext = shifts[q, :, cs, :]
            for a in range(7):
                tap = jnp.sum(d_conv * ext[a : a + R], axis=0)
                got = jnp.where(lanes == a * 8 + q, jnp.sum(tap, axis=1, keepdims=True), got)
        for n in range(3):
            got = jnp.where(lanes == 56 + n, jnp.sum(acc_s[n, cs, :], axis=1, keepdims=True), got)
        rows_f[cs, :] = got

    rows_f[C : 2 * C] = jnp.zeros((C, L), F32)
    taps = jnp.transpose(rows_f[0:L, :])[:C]
    up_b = up[C : C + 1]
    row_of = lax.broadcasted_iota(jnp.int32, (C, L), 0)
    for k in range(4):
        piece = jnp.broadcast_to(up_b[:, L * (k // 2) : L * (k // 2) + L], (C, L))
        taps = jnp.where(row_of == 59 + k, roll(piece, 64 * (k % 2)), taps)
    rest_src[...] = jnp.where(low_half[:32], taps[:32], roll(taps[32:], 64))
    rest_sum.step1()

    @pl.when(is_top)
    def _():
        fold_second(1)

    mlp_sum.step2()

    for copy in row_copies(1) + pack_copies(1, (0, 2), 1) + pack_copies(1, (1,), 2):
        copy.wait()
    unpack_beside(1)
    unpack_rows(1, df)

    def clear(u):
        df[u] = jnp.zeros((C, L), F32)
        hal[u] = jnp.zeros((C, L), F32)

    @pl.when(is_bottom)
    def _():
        for u in range(3):
            clear(u)

    @pl.when(is_top)
    def _():
        for u in range(R + 3, RE):
            clear(u)

    def adjoint(first, last):
        @pl.loop(first, last)
        def _(s):
            cs = part_of(s)
            lanes = lax.broadcasted_iota(jnp.int32, (RE, 8, L), 2)
            total = gmask[:, cs, :]
            for q in range(7):
                ext = shifted(6 - q, df[:, cs, :], hal[:, cs, :], lanes)
                for a in range(7):
                    total = total + wts[a * 7 + q, cs, :][None] * ext[6 - a : 6 - a + R]
            gmask[:, cs, :] = total

    adjoint(0, C // 16)

    @pl.when(is_top)
    def _():
        fold_third(1)

    rest_sum.step2()
    mlp_sum.step3()
    adjoint(C // 16, C // 8)
    rest_sum.step3()
    mlp_sum.step4()

    @pl.when(is_top)
    def _():
        mains, halos = fold_last(1)
        for k in range(3):
            for q in range(7):
                fshift[q, k] = shifted(q, mains[k], halos[k], lane)
        for k in range(3):
            total = gmask[R - 1 - k]
            for a in range(k + 4, 7):
                for q in range(7):
                    total = total + wts[a * 7 + q] * fshift[q, a - k - 4]
            gmask[R - 1 - k] = total

    for i in range(R):
        rows_f[pl.ds(i, C, stride=R), :] = gmask[i]
    gf_ref[...] = rows_f[...].reshape(C, R, L).astype(BF16)
    rest_sum.step4()
    for i in range(R):
        rows_f[pl.ds(i, C, stride=R), :] = outr[i]
    out_ref[...] = rows_f[...].reshape(C, R, L).astype(BF16)
    mlp_sum.finish()
    for p in range(nlat):
        mlp_ref[p * mlp_sum.chunk : (p + 1) * mlp_sum.chunk] = mlpg[p]
    rest_sum.finish()
    for p in range(restg.shape[0]):
        rest_ref[p * rest_sum.chunk : (p + 1) * rest_sum.chunk] = restg[p]


def unpack_sums(out_ref, gf_ref, mlp_ref, rest_ref, o_out, o_gf, o_depth, o_gain, o_bias, o_up, o_upb, o_down, o_scale, sems):
    stores = [pltpu.make_async_copy(out_ref, o_out, sems.at[0]), pltpu.make_async_copy(gf_ref, o_gf, sems.at[1])]
    for store in stores:
        store.start()
    o_up[:, :L] = mlp_ref[0:64]
    o_up[:, L:] = mlp_ref[64:128]
    o_down[:, :L] = mlp_ref[128:192]
    o_down[:, L:] = mlp_ref[192:256]
    low = rest_ref[...]
    high = pltpu.roll(low, 64, 1)
    for a in range(7):
        part = low[8 * a : 8 * a + 7] if a < 4 else high[8 * a - 32 : 8 * a - 25]
        o_depth[a] = part[:, :C]
    o_gain[...] = high[24:25, :C]
    o_bias[...] = high[25:26, :C]
    o_scale[...] = high[26:27, :C]
    lane = lax.broadcasted_iota(jnp.int32, (1, L), 1)
    for k in range(2):
        o_upb[:, L * k : L * (k + 1)] = jnp.where(lane < 64, high[27 + 2 * k : 28 + 2 * k], low[28 + 2 * k : 29 + 2 * k])
    for store in stores:
        store.wait()


def shards(
    dims,
    fields,
    cotangent,
    ocean_mask,
    seam_partner,
    depth_weight,
    norm_gain,
    layer_norm_bias,
    up_weight,
    up_bias,
    down_weight,
    layer_scale,
):
    nlon, nlat, nx = dims
    nzc = nlon // nx
    nz = nzc // CORES
    ng = nx * CORES
    owners = min(4, nlat)
    vmem = pl.BlockSpec(memory_space=pltpu.VMEM)
    hbm = pl.BlockSpec(memory_space=pltpu.HBM)
    dma = pltpu.SemaphoreType.DMA

    def part_bufs(rows, n):
        chunk = rows // n
        return [pltpu.VMEM((count, chunk, L), F32) for count in (nlat, ng, nz, n)]

    def part_sems(n):
        return [dma((count,)) for count in (n, nlat, ng, ng, nz, nz, nlat, n)]

    cells = jax.ShapeDtypeStruct((C, R, L), BF16)
    out, grad_fields, mlp, rest = pl.pallas_call(
        functools.partial(kernel, dims),
        out_shape=(
            pltpu.VMEM((C, R, L), BF16),
            pltpu.VMEM((C, R, L), BF16),
            pltpu.VMEM((MLP_ROWS, L), F32),
            pltpu.VMEM((REST_ROWS, L), F32),
        ),
        in_specs=[hbm] * 11,
        out_specs=(vmem,) * 4,
        scratch_shapes=[
            pltpu.VMEM((C * R, L), F32),
            pltpu.VMEM((R, C, L), F32),
            pltpu.VMEM((R, C, L), F32),
            pltpu.VMEM((RE, C, L), F32),
            pltpu.VMEM((RE, C, L), F32),
            pltpu.VMEM((7, RE, C, L), F32),
            pltpu.VMEM((RE, C, L), F32),
            pltpu.VMEM((7, 3, C, L), F32),
            pltpu.VMEM((49, C, L), F32),
            pltpu.VMEM((R, C, L), F32),
            pltpu.VMEM((2, 2, 3, C, L), BF16),
            pltpu.VMEM((2, 2, 3, C, L), BF16),
            pltpu.VMEM((3, 2, C, L), BF16),
            pltpu.VMEM((2, 2, 3, C, L), BF16),
            pltpu.VMEM((2, nx, 3, C, L), BF16),
            pltpu.VMEM((2, nz, 3, C, L), BF16),
            pltpu.VMEM((2, nz, 3, C, L), BF16),
            pltpu.VMEM((2, CORES, 4, C, L), BF16),
            pltpu.VMEM((2, 4, C, L), BF16),
            pltpu.VMEM((CORES, nz * L, 2 * L), BF16),
            pltpu.VMEM((C, C), F32),
            pltpu.VMEM((HID, 80), BF16),
            pltpu.VMEM((HID, C), BF16),
            pltpu.VMEM((3, C, WIDE), F32),
            pltpu.VMEM((3, C, WIDE), F32),
            pltpu.VMEM((C, HID), F32),
            pltpu.VMEM((80, HID), F32),
            pltpu.VMEM((MLP_ROWS, L), F32),
            pltpu.VMEM((REST_ROWS, L), F32),
            *part_bufs(MLP_ROWS, nlat),
            *part_bufs(REST_ROWS, owners),
            dma((2, 8)),
            dma((2, 8)),
            dma((2, nx)),
            dma((2, nx)),
            dma((2, nz)),
            dma((2, nz)),
            dma((2,)),
            dma((2,)),
            dma((11,)),
            pltpu.VMEM((C, R, L), BF16),
            pltpu.VMEM((C, R, L), BF16),
            pltpu.VMEM((R, L), jnp.int32),
            pltpu.VMEM((nlon, L), jnp.int32),
            pltpu.VMEM((7, 7, C), BF16),
            pltpu.VMEM((1, C), BF16),
            pltpu.VMEM((1, C), BF16),
            pltpu.VMEM((1, C), BF16),
            pltpu.VMEM((C, HID), BF16),
            pltpu.VMEM((2, L), BF16),
            pltpu.VMEM((C, HID), BF16),
            *part_sems(nlat),
            *part_sems(owners),
        ],
        compiler_params=pltpu.CompilerParams(
            collective_id=0, has_side_effects=True, vmem_limit_bytes=60 * 2**20
        ),
        name="block",
    )(
        fields[0],
        cotangent[0],
        ocean_mask,
        seam_partner.reshape(nlon, L),
        jnp.transpose(depth_weight, (1, 2, 0)),
        norm_gain[None],
        layer_norm_bias[None],
        layer_scale[None],
        up_weight.T,
        up_bias.reshape(2, L),
        down_weight,
    )
    vector = jax.ShapeDtypeStruct((1, C), F32)
    wide = jax.ShapeDtypeStruct((C, HID), F32)
    out, grad_fields, depth, gain, bias, up, up_b, down, scale = pl.pallas_call(
        unpack_sums,
        out_shape=(
            cells,
            cells,
            jax.ShapeDtypeStruct((7, 7, C), F32),
            vector,
            vector,
            wide,
            jax.ShapeDtypeStruct((1, HID), F32),
            wide,
            vector,
        ),
        in_specs=[vmem] * 4,
        out_specs=(hbm,) * 2 + (vmem,) * 7,
        name="unpack_sums",
        scratch_shapes=[dma((2,))],
    )(*(pltpu.with_memory_space_constraint(x, pltpu.VMEM) for x in (out, grad_fields, mlp, rest)))
    return (
        out[None],
        grad_fields[None],
        jnp.transpose(depth, (2, 0, 1)),
        gain[0],
        bias[0],
        up.T,
        up_b[0],
        down,
        scale[0],
    )


def solution(mesh):
    nlon, nlat = mesh.shape["lon"], mesh.shape["lat"]
    dims = (nlon, nlat, 4 if nlon % 16 == 0 else 2)
    cells = P(None, None, "lat", "lon")
    return jax.shard_map(
        functools.partial(shards, dims),
        mesh=mesh,
        in_specs=(cells, cells, P("lat", "lon")) + (P(),) * 8,
        out_specs=(cells, cells) + (P(),) * 7,
        check_vma=False,
    )
```

```python
import functools
import math

import jax
import jax.numpy as jnp
from jax import lax
from jax.experimental import pallas as pl
from jax.experimental.pallas import tpu as pltpu
from jax.sharding import PartitionSpec as P

F32 = jnp.float32
BF16 = jnp.bfloat16
MESH = pl.DeviceIdType.MESH
C = 64
R = 16
L = 128
HID = 256
RE = R + 6
BLOCK = 4
WIDE = BLOCK * L
MLP_ROWS = 256
REST_ROWS = 32
CORES = 2

ERF_P = 0.3275911 / math.sqrt(2.0)
ERF_C = (
    0.5 * 0.254829592,
    0.5 * -0.284496736,
    0.5 * 1.421413741,
    0.5 * -1.453152027,
    0.5 * 1.061405429,
)
PDF = 1.0 / math.sqrt(2.0 * math.pi)


def phi_and_density(v):
    d = 1.0 + ERF_P * jnp.abs(v)
    t = pl.reciprocal(d, approx=True)
    t = t * (2.0 - d * t)
    e = jnp.exp(-0.5 * (v * v))
    poly = ERF_C[4]
    for coef in ERF_C[3::-1]:
        poly = poly * t + coef
    tail = poly * t * e
    return jnp.where(v >= 0.0, 1.0 - tail, tail), e


def nt_dot(a, b):
    return lax.dot_general(a, b, (((1,), (1,)), ((), ())), preferred_element_type=F32)


def dot(a, b):
    return jnp.dot(a, b, preferred_element_type=F32)


def roll(x, amount):
    amount %= L
    return pltpu.roll(x, amount, x.ndim - 1) if amount else x


class PartSum:
    def __init__(self, at, src, bufs, sems, owners):
        self.at, self.src, self.owners = at, src, owners
        self.b1, self.b2, self.b3, self.out = bufs
        self.sems = sems
        self.chunk = self.b1.shape[1]

    def piece(self, p):
        return self.src.at[pl.ds(pl.multiple_of(p * self.chunk, 8), self.chunk)]

    def others(self, count, body):
        @pl.loop(0, count)
        def _(p):
            @pl.when(p != self.at.lat)
            def _():
                body(p)

    def owner(self, body):
        if self.owners == self.at.nlat:
            body()
        else:
            pl.when(self.at.lat < self.owners)(body)

    def first(self, to, slot):
        return remote(self.piece(to), self.b1.at[slot], self.sems[0].at[to], self.sems[1].at[slot],
                      self.at.place(self.at.lon, to))

    def second(self, j, mine):
        at = self.at
        to = (at.mg + j) % at.ng
        slot = at.mg if mine else to
        return remote(self.b2.at[at.mg], self.b2.at[slot], self.sems[2].at[to], self.sems[3].at[slot],
                      at.place(at.lon_of_group(to), at.lat))

    def third(self, j, mine):
        at = self.at
        to = (at.mz + j) % at.nz
        slot = at.mz if mine else to
        return remote(self.b3.at[at.mz], self.b3.at[slot], self.sems[4].at[to], self.sems[5].at[slot],
                      at.place(at.mx * at.nzc + to * CORES + at.mc, at.lat))

    def last(self, to, slot):
        return remote(self.out.at[self.at.lat % self.owners], self.out.at[slot], self.sems[6].at[to],
                      self.sems[7].at[slot], self.at.place(self.at.lon, to))

    def step1(self):
        self.others(self.owners, lambda p: self.first(p, self.at.lat).start())

    def step2(self):
        at = self.at

        def go():
            self.others(at.nlat, lambda p: self.first(0, p).wait_recv())
            self.b1[at.lat] = self.src[pl.ds(pl.multiple_of(at.lat * self.chunk, 8), self.chunk)]
            self.b2[at.mg] = jnp.sum(self.b1[...], axis=0)

            @pl.loop(1, at.ng)
            def _(j):
                self.second(j, True).start()

        self.owner(go)

    def step3(self):
        at = self.at

        def go():
            @pl.loop(1, at.ng)
            def _(j):
                self.second(j, False).wait()

            self.b3[at.mz] = jnp.sum(self.b2[...], axis=0)

            @pl.loop(1, at.nz)
            def _(j):
                self.third(j, True).start()

        self.owner(go)

    def step4(self):
        at = self.at

        def go():
            @pl.loop(1, at.nz)
            def _(j):
                self.third(j, False).wait()

            self.out[at.lat] = jnp.sum(self.b3[...], axis=0)
            self.others(at.nlat, lambda p: self.last(p, at.lat).start())

        self.owner(go)

    def finish(self):
        at = self.at
        self.others(self.owners, lambda p: self.last(p, p).wait_recv())
        self.owner(lambda: self.others(at.nlat, lambda p: self.last(p, at.lat).wait_send()))
        self.others(self.owners, lambda p: self.first(p, at.lat).wait_send())


def remote(src, dst, send, recv, where):
    return pltpu.make_async_remote_copy(
        src_ref=src, dst_ref=dst, send_sem=send, recv_sem=recv,
        device_id=where, device_id_type=MESH,
    )


class Place:
    def __init__(self, dims):
        nlon, nlat, nx = dims
        self.nlon, self.nlat, self.nx = dims
        self.nzc = nlon // nx
        self.nz = self.nzc // CORES
        self.ng = nx * CORES
        self.lon = lax.axis_index("lon")
        self.lat = lax.axis_index("lat")
        self.mx, self.mzc = self.lon // self.nzc, self.lon % self.nzc
        self.mz, self.mc = self.mzc // CORES, self.mzc % CORES
        self.mg = self.mx * CORES + self.mc

    def place(self, a, b):
        return {"lon": a, "lat": b}

    def lon_of_group(self, g):
        return (g // CORES) * self.nzc + self.mz * CORES + g % CORES


def kernel(
    dims,
    fields_hbm,
    cot_hbm,
    mask_hbm,
    seam_hbm,
    depth_hbm,
    gain_hbm,
    bias_hbm,
    scale_hbm,
    upt_hbm,
    upb_hbm,
    down_hbm,
    out_ref,
    gf_ref,
    mlp_ref,
    rest_ref,
    rows_f,
    gmask,
    outr,
    xf,
    df,
    shifts,
    hal,
    fshift,
    wts,
    conv,
    edges,
    edgesr,
    pks,
    pkr,
    fx,
    fsel,
    fz,
    fout,
    fin,
    onehot,
    pmat,
    upx,
    downt,
    parb,
    acc_s,
    acc_down,
    acc_up,
    mlp_src,
    rest_src,
    mlp1,
    mlp2,
    mlp3,
    mlpg,
    rest1,
    rest2,
    rest3,
    restg,
    halo_send,
    halo_recv,
    fx_send,
    fx_recv,
    fz_send,
    fz_recv,
    fc_send,
    fc_recv,
    in_sems,
    fields_ref,
    cot_ref,
    mask_ref,
    seam_ref,
    depth_ref,
    gain_ref,
    bias_ref,
    scale_ref,
    upt_ref,
    upb_ref,
    down_ref,
    *part_sems,
):
    at = Place(dims)
    nlon, nlat, nx, nzc, ng = at.nlon, at.nlat, at.nx, at.nzc, at.ng
    lon, lat, mx, mzc, mg = at.lon, at.lat, at.mx, at.mzc, at.mg
    nz, mz, mc = at.nz, at.mz, at.mc
    place = at.place
    left, right = (lon + nlon - 1) % nlon, (lon + 1) % nlon
    down_lat, up_lat = (lat + nlat - 1) % nlat, (lat + 1) % nlat
    lats = (down_lat, lat, up_lat)
    is_top = lat == nlat - 1
    is_bottom = lat == 0
    mlp_sum = PartSum(at, mlp_src, (mlp1, mlp2, mlp3, mlpg), part_sems[:8], nlat)
    rest_sum = PartSum(at, rest_src, (rest1, rest2, rest3, restg), part_sems[8:], restg.shape[0])

    barrier = pltpu.get_barrier_semaphore()

    def hail(a, b):
        pl.semaphore_signal(barrier, inc=1, device_id=place(a, b), device_id_type=MESH)

    for b in lats:
        hail(left, b)
        hail(right, b)
    hail(lon, down_lat)
    hail(lon, up_lat)

    @pl.loop(1, nlat)
    def _(j):
        hail(lon, (lat + j) % nlat)

    @pl.loop(1, ng)
    def _(j):
        hail(at.lon_of_group((mg + j) % ng), lat)

    @pl.loop(1, nz)
    def _(j):
        hail(mx * nzc + (mz + j) % nz * CORES + mc, lat)

    loads = [
        pltpu.make_async_copy(src, dst, in_sems.at[n])
        for n, (src, dst) in enumerate(
            (
                (fields_hbm, fields_ref),
                (cot_hbm, cot_ref),
                (mask_hbm, mask_ref),
                (seam_hbm, seam_ref),
                (depth_hbm, depth_ref),
                (gain_hbm, gain_ref),
                (bias_hbm, bias_ref),
                (scale_hbm, scale_ref),
                (upt_hbm, upt_ref),
                (upb_hbm, upb_ref),
                (down_hbm, down_ref),
            )
        )
    ]
    for load in loads:
        load.start()

    lane = lax.broadcasted_iota(jnp.int32, (C, L), 1)
    slot_of_lane = lane // 8
    low_half = lane < 64

    def row_copies(ph):
        return [
            remote(edges.at[ph, 0], edgesr.at[ph, 1],
                   halo_send.at[ph, 0], halo_recv.at[ph, 0], place(lon, down_lat)),
            remote(edges.at[ph, 1], edgesr.at[ph, 0],
                   halo_send.at[ph, 1], halo_recv.at[ph, 1], place(lon, up_lat)),
        ]

    def pack_copies(ph, kinds, src):
        return [
            remote(pks.at[src, side], pkr.at[ph, side, k],
                   halo_send.at[ph, 2 + 3 * side + k], halo_recv.at[ph, 2 + 3 * side + k], place(to, lats[k]))
            for side, to in ((0, left), (1, right))
            for k in kinds
        ]

    def pack(src, row, which):
        low = jnp.zeros((C, L), F32)
        high = jnp.zeros((C, L), F32)
        for i in which:
            here = slot_of_lane == i
            low = jnp.where(here, roll(row(i), 8 * i), low)
            high = jnp.where(here, roll(row(i), 8 * i + 8), high)
        pks[src, 0] = low.astype(BF16)
        pks[src, 1] = high.astype(BF16)

    def unpack(ph, k, ext_rows):
        from_right = pkr[ph, 0, k].astype(F32)
        from_left = pkr[ph, 1, k].astype(F32)
        for u in ext_rows:
            i = (u - 3) % R
            hal[u] = jnp.where(low_half, roll(from_right, -8 * i), roll(from_left, 120 - 8 * i))

    def unpack_beside(ph):
        unpack(ph, 1, range(3, R + 3))

    def unpack_rows(ph, rows):
        unpack(ph, 2, range(0, 3))
        unpack(ph, 0, range(R + 3, RE))
        rows[0:3] = edgesr[ph, 0].astype(F32)
        rows[R + 3 : RE] = edgesr[ph, 1].astype(F32)

    def shifted(q, main, halo, lanes):
        if q == 3:
            return main
        edge = lanes >= 125 + q if q < 3 else lanes < q - 3
        return roll(jnp.where(edge, halo, main), 3 - q)

    def part_of(s):
        return pl.ds(pl.multiple_of(s * 8, 8), 8)

    def fold_copy(ph, j, mine):
        to = (mx + j) % nx
        slot = mx if mine else to
        return remote(fx.at[ph, mx], fx.at[ph, slot], fx_send.at[ph, to], fx_recv.at[ph, slot],
                      place(to * nzc + mzc, lat))

    def fold_copy2(ph, j, mine):
        to = (mz + j) % nz
        slot = mz if mine else to
        return remote(fsel.at[ph, to], fz.at[ph, slot], fz_send.at[ph, to], fz_recv.at[ph, slot],
                      place(mx * nzc + to * CORES + mc, lat))

    def fold_copy3(ph):
        return remote(fout.at[ph, 1], fin.at[ph], fc_send.at[ph], fc_recv.at[ph],
                      place(mx * nzc + mz * CORES + 1 - mc, lat))

    def needed(x, m, z):
        start = L * (x * nzc + m)
        least = seam_ref[0:1, 0:1] - L * (mx * nzc + z * CORES) - (CORES * L + 2)
        last = nlon * L - 1
        return (((start - least) & last) < CORES * L + 6) | (((least - start) & last) < L)

    def fold_first(ph, rows):
        fx[ph, mx] = rows[R : R + 3].astype(BF16)

        @pl.loop(1, nx)
        def _(j):
            fold_copy(ph, j, True).start()

    def fold_second(ph):
        @pl.loop(1, nx)
        def _(j):
            fold_copy(ph, j, False).wait()

        @pl.loop(0, nz)
        def _(z):
            picked = jnp.zeros((3, C, L), F32)
            for x in range(nx):
                use = jnp.where(needed(x, mzc, z), 1.0, 0.0)
                picked = jnp.where(jnp.broadcast_to(use, (C, L))[None] > 0.5, fx[ph, x].astype(F32), picked)
            fsel[ph, z] = picked.astype(BF16)

        fz[ph, mz] = fsel[ph, mz]

        @pl.loop(1, nz)
        def _(j):
            fold_copy2(ph, j, True).start()

    def fold_third(ph):
        @pl.loop(1, nz)
        def _(j):
            fold_copy2(ph, j, False).wait()

        held = jnp.concatenate([fz[ph, z].reshape(3 * C, L) for z in range(nz)], axis=1)
        for other in range(CORES):
            got = dot(held, onehot[other])
            mirrored = [got[C * (2 - k) : C * (3 - k)] for k in range(3)]
            slot = slot_of_lane % 8
            ends = mirrored[2][:, L:]
            for k in (1, 0):
                ends = jnp.where(slot == k, mirrored[k][:, L:], ends)
            for k in range(3):
                fout[ph, other, k] = mirrored[k][:, :L].astype(BF16)
            fout[ph, other, 3] = ends.astype(BF16)
        fold_copy3(ph).start()

    def fold_last(ph):
        fold_copy3(ph).wait()
        total = fout[ph, 0].astype(F32) + fin[ph].astype(F32)
        halos = [
            jnp.where(low_half, roll(total[3], -8 * k), roll(total[3], 56 - 8 * k))
            for k in range(3)
        ]
        return [total[k] for k in range(3)], halos

    loads[0].wait()
    rows_f[...] = fields_ref[...].astype(F32).reshape(C * R, L)
    for i in range(R):
        xf[3 + i] = rows_f[pl.ds(i, C, stride=R), :]
    edges[0, 0] = xf[3:6].astype(BF16)
    edges[0, 1] = xf[R : R + 3].astype(BF16)
    pack(0, lambda i: xf[3 + i], range(R))
    pl.semaphore_wait(barrier, 8 + (nlat - 1) + (ng - 1) + (nz - 1))
    @pl.when(is_top)
    def _():
        fold_first(0, xf)

    beside = pack_copies(0, (1,), 0)
    sent = row_copies(0) + pack_copies(0, (0, 2), 0)
    for copy in beside + sent:
        copy.start()
    loads[3].wait()

    @pl.when(is_top)
    def _():
        rows_i = lax.broadcasted_iota(jnp.int32, (nz * L, L), 0)
        block = jnp.full((nz * L, L), -(2**20), jnp.int32)
        for z in range(nz):
            for x in range(nx):
                here = jnp.where(needed(x, z * CORES + mc, mz), 1, 0)
                here = (jnp.broadcast_to(here, (nz * L, L)) > 0) & (rows_i // L == z)
                block = jnp.where(here, L * (x * nzc + z * CORES + mc), block)
        held_col = block + rows_i % L
        col = lax.broadcasted_iota(jnp.int32, (1, L), 1)
        ahead = jnp.where(col < 64, L + col % 8, col % 8 - 8)
        for other in range(CORES):
            core = mc + other * (1 - 2 * mc)
            origin = seam_ref[0:1, 0:1] - L * (mx * nzc + mz * CORES + core)
            for half, offset in enumerate((col, ahead)):
                wanted = (origin - offset) & (nlon * L - 1)
                onehot[other, :, L * half : L * (half + 1)] = jnp.where(held_col == wanted, 1.0, 0.0).astype(BF16)

    for load in loads[1:3] + loads[4:]:
        load.wait()

    def eye(n):
        return jnp.where(
            lax.broadcasted_iota(jnp.int32, (n, n), 0) == lax.broadcasted_iota(jnp.int32, (n, n), 1), 1.0, 0.0
        ).astype(BF16)

    pmat[...] = jnp.zeros_like(pmat)
    for a in range(7):
        pmat[8 * a : 8 * a + 7] = depth_ref[a].astype(F32)
    for n, ref in enumerate((gain_ref, bias_ref, scale_ref)):
        pmat[56 + n : 57 + n] = ref[...].astype(F32)
    par = nt_dot(eye(C), pmat[...].astype(BF16))
    for a in range(7):
        for q in range(7):
            wts[a * 7 + q] = jnp.broadcast_to(par[:, 8 * a + q : 8 * a + q + 1], (C, L))
    for n in range(3):
        parb[n] = jnp.broadcast_to(par[:, 56 + n : 57 + n], (C, WIDE))
    first_row = lax.broadcasted_iota(jnp.int32, (16, HID), 0) == 0
    upb = upb_ref[...].astype(F32)
    upb = jnp.concatenate([upb[0:1], upb[1:2]], axis=1)
    bias_row = jnp.where(first_row, jnp.broadcast_to(upb, (16, HID)), 0.0)
    with_bias = jnp.concatenate([upt_ref[...], bias_row.astype(BF16)], axis=0)
    upx[...] = nt_dot(eye(HID), with_bias).astype(BF16)
    downt[...] = nt_dot(eye(HID), down_ref[...]).astype(BF16)
    acc_s[...] = jnp.zeros_like(acc_s)
    acc_down[...] = jnp.zeros_like(acc_down)
    acc_up[...] = jnp.zeros_like(acc_up)
    rows_f[...] = cot_ref[...].astype(F32).reshape(C * R, L)
    for i in range(R):
        gmask[i] = rows_f[pl.ds(i, C, stride=R), :] * mask_ref[i : i + 1, :].astype(F32)

    def conv_rows(first, count):
        ext_rows = pl.ds(first, count + 6)

        @pl.loop(0, C // 8)
        def _(s):
            cs = part_of(s)
            lanes = lax.broadcasted_iota(jnp.int32, (count + 6, 8, L), 2)
            total = jnp.zeros((count, 8, L), F32)
            for q in range(7):
                ext = shifted(q, xf[ext_rows, cs, :], hal[ext_rows, cs, :], lanes)
                shifts[q, ext_rows, cs, :] = ext
                for a in range(7):
                    total = total + wts[a * 7 + q, cs, :][None] * ext[a : a + count]
            conv[pl.ds(first, count), cs, :] = total

    for copy in beside:
        copy.wait()
    unpack_beside(0)
    @pl.when(is_top)
    def _():
        fold_second(0)

    conv_rows(3, R - 6)

    for copy in sent:
        copy.wait()
    unpack_rows(0, xf)

    @pl.when(is_bottom)
    def _():
        for u in range(3):
            xf[u] = jnp.zeros((C, L), F32)
            hal[u] = jnp.zeros((C, L), F32)

    conv_rows(0, 3)

    top_flag = (lat + 1) // nlat

    def flat(x):
        return jnp.concatenate([x[i] for i in range(BLOCK)], axis=1)

    @pl.loop(0, R // BLOCK)
    def _(step):
        first = BLOCK * (((3 - 2 * top_flag) * step) % (R // BLOCK))

        @pl.when(step == 3 * top_flag)
        def _():
            @pl.when(is_top)
            def _():
                mains, halos = fold_last(0)
                for k in range(3):
                    xf[R + 3 + k] = mains[k]
                    hal[R + 3 + k] = halos[k]

            conv_rows(R - 3, 3)

        rows = pl.ds(first, BLOCK)
        gain, bias, scale = parb[0], parb[1], parb[2]
        x = flat(conv[rows])
        mean = jnp.mean(x, axis=0, keepdims=True)
        x = x - mean
        rstd = lax.rsqrt(jnp.mean(x * x, axis=0, keepdims=True) + 1e-06)
        xhat = x * rstd
        normed = (xhat * gain + bias).astype(BF16)
        normed_one = jnp.concatenate([normed, jnp.ones((16, WIDE), BF16)], axis=0)
        pre = dot(upx[...], normed_one)
        phi, density = phi_and_density(pre)
        hidden = (pre * phi).astype(BF16)
        slope = phi + pre * density * PDF
        branch = dot(down_ref[...], hidden)
        mask = mask_ref[rows, :].astype(F32)
        mask = jnp.concatenate([mask[i : i + 1] for i in range(BLOCK)], axis=1)
        out = mask * (flat(xf[pl.ds(3 + first, BLOCK)]) + scale * branch)
        g = flat(gmask[rows])
        d_branch = (g * scale).astype(BF16)
        acc_s[2] += g * branch
        acc_down[...] += nt_dot(d_branch, hidden)
        d_hidden = dot(downt[...], d_branch)
        d_pre = (d_hidden * slope).astype(BF16)
        acc_up[...] += nt_dot(normed_one, d_pre)
        d_normed = dot(upt_ref[...], d_pre)
        acc_s[0] += d_normed * xhat
        acc_s[1] += d_normed
        gd = d_normed * gain
        d_conv = rstd * (
            gd
            - jnp.mean(gd, axis=0, keepdims=True)
            - xhat * jnp.mean(gd * xhat, axis=0, keepdims=True)
        )
        d_conv = d_conv.astype(BF16).astype(F32)
        for i in range(BLOCK):
            outr[first + i] = out[:, L * i : L * (i + 1)]
            df[3 + first + i] = d_conv[:, L * i : L * (i + 1)]

        @pl.when(step == 1)
        def _():
            edges[1, 0] = df[3:6].astype(BF16)
            edges[1, 1] = df[R : R + 3].astype(BF16)
            pack(1, lambda i: df[3 + i], (0, 1, 2, 13, 14, 15))
            for copy in row_copies(1) + pack_copies(1, (0, 2), 1):
                copy.start()

            @pl.when(is_top)
            def _():
                fold_third(0)

    @pl.when(is_top)
    def _():
        fold_first(1, df)

    pack(2, lambda i: df[3 + i], range(R))
    for copy in pack_copies(1, (1,), 2):
        copy.start()

    up = acc_up[...]
    mlp_src[0:64] = up[:64, :L]
    mlp_src[64:128] = up[:64, L:]
    down = acc_down[...]
    mlp_src[128:192] = down[:, :L]
    mlp_src[192:256] = down[:, L:]
    mlp_sum.step1()

    @pl.loop(0, C // 8)
    def _(s):
        cs = part_of(s)
        d_conv = df[3 : R + 3, cs, :]
        lanes = lax.broadcasted_iota(jnp.int32, (8, L), 1)
        got = jnp.zeros((8, L), F32)
        for q in range(7):
            ext = shifts[q, :, cs, :]
            for a in range(7):
                tap = jnp.sum(d_conv * ext[a : a + R], axis=0)
                got = jnp.where(lanes == a * 8 + q, jnp.sum(tap, axis=1, keepdims=True), got)
        for n in range(3):
            got = jnp.where(lanes == 56 + n, jnp.sum(acc_s[n, cs, :], axis=1, keepdims=True), got)
        rows_f[cs, :] = got

    rows_f[C : 2 * C] = jnp.zeros((C, L), F32)
    taps = jnp.transpose(rows_f[0:L, :])[:C]
    up_b = up[C : C + 1]
    row_of = lax.broadcasted_iota(jnp.int32, (C, L), 0)
    for k in range(4):
        piece = jnp.broadcast_to(up_b[:, L * (k // 2) : L * (k // 2) + L], (C, L))
        taps = jnp.where(row_of == 59 + k, roll(piece, 64 * (k % 2)), taps)
    rest_src[...] = jnp.where(low_half[:32], taps[:32], roll(taps[32:], 64))
    rest_sum.step1()

    @pl.when(is_top)
    def _():
        fold_second(1)

    mlp_sum.step2()

    for copy in row_copies(1) + pack_copies(1, (0, 2), 1) + pack_copies(1, (1,), 2):
        copy.wait()
    unpack_beside(1)
    unpack_rows(1, df)

    def clear(u):
        df[u] = jnp.zeros((C, L), F32)
        hal[u] = jnp.zeros((C, L), F32)

    @pl.when(is_bottom)
    def _():
        for u in range(3):
            clear(u)

    @pl.when(is_top)
    def _():
        for u in range(R + 3, RE):
            clear(u)

    def adjoint(first, last):
        @pl.loop(first, last)
        def _(s):
            cs = part_of(s)
            lanes = lax.broadcasted_iota(jnp.int32, (RE, 8, L), 2)
            total = gmask[:, cs, :]
            for q in range(7):
                ext = shifted(6 - q, df[:, cs, :], hal[:, cs, :], lanes)
                for a in range(7):
                    total = total + wts[a * 7 + q, cs, :][None] * ext[6 - a : 6 - a + R]
            gmask[:, cs, :] = total

    adjoint(0, C // 16)

    @pl.when(is_top)
    def _():
        fold_third(1)

    rest_sum.step2()
    mlp_sum.step3()
    adjoint(C // 16, C // 8)
    rest_sum.step3()
    mlp_sum.step4()

    @pl.when(is_top)
    def _():
        mains, halos = fold_last(1)
        for k in range(3):
            for q in range(7):
                fshift[q, k] = shifted(q, mains[k], halos[k], lane)
        for k in range(3):
            total = gmask[R - 1 - k]
            for a in range(k + 4, 7):
                for q in range(7):
                    total = total + wts[a * 7 + q] * fshift[q, a - k - 4]
            gmask[R - 1 - k] = total

    for i in range(R):
        rows_f[pl.ds(i, C, stride=R), :] = gmask[i]
    gf_ref[...] = rows_f[...].reshape(C, R, L).astype(BF16)
    rest_sum.step4()
    for i in range(R):
        rows_f[pl.ds(i, C, stride=R), :] = outr[i]
    out_ref[...] = rows_f[...].reshape(C, R, L).astype(BF16)
    mlp_sum.finish()
    for p in range(nlat):
        mlp_ref[p * mlp_sum.chunk : (p + 1) * mlp_sum.chunk] = mlpg[p]
    rest_sum.finish()
    for p in range(restg.shape[0]):
        rest_ref[p * rest_sum.chunk : (p + 1) * rest_sum.chunk] = restg[p]


def unpack_sums(out_ref, gf_ref, mlp_ref, rest_ref, o_out, o_gf, o_depth, o_gain, o_bias, o_up, o_upb, o_down, o_scale, sems):
    stores = [pltpu.make_async_copy(out_ref, o_out, sems.at[0]), pltpu.make_async_copy(gf_ref, o_gf, sems.at[1])]
    for store in stores:
        store.start()
    o_up[:, :L] = mlp_ref[0:64]
    o_up[:, L:] = mlp_ref[64:128]
    o_down[:, :L] = mlp_ref[128:192]
    o_down[:, L:] = mlp_ref[192:256]
    low = rest_ref[...]
    high = pltpu.roll(low, 64, 1)
    for a in range(7):
        part = low[8 * a : 8 * a + 7] if a < 4 else high[8 * a - 32 : 8 * a - 25]
        o_depth[a] = part[:, :C]
    o_gain[...] = high[24:25, :C]
    o_bias[...] = high[25:26, :C]
    o_scale[...] = high[26:27, :C]
    lane = lax.broadcasted_iota(jnp.int32, (1, L), 1)
    for k in range(2):
        o_upb[:, L * k : L * (k + 1)] = jnp.where(lane < 64, high[27 + 2 * k : 28 + 2 * k], low[28 + 2 * k : 29 + 2 * k])
    for store in stores:
        store.wait()


def shards(
    dims,
    fields,
    cotangent,
    ocean_mask,
    seam_partner,
    depth_weight,
    norm_gain,
    layer_norm_bias,
    up_weight,
    up_bias,
    down_weight,
    layer_scale,
):
    nlon, nlat, nx = dims
    nzc = nlon // nx
    nz = nzc // CORES
    ng = nx * CORES
    owners = min(4, nlat)
    vmem = pl.BlockSpec(memory_space=pltpu.VMEM)
    hbm = pl.BlockSpec(memory_space=pltpu.HBM)
    dma = pltpu.SemaphoreType.DMA

    def part_bufs(rows, n):
        chunk = rows // n
        return [pltpu.VMEM((count, chunk, L), F32) for count in (nlat, ng, nz, n)]

    def part_sems(n):
        return [dma((count,)) for count in (n, nlat, ng, ng, nz, nz, nlat, n)]

    cells = jax.ShapeDtypeStruct((C, R, L), BF16)
    out, grad_fields, mlp, rest = pl.pallas_call(
        functools.partial(kernel, dims),
        out_shape=(
            pltpu.VMEM((C, R, L), BF16),
            pltpu.VMEM((C, R, L), BF16),
            pltpu.VMEM((MLP_ROWS, L), F32),
            pltpu.VMEM((REST_ROWS, L), F32),
        ),
        in_specs=[hbm] * 11,
        out_specs=(vmem,) * 4,
        scratch_shapes=[
            pltpu.VMEM((C * R, L), F32),
            pltpu.VMEM((R, C, L), F32),
            pltpu.VMEM((R, C, L), F32),
            pltpu.VMEM((RE, C, L), F32),
            pltpu.VMEM((RE, C, L), F32),
            pltpu.VMEM((7, RE, C, L), F32),
            pltpu.VMEM((RE, C, L), F32),
            pltpu.VMEM((7, 3, C, L), F32),
            pltpu.VMEM((49, C, L), F32),
            pltpu.VMEM((R, C, L), F32),
            pltpu.VMEM((2, 2, 3, C, L), BF16),
            pltpu.VMEM((2, 2, 3, C, L), BF16),
            pltpu.VMEM((3, 2, C, L), BF16),
            pltpu.VMEM((2, 2, 3, C, L), BF16),
            pltpu.VMEM((2, nx, 3, C, L), BF16),
            pltpu.VMEM((2, nz, 3, C, L), BF16),
            pltpu.VMEM((2, nz, 3, C, L), BF16),
            pltpu.VMEM((2, CORES, 4, C, L), BF16),
            pltpu.VMEM((2, 4, C, L), BF16),
            pltpu.VMEM((CORES, nz * L, 2 * L), BF16),
            pltpu.VMEM((C, C), F32),
            pltpu.VMEM((HID, 80), BF16),
            pltpu.VMEM((HID, C), BF16),
            pltpu.VMEM((3, C, WIDE), F32),
            pltpu.VMEM((3, C, WIDE), F32),
            pltpu.VMEM((C, HID), F32),
            pltpu.VMEM((80, HID), F32),
            pltpu.VMEM((MLP_ROWS, L), F32),
            pltpu.VMEM((REST_ROWS, L), F32),
            *part_bufs(MLP_ROWS, nlat),
            *part_bufs(REST_ROWS, owners),
            dma((2, 8)),
            dma((2, 8)),
            dma((2, nx)),
            dma((2, nx)),
            dma((2, nz)),
            dma((2, nz)),
            dma((2,)),
            dma((2,)),
            dma((11,)),
            pltpu.VMEM((C, R, L), BF16),
            pltpu.VMEM((C, R, L), BF16),
            pltpu.VMEM((R, L), jnp.int32),
            pltpu.VMEM((nlon, L), jnp.int32),
            pltpu.VMEM((7, 7, C), BF16),
            pltpu.VMEM((1, C), BF16),
            pltpu.VMEM((1, C), BF16),
            pltpu.VMEM((1, C), BF16),
            pltpu.VMEM((C, HID), BF16),
            pltpu.VMEM((2, L), BF16),
            pltpu.VMEM((C, HID), BF16),
            *part_sems(nlat),
            *part_sems(owners),
        ],
        compiler_params=pltpu.CompilerParams(
            collective_id=0, has_side_effects=True, vmem_limit_bytes=60 * 2**20
        ),
        name="block",
    )(
        fields[0],
        cotangent[0],
        ocean_mask,
        seam_partner.reshape(nlon, L),
        jnp.transpose(depth_weight, (1, 2, 0)),
        norm_gain[None],
        layer_norm_bias[None],
        layer_scale[None],
        up_weight.T,
        up_bias.reshape(2, L),
        down_weight,
    )
    vector = jax.ShapeDtypeStruct((1, C), F32)
    wide = jax.ShapeDtypeStruct((C, HID), F32)
    out, grad_fields, depth, gain, bias, up, up_b, down, scale = pl.pallas_call(
        unpack_sums,
        out_shape=(
            cells,
            cells,
            jax.ShapeDtypeStruct((7, 7, C), F32),
            vector,
            vector,
            wide,
            jax.ShapeDtypeStruct((1, HID), F32),
            wide,
            vector,
        ),
        in_specs=[vmem] * 4,
        out_specs=(hbm,) * 2 + (vmem,) * 7,
        name="unpack_sums",
        scratch_shapes=[dma((2,))],
    )(*(pltpu.with_memory_space_constraint(x, pltpu.VMEM) for x in (out, grad_fields, mlp, rest)))
    return (
        out[None],
        grad_fields[None],
        jnp.transpose(depth, (2, 0, 1)),
        gain[0],
        bias[0],
        up.T,
        up_b[0],
        down,
        scale[0],
    )


def solution(mesh):
    nlon, nlat = mesh.shape["lon"], mesh.shape["lat"]
    dims = (nlon, nlat, 4 if nlon % 16 == 0 else 2)
    cells = P(None, None, "lat", "lon")
    return jax.shard_map(
        functools.partial(shards, dims),
        mesh=mesh,
        in_specs=(cells, cells, P("lat", "lon")) + (P(),) * 8,
        out_specs=(cells, cells) + (P(),) * 7,
        check_vma=False,
    )
```

```python
import functools
import math

import jax
import jax.numpy as jnp
from jax import lax
from jax.experimental import pallas as pl
from jax.experimental.pallas import tpu as pltpu
from jax.sharding import PartitionSpec as P

F32 = jnp.float32
BF16 = jnp.bfloat16
MESH = pl.DeviceIdType.MESH
C = 64
R = 16
L = 128
HID = 256
RE = R + 6
BLOCK = 4
WIDE = BLOCK * L
MLP_ROWS = 256
REST_ROWS = 32
CORES = 2

ERF_P = 0.3275911 / math.sqrt(2.0)
ERF_C = (
    0.5 * 0.254829592,
    0.5 * -0.284496736,
    0.5 * 1.421413741,
    0.5 * -1.453152027,
    0.5 * 1.061405429,
)
PDF = 1.0 / math.sqrt(2.0 * math.pi)
HALF_LOG2E = -0.5 * math.log2(math.e)


def phi_and_density(v):
    d = 1.0 + ERF_P * jnp.abs(v)
    t = pl.reciprocal(d, approx=True)
    t = t * (2.0 - d * t)
    e = jnp.exp2(HALF_LOG2E * (v * v))
    poly = ERF_C[4]
    for coef in ERF_C[3::-1]:
        poly = poly * t + coef
    tail = poly * t * e
    return jnp.where(v >= 0.0, 1.0 - tail, tail), e


def nt_dot(a, b):
    return lax.dot_general(a, b, (((1,), (1,)), ((), ())), preferred_element_type=F32)


def dot(a, b):
    return jnp.dot(a, b, preferred_element_type=F32)


def roll(x, amount):
    amount %= L
    return pltpu.roll(x, amount, x.ndim - 1) if amount else x


class PartSum:
    def __init__(self, at, src, bufs, sems, owners):
        self.at, self.src, self.owners = at, src, owners
        self.b1, self.b2, self.b3, self.out = bufs
        self.sems = sems
        self.chunk = self.b1.shape[1]

    def piece(self, p):
        return self.src.at[pl.ds(pl.multiple_of(p * self.chunk, 8), self.chunk)]

    def others(self, count, body):
        @pl.loop(0, count)
        def _(p):
            @pl.when(p != self.at.lat)
            def _():
                body(p)

    def owner(self, body):
        if self.owners == self.at.nlat:
            body()
        else:
            pl.when(self.at.lat < self.owners)(body)

    def first(self, to, slot):
        return remote(self.piece(to), self.b1.at[slot], self.sems[0].at[to], self.sems[1].at[slot],
                      self.at.place(self.at.lon, to))

    def second(self, j, mine):
        at = self.at
        to = (at.mg + j) % at.ng
        slot = at.mg if mine else to
        return remote(self.b2.at[at.mg], self.b2.at[slot], self.sems[2].at[to], self.sems[3].at[slot],
                      at.place(at.lon_of_group(to), at.lat))

    def third(self, j, mine):
        at = self.at
        to = (at.mz + j) % at.nz
        slot = at.mz if mine else to
        return remote(self.b3.at[at.mz], self.b3.at[slot], self.sems[4].at[to], self.sems[5].at[slot],
                      at.place(at.mx * at.nzc + to * CORES + at.mc, at.lat))

    def last(self, to, slot):
        return remote(self.out.at[self.at.lat % self.owners], self.out.at[slot], self.sems[6].at[to],
                      self.sems[7].at[slot], self.at.place(self.at.lon, to))

    def step1(self):
        self.others(self.owners, lambda p: self.first(p, self.at.lat).start())

    def step2(self):
        at = self.at

        def go():
            self.others(at.nlat, lambda p: self.first(0, p).wait_recv())
            self.b1[at.lat] = self.src[pl.ds(pl.multiple_of(at.lat * self.chunk, 8), self.chunk)]
            self.b2[at.mg] = jnp.sum(self.b1[...], axis=0)

            @pl.loop(1, at.ng)
            def _(j):
                self.second(j, True).start()

        self.owner(go)

    def step3(self):
        at = self.at

        def go():
            @pl.loop(1, at.ng)
            def _(j):
                self.second(j, False).wait()

            self.b3[at.mz] = jnp.sum(self.b2[...], axis=0)

            @pl.loop(1, at.nz)
            def _(j):
                self.third(j, True).start()

        self.owner(go)

    def step4(self):
        at = self.at

        def go():
            @pl.loop(1, at.nz)
            def _(j):
                self.third(j, False).wait()

            self.out[at.lat] = jnp.sum(self.b3[...], axis=0)
            self.others(at.nlat, lambda p: self.last(p, at.lat).start())

        self.owner(go)

    def finish(self):
        at = self.at
        self.others(self.owners, lambda p: self.last(p, p).wait_recv())
        self.owner(lambda: self.others(at.nlat, lambda p: self.last(p, at.lat).wait_send()))
        self.others(self.owners, lambda p: self.first(p, at.lat).wait_send())


def remote(src, dst, send, recv, where):
    return pltpu.make_async_remote_copy(
        src_ref=src, dst_ref=dst, send_sem=send, recv_sem=recv,
        device_id=where, device_id_type=MESH,
    )


class Place:
    def __init__(self, dims):
        nlon, nlat, nx = dims
        self.nlon, self.nlat, self.nx = dims
        self.nzc = nlon // nx
        self.nz = self.nzc // CORES
        self.ng = nx * CORES
        self.lon = lax.axis_index("lon")
        self.lat = lax.axis_index("lat")
        self.mx, self.mzc = self.lon // self.nzc, self.lon % self.nzc
        self.mz, self.mc = self.mzc // CORES, self.mzc % CORES
        self.mg = self.mx * CORES + self.mc

    def place(self, a, b):
        return {"lon": a, "lat": b}

    def lon_of_group(self, g):
        return (g // CORES) * self.nzc + self.mz * CORES + g % CORES


def kernel(
    dims,
    fields_hbm,
    cot_hbm,
    mask_hbm,
    seam_hbm,
    depth_hbm,
    gain_hbm,
    bias_hbm,
    scale_hbm,
    upt_hbm,
    upb_hbm,
    down_hbm,
    out_ref,
    gf_ref,
    mlp_ref,
    rest_ref,
    rows_f,
    gmask,
    outr,
    xf,
    df,
    shifts,
    hal,
    fshift,
    wts,
    conv,
    edges,
    edgesr,
    pks,
    pkr,
    fx,
    fsel,
    fz,
    fout,
    fin,
    onehot,
    pmat,
    upx,
    downt,
    parb,
    acc_s,
    acc_down,
    acc_up,
    mlp_src,
    rest_src,
    mlp1,
    mlp2,
    mlp3,
    mlpg,
    rest1,
    rest2,
    rest3,
    restg,
    halo_send,
    halo_recv,
    fx_send,
    fx_recv,
    fz_send,
    fz_recv,
    fc_send,
    fc_recv,
    in_sems,
    fields_ref,
    cot_ref,
    mask_ref,
    seam_ref,
    depth_ref,
    gain_ref,
    bias_ref,
    scale_ref,
    upt_ref,
    upb_ref,
    down_ref,
    *part_sems,
):
    at = Place(dims)
    nlon, nlat, nx, nzc, ng = at.nlon, at.nlat, at.nx, at.nzc, at.ng
    lon, lat, mx, mzc, mg = at.lon, at.lat, at.mx, at.mzc, at.mg
    nz, mz, mc = at.nz, at.mz, at.mc
    place = at.place
    left, right = (lon + nlon - 1) % nlon, (lon + 1) % nlon
    down_lat, up_lat = (lat + nlat - 1) % nlat, (lat + 1) % nlat
    lats = (down_lat, lat, up_lat)
    is_top = lat == nlat - 1
    is_bottom = lat == 0
    mlp_sum = PartSum(at, mlp_src, (mlp1, mlp2, mlp3, mlpg), part_sems[:8], nlat)
    rest_sum = PartSum(at, rest_src, (rest1, rest2, rest3, restg), part_sems[8:], restg.shape[0])

    loads = [
        pltpu.make_async_copy(src, dst, in_sems.at[n])
        for n, (src, dst) in enumerate(
            (
                (fields_hbm, fields_ref),
                (cot_hbm, cot_ref),
                (mask_hbm, mask_ref),
                (seam_hbm, seam_ref),
                (depth_hbm, depth_ref),
                (gain_hbm, gain_ref),
                (bias_hbm, bias_ref),
                (scale_hbm, scale_ref),
                (upt_hbm, upt_ref),
                (upb_hbm, upb_ref),
                (down_hbm, down_ref),
            )
        )
    ]
    for load in loads:
        load.start()

    barrier = pltpu.get_barrier_semaphore()

    def hail(a, b):
        pl.semaphore_signal(barrier, inc=1, device_id=place(a, b), device_id_type=MESH)

    for b in lats:
        hail(left, b)
        hail(right, b)
    hail(lon, down_lat)
    hail(lon, up_lat)

    @pl.loop(1, nlat)
    def _(j):
        hail(lon, (lat + j) % nlat)

    @pl.loop(1, ng)
    def _(j):
        hail(at.lon_of_group((mg + j) % ng), lat)

    @pl.loop(1, nz)
    def _(j):
        hail(mx * nzc + (mz + j) % nz * CORES + mc, lat)

    lane = lax.broadcasted_iota(jnp.int32, (C, L), 1)
    slot_of_lane = lane // 8
    low_half = lane < 64

    def row_copies(ph):
        return [
            remote(edges.at[ph, 0], edgesr.at[ph, 1],
                   halo_send.at[ph, 0], halo_recv.at[ph, 0], place(lon, down_lat)),
            remote(edges.at[ph, 1], edgesr.at[ph, 0],
                   halo_send.at[ph, 1], halo_recv.at[ph, 1], place(lon, up_lat)),
        ]

    def pack_copies(ph, kinds, src):
        return [
            remote(pks.at[src, side], pkr.at[ph, side, k],
                   halo_send.at[ph, 2 + 3 * side + k], halo_recv.at[ph, 2 + 3 * side + k], place(to, lats[k]))
            for side, to in ((0, left), (1, right))
            for k in kinds
        ]

    def pack(src, row, which):
        low = jnp.zeros((C, L), F32)
        high = jnp.zeros((C, L), F32)
        for i in which:
            here = slot_of_lane == i
            low = jnp.where(here, roll(row(i), 8 * i), low)
            high = jnp.where(here, roll(row(i), 8 * i + 8), high)
        pks[src, 0] = low.astype(BF16)
        pks[src, 1] = high.astype(BF16)

    def unpack(ph, k, ext_rows):
        from_right = pkr[ph, 0, k].astype(F32)
        from_left = pkr[ph, 1, k].astype(F32)
        for u in ext_rows:
            i = (u - 3) % R
            hal[u] = jnp.where(low_half, roll(from_right, -8 * i), roll(from_left, 120 - 8 * i))

    def unpack_beside(ph):
        unpack(ph, 1, range(3, R + 3))

    def unpack_rows(ph, rows):
        unpack(ph, 2, range(0, 3))
        unpack(ph, 0, range(R + 3, RE))
        rows[0:3] = edgesr[ph, 0].astype(F32)
        rows[R + 3 : RE] = edgesr[ph, 1].astype(F32)

    def shifted(q, main, halo, lanes):
        if q == 3:
            return main
        edge = lanes >= 125 + q if q < 3 else lanes < q - 3
        return roll(jnp.where(edge, halo, main), 3 - q)

    def part_of(s):
        return pl.ds(pl.multiple_of(s * 8, 8), 8)

    def fold_copy(ph, j, mine):
        to = (mx + j) % nx
        slot = mx if mine else to
        return remote(fx.at[ph, mx], fx.at[ph, slot], fx_send.at[ph, to], fx_recv.at[ph, slot],
                      place(to * nzc + mzc, lat))

    def fold_copy2(ph, j, mine):
        to = (mz + j) % nz
        slot = mz if mine else to
        return remote(fsel.at[ph, to], fz.at[ph, slot], fz_send.at[ph, to], fz_recv.at[ph, slot],
                      place(mx * nzc + to * CORES + mc, lat))

    def fold_copy3(ph):
        return remote(fout.at[ph, 1], fin.at[ph], fc_send.at[ph], fc_recv.at[ph],
                      place(mx * nzc + mz * CORES + 1 - mc, lat))

    def needed(x, m, z):
        start = L * (x * nzc + m)
        least = seam_ref[0:1, 0:1] - L * (mx * nzc + z * CORES) - (CORES * L + 2)
        last = nlon * L - 1
        return (((start - least) & last) < CORES * L + 6) | (((least - start) & last) < L)

    def fold_first(ph, rows):
        fx[ph, mx] = rows[R : R + 3].astype(BF16)

        @pl.loop(1, nx)
        def _(j):
            fold_copy(ph, j, True).start()

    def fold_second(ph):
        @pl.loop(1, nx)
        def _(j):
            fold_copy(ph, j, False).wait()

        @pl.loop(0, nz)
        def _(z):
            picked = jnp.zeros((3, C, L), F32)
            for x in range(nx):
                use = jnp.where(needed(x, mzc, z), 1.0, 0.0)
                picked = jnp.where(jnp.broadcast_to(use, (C, L))[None] > 0.5, fx[ph, x].astype(F32), picked)
            fsel[ph, z] = picked.astype(BF16)

        fz[ph, mz] = fsel[ph, mz]

        @pl.loop(1, nz)
        def _(j):
            fold_copy2(ph, j, True).start()

    def fold_third(ph):
        @pl.loop(1, nz)
        def _(j):
            fold_copy2(ph, j, False).wait()

        held = jnp.concatenate([fz[ph, z].reshape(3 * C, L) for z in range(nz)], axis=1)
        for other in range(CORES):
            got = dot(held, onehot[other])
            mirrored = [got[C * (2 - k) : C * (3 - k)] for k in range(3)]
            slot = slot_of_lane % 8
            ends = mirrored[2][:, L:]
            for k in (1, 0):
                ends = jnp.where(slot == k, mirrored[k][:, L:], ends)
            for k in range(3):
                fout[ph, other, k] = mirrored[k][:, :L].astype(BF16)
            fout[ph, other, 3] = ends.astype(BF16)
        fold_copy3(ph).start()

    def fold_last(ph):
        fold_copy3(ph).wait()
        total = fout[ph, 0].astype(F32) + fin[ph].astype(F32)
        halos = [
            jnp.where(low_half, roll(total[3], -8 * k), roll(total[3], 56 - 8 * k))
            for k in range(3)
        ]
        return [total[k] for k in range(3)], halos

    loads[0].wait()
    rows_f[...] = fields_ref[...].astype(F32).reshape(C * R, L)
    for i in range(R):
        xf[3 + i] = rows_f[pl.ds(i, C, stride=R), :]
    edges[0, 0] = xf[3:6].astype(BF16)
    edges[0, 1] = xf[R : R + 3].astype(BF16)
    pack(0, lambda i: xf[3 + i], range(R))
    pl.semaphore_wait(barrier, 8 + (nlat - 1) + (ng - 1) + (nz - 1))
    @pl.when(is_top)
    def _():
        fold_first(0, xf)

    beside = pack_copies(0, (1,), 0)
    sent = row_copies(0) + pack_copies(0, (0, 2), 0)
    for copy in beside + sent:
        copy.start()
    loads[3].wait()

    @pl.when(is_top)
    def _():
        rows_i = lax.broadcasted_iota(jnp.int32, (nz * L, L), 0)
        block = jnp.full((nz * L, L), -(2**20), jnp.int32)
        for z in range(nz):
            for x in range(nx):
                here = jnp.where(needed(x, z * CORES + mc, mz), 1, 0)
                here = (jnp.broadcast_to(here, (nz * L, L)) > 0) & (rows_i // L == z)
                block = jnp.where(here, L * (x * nzc + z * CORES + mc), block)
        held_col = block + rows_i % L
        col = lax.broadcasted_iota(jnp.int32, (1, L), 1)
        ahead = jnp.where(col < 64, L + col % 8, col % 8 - 8)
        for other in range(CORES):
            core = mc + other * (1 - 2 * mc)
            origin = seam_ref[0:1, 0:1] - L * (mx * nzc + mz * CORES + core)
            for half, offset in enumerate((col, ahead)):
                wanted = (origin - offset) & (nlon * L - 1)
                onehot[other, :, L * half : L * (half + 1)] = jnp.where(held_col == wanted, 1.0, 0.0).astype(BF16)

    for load in loads[1:3] + loads[4:]:
        load.wait()

    def eye(n):
        return jnp.where(
            lax.broadcasted_iota(jnp.int32, (n, n), 0) == lax.broadcasted_iota(jnp.int32, (n, n), 1), 1.0, 0.0
        ).astype(BF16)

    pmat[...] = jnp.zeros_like(pmat)
    for a in range(7):
        pmat[8 * a : 8 * a + 7] = depth_ref[a].astype(F32)
    for n, ref in enumerate((gain_ref, bias_ref, scale_ref)):
        pmat[56 + n : 57 + n] = ref[...].astype(F32)
    par = nt_dot(eye(C), pmat[...].astype(BF16))
    for a in range(7):
        for q in range(7):
            wts[a * 7 + q] = jnp.broadcast_to(par[:, 8 * a + q : 8 * a + q + 1], (C, L))
    for n in range(3):
        parb[n] = jnp.broadcast_to(par[:, 56 + n : 57 + n], (C, WIDE))
    first_row = lax.broadcasted_iota(jnp.int32, (16, HID), 0) == 0
    upb = upb_ref[...].astype(F32)
    upb = jnp.concatenate([upb[0:1], upb[1:2]], axis=1)
    bias_row = jnp.where(first_row, jnp.broadcast_to(upb, (16, HID)), 0.0)
    with_bias = jnp.concatenate([upt_ref[...], bias_row.astype(BF16)], axis=0)
    upx[...] = nt_dot(eye(HID), with_bias).astype(BF16)
    downt[...] = nt_dot(eye(HID), down_ref[...]).astype(BF16)
    acc_s[...] = jnp.zeros_like(acc_s)
    acc_down[...] = jnp.zeros_like(acc_down)
    acc_up[...] = jnp.zeros_like(acc_up)
    rows_f[...] = cot_ref[...].astype(F32).reshape(C * R, L)
    for i in range(R):
        gmask[i] = rows_f[pl.ds(i, C, stride=R), :] * mask_ref[i : i + 1, :].astype(F32)

    def conv_rows(first, count):
        ext_rows = pl.ds(first, count + 6)

        @pl.loop(0, C // 8)
        def _(s):
            cs = part_of(s)
            lanes = lax.broadcasted_iota(jnp.int32, (count + 6, 8, L), 2)
            total = jnp.zeros((count, 8, L), F32)
            for q in range(7):
                ext = shifted(q, xf[ext_rows, cs, :], hal[ext_rows, cs, :], lanes)
                shifts[q, ext_rows, cs, :] = ext
                for a in range(7):
                    total = total + wts[a * 7 + q, cs, :][None] * ext[a : a + count]
            conv[pl.ds(first, count), cs, :] = total

    for copy in beside:
        copy.wait()
    unpack_beside(0)
    @pl.when(is_top)
    def _():
        fold_second(0)

    conv_rows(3, R - 6)

    for copy in sent:
        copy.wait()
    unpack_rows(0, xf)

    @pl.when(is_bottom)
    def _():
        for u in range(3):
            xf[u] = jnp.zeros((C, L), F32)
            hal[u] = jnp.zeros((C, L), F32)

    conv_rows(0, 3)

    top_flag = (lat + 1) // nlat

    def flat(x):
        return jnp.concatenate([x[i] for i in range(BLOCK)], axis=1)

    @pl.loop(0, R // BLOCK)
    def _(step):
        first = BLOCK * (((3 - 2 * top_flag) * step) % (R // BLOCK))

        @pl.when(step == 3 * top_flag)
        def _():
            @pl.when(is_top)
            def _():
                mains, halos = fold_last(0)
                for k in range(3):
                    xf[R + 3 + k] = mains[k]
                    hal[R + 3 + k] = halos[k]

            conv_rows(R - 3, 3)

        rows = pl.ds(first, BLOCK)
        gain, bias, scale = parb[0], parb[1], parb[2]
        x = flat(conv[rows])
        mean = jnp.mean(x, axis=0, keepdims=True)
        x = x - mean
        rstd = lax.rsqrt(jnp.mean(x * x, axis=0, keepdims=True) + 1e-06)
        xhat = x * rstd
        normed = (xhat * gain + bias).astype(BF16)
        normed_one = jnp.concatenate([normed, jnp.ones((16, WIDE), BF16)], axis=0)
        pre = dot(upx[...], normed_one)
        phi, density = phi_and_density(pre)
        hidden = (pre * phi).astype(BF16)
        slope = phi + pre * density * PDF
        branch = dot(down_ref[...], hidden)
        mask = mask_ref[rows, :].astype(F32)
        mask = jnp.concatenate([mask[i : i + 1] for i in range(BLOCK)], axis=1)
        out = mask * (flat(xf[pl.ds(3 + first, BLOCK)]) + scale * branch)
        g = flat(gmask[rows])
        d_branch = (g * scale).astype(BF16)
        acc_s[2] += g * branch
        acc_down[...] += nt_dot(d_branch, hidden)
        d_hidden = dot(downt[...], d_branch)
        d_pre = (d_hidden * slope).astype(BF16)
        acc_up[...] += nt_dot(normed_one, d_pre)
        d_normed = dot(upt_ref[...], d_pre)
        acc_s[0] += d_normed * xhat
        acc_s[1] += d_normed
        gd = d_normed * gain
        d_conv = rstd * (
            gd
            - jnp.mean(gd, axis=0, keepdims=True)
            - xhat * jnp.mean(gd * xhat, axis=0, keepdims=True)
        )
        d_conv = d_conv.astype(BF16).astype(F32)
        for i in range(BLOCK):
            outr[first + i] = out[:, L * i : L * (i + 1)]
            df[3 + first + i] = d_conv[:, L * i : L * (i + 1)]

        @pl.when(step == 1)
        def _():
            edges[1, 0] = df[3:6].astype(BF16)
            edges[1, 1] = df[R : R + 3].astype(BF16)
            pack(1, lambda i: df[3 + i], (0, 1, 2, 13, 14, 15))
            for copy in row_copies(1) + pack_copies(1, (0, 2), 1):
                copy.start()

            @pl.when(is_top)
            def _():
                fold_third(0)

    @pl.when(is_top)
    def _():
        fold_first(1, df)

    pack(2, lambda i: df[3 + i], range(R))
    for copy in pack_copies(1, (1,), 2):
        copy.start()

    up = acc_up[...]
    mlp_src[0:64] = up[:64, :L]
    mlp_src[64:128] = up[:64, L:]
    down = acc_down[...]
    mlp_src[128:192] = down[:, :L]
    mlp_src[192:256] = down[:, L:]
    mlp_sum.step1()

    @pl.loop(0, C // 8)
    def _(s):
        cs = part_of(s)
        d_conv = df[3 : R + 3, cs, :]
        lanes = lax.broadcasted_iota(jnp.int32, (8, L), 1)
        got = jnp.zeros((8, L), F32)
        for q in range(7):
            ext = shifts[q, :, cs, :]
            for a in range(7):
                tap = jnp.sum(d_conv * ext[a : a + R], axis=0)
                got = jnp.where(lanes == a * 8 + q, jnp.sum(tap, axis=1, keepdims=True), got)
        for n in range(3):
            got = jnp.where(lanes == 56 + n, jnp.sum(acc_s[n, cs, :], axis=1, keepdims=True), got)
        rows_f[cs, :] = got

    rows_f[C : 2 * C] = jnp.zeros((C, L), F32)
    taps = jnp.transpose(rows_f[0:L, :])[:C]
    up_b = up[C : C + 1]
    row_of = lax.broadcasted_iota(jnp.int32, (C, L), 0)
    for k in range(4):
        piece = jnp.broadcast_to(up_b[:, L * (k // 2) : L * (k // 2) + L], (C, L))
        taps = jnp.where(row_of == 59 + k, roll(piece, 64 * (k % 2)), taps)
    rest_src[...] = jnp.where(low_half[:32], taps[:32], roll(taps[32:], 64))
    rest_sum.step1()

    @pl.when(is_top)
    def _():
        fold_second(1)

    mlp_sum.step2()

    for copy in row_copies(1) + pack_copies(1, (0, 2), 1) + pack_copies(1, (1,), 2):
        copy.wait()
    unpack_beside(1)
    unpack_rows(1, df)

    def clear(u):
        df[u] = jnp.zeros((C, L), F32)
        hal[u] = jnp.zeros((C, L), F32)

    @pl.when(is_bottom)
    def _():
        for u in range(3):
            clear(u)

    @pl.when(is_top)
    def _():
        for u in range(R + 3, RE):
            clear(u)

    def adjoint(first, last):
        @pl.loop(first, last)
        def _(s):
            cs = part_of(s)
            lanes = lax.broadcasted_iota(jnp.int32, (RE, 8, L), 2)
            total = gmask[:, cs, :]
            for q in range(7):
                ext = shifted(6 - q, df[:, cs, :], hal[:, cs, :], lanes)
                for a in range(7):
                    total = total + wts[a * 7 + q, cs, :][None] * ext[6 - a : 6 - a + R]
            gmask[:, cs, :] = total

    adjoint(0, C // 16)

    @pl.when(is_top)
    def _():
        fold_third(1)

    rest_sum.step2()
    mlp_sum.step3()
    adjoint(C // 16, C // 8)
    rest_sum.step3()
    mlp_sum.step4()

    @pl.when(is_top)
    def _():
        mains, halos = fold_last(1)
        for k in range(3):
            for q in range(7):
                fshift[q, k] = shifted(q, mains[k], halos[k], lane)
        for k in range(3):
            total = gmask[R - 1 - k]
            for a in range(k + 4, 7):
                for q in range(7):
                    total = total + wts[a * 7 + q] * fshift[q, a - k - 4]
            gmask[R - 1 - k] = total

    for i in range(R):
        rows_f[pl.ds(i, C, stride=R), :] = gmask[i]
    gf_ref[...] = rows_f[...].reshape(C, R, L).astype(BF16)
    rest_sum.step4()
    for i in range(R):
        rows_f[pl.ds(i, C, stride=R), :] = outr[i]
    out_ref[...] = rows_f[...].reshape(C, R, L).astype(BF16)
    mlp_sum.finish()
    for p in range(nlat):
        mlp_ref[p * mlp_sum.chunk : (p + 1) * mlp_sum.chunk] = mlpg[p]
    rest_sum.finish()
    for p in range(restg.shape[0]):
        rest_ref[p * rest_sum.chunk : (p + 1) * rest_sum.chunk] = restg[p]


def unpack_sums(out_ref, gf_ref, mlp_ref, rest_ref, o_out, o_gf, o_depth, o_gain, o_bias, o_up, o_upb, o_down, o_scale, sems):
    stores = [pltpu.make_async_copy(out_ref, o_out, sems.at[0]), pltpu.make_async_copy(gf_ref, o_gf, sems.at[1])]
    for store in stores:
        store.start()
    o_up[:, :L] = mlp_ref[0:64]
    o_up[:, L:] = mlp_ref[64:128]
    o_down[:, :L] = mlp_ref[128:192]
    o_down[:, L:] = mlp_ref[192:256]
    low = rest_ref[...]
    high = pltpu.roll(low, 64, 1)
    for a in range(7):
        part = low[8 * a : 8 * a + 7] if a < 4 else high[8 * a - 32 : 8 * a - 25]
        o_depth[a] = part[:, :C]
    o_gain[...] = high[24:25, :C]
    o_bias[...] = high[25:26, :C]
    o_scale[...] = high[26:27, :C]
    lane = lax.broadcasted_iota(jnp.int32, (1, L), 1)
    for k in range(2):
        o_upb[:, L * k : L * (k + 1)] = jnp.where(lane < 64, high[27 + 2 * k : 28 + 2 * k], low[28 + 2 * k : 29 + 2 * k])
    for store in stores:
        store.wait()


def shards(
    dims,
    fields,
    cotangent,
    ocean_mask,
    seam_partner,
    depth_weight,
    norm_gain,
    layer_norm_bias,
    up_weight,
    up_bias,
    down_weight,
    layer_scale,
):
    nlon, nlat, nx = dims
    nzc = nlon // nx
    nz = nzc // CORES
    ng = nx * CORES
    owners = min(4, nlat)
    vmem = pl.BlockSpec(memory_space=pltpu.VMEM)
    hbm = pl.BlockSpec(memory_space=pltpu.HBM)
    dma = pltpu.SemaphoreType.DMA

    def part_bufs(rows, n):
        chunk = rows // n
        return [pltpu.VMEM((count, chunk, L), F32) for count in (nlat, ng, nz, n)]

    def part_sems(n):
        return [dma((count,)) for count in (n, nlat, ng, ng, nz, nz, nlat, n)]

    cells = jax.ShapeDtypeStruct((C, R, L), BF16)
    out, grad_fields, mlp, rest = pl.pallas_call(
        functools.partial(kernel, dims),
        out_shape=(
            pltpu.VMEM((C, R, L), BF16),
            pltpu.VMEM((C, R, L), BF16),
            pltpu.VMEM((MLP_ROWS, L), F32),
            pltpu.VMEM((REST_ROWS, L), F32),
        ),
        in_specs=[hbm] * 11,
        out_specs=(vmem,) * 4,
        scratch_shapes=[
            pltpu.VMEM((C * R, L), F32),
            pltpu.VMEM((R, C, L), F32),
            pltpu.VMEM((R, C, L), F32),
            pltpu.VMEM((RE, C, L), F32),
            pltpu.VMEM((RE, C, L), F32),
            pltpu.VMEM((7, RE, C, L), F32),
            pltpu.VMEM((RE, C, L), F32),
            pltpu.VMEM((7, 3, C, L), F32),
            pltpu.VMEM((49, C, L), F32),
            pltpu.VMEM((R, C, L), F32),
            pltpu.VMEM((2, 2, 3, C, L), BF16),
            pltpu.VMEM((2, 2, 3, C, L), BF16),
            pltpu.VMEM((3, 2, C, L), BF16),
            pltpu.VMEM((2, 2, 3, C, L), BF16),
            pltpu.VMEM((2, nx, 3, C, L), BF16),
            pltpu.VMEM((2, nz, 3, C, L), BF16),
            pltpu.VMEM((2, nz, 3, C, L), BF16),
            pltpu.VMEM((2, CORES, 4, C, L), BF16),
            pltpu.VMEM((2, 4, C, L), BF16),
            pltpu.VMEM((CORES, nz * L, 2 * L), BF16),
            pltpu.VMEM((C, C), F32),
            pltpu.VMEM((HID, 80), BF16),
            pltpu.VMEM((HID, C), BF16),
            pltpu.VMEM((3, C, WIDE), F32),
            pltpu.VMEM((3, C, WIDE), F32),
            pltpu.VMEM((C, HID), F32),
            pltpu.VMEM((80, HID), F32),
            pltpu.VMEM((MLP_ROWS, L), F32),
            pltpu.VMEM((REST_ROWS, L), F32),
            *part_bufs(MLP_ROWS, nlat),
            *part_bufs(REST_ROWS, owners),
            dma((2, 8)),
            dma((2, 8)),
            dma((2, nx)),
            dma((2, nx)),
            dma((2, nz)),
            dma((2, nz)),
            dma((2,)),
            dma((2,)),
            dma((11,)),
            pltpu.VMEM((C, R, L), BF16),
            pltpu.VMEM((C, R, L), BF16),
            pltpu.VMEM((R, L), jnp.int32),
            pltpu.VMEM((nlon, L), jnp.int32),
            pltpu.VMEM((7, 7, C), BF16),
            pltpu.VMEM((1, C), BF16),
            pltpu.VMEM((1, C), BF16),
            pltpu.VMEM((1, C), BF16),
            pltpu.VMEM((C, HID), BF16),
            pltpu.VMEM((2, L), BF16),
            pltpu.VMEM((C, HID), BF16),
            *part_sems(nlat),
            *part_sems(owners),
        ],
        compiler_params=pltpu.CompilerParams(
            collective_id=0, has_side_effects=True, vmem_limit_bytes=60 * 2**20
        ),
        name="block",
    )(
        fields[0],
        cotangent[0],
        ocean_mask,
        seam_partner.reshape(nlon, L),
        jnp.transpose(depth_weight, (1, 2, 0)),
        norm_gain[None],
        layer_norm_bias[None],
        layer_scale[None],
        up_weight.T,
        up_bias.reshape(2, L),
        down_weight,
    )
    vector = jax.ShapeDtypeStruct((1, C), F32)
    wide = jax.ShapeDtypeStruct((C, HID), F32)
    out, grad_fields, depth, gain, bias, up, up_b, down, scale = pl.pallas_call(
        unpack_sums,
        out_shape=(
            cells,
            cells,
            jax.ShapeDtypeStruct((7, 7, C), F32),
            vector,
            vector,
            wide,
            jax.ShapeDtypeStruct((1, HID), F32),
            wide,
            vector,
        ),
        in_specs=[vmem] * 4,
        out_specs=(hbm,) * 2 + (vmem,) * 7,
        name="unpack_sums",
        scratch_shapes=[dma((2,))],
    )(*(pltpu.with_memory_space_constraint(x, pltpu.VMEM) for x in (out, grad_fields, mlp, rest)))
    return (
        out[None],
        grad_fields[None],
        jnp.transpose(depth, (2, 0, 1)),
        gain[0],
        bias[0],
        up.T,
        up_b[0],
        down,
        scale[0],
    )


def solution(mesh):
    nlon, nlat = mesh.shape["lon"], mesh.shape["lat"]
    dims = (nlon, nlat, 4 if nlon % 16 == 0 else 2)
    cells = P(None, None, "lat", "lon")
    return jax.shard_map(
        functools.partial(shards, dims),
        mesh=mesh,
        in_specs=(cells, cells, P("lat", "lon")) + (P(),) * 8,
        out_specs=(cells, cells) + (P(),) * 7,
        check_vma=False,
    )
```
